32 devices in a mesh: heads: 4 (over y, x), tokens: 8 (over z, core).
Axes of the slice: x: 2, y: 2, z: 4, core: 2. Of those that a mesh axis runs over, the one named last changes fastest.
Arguments:
- tokens: bfloat16 [8192, 1024], P(('tokens', 'heads')), may hold values from -6 to 6
- segment_ids: int32 [8, 1024], P('tokens'), may hold values from 0 to 7, never falling along the last dimension, each value on 1 to 512 neighbouring positions
- routes: int32 [8192, 8], P(('tokens', 'heads')), may hold values from 0 to 31, all different within a row; in each aligned block of 256 rows (0 to 255, 256 to 511, ...) at most 96 rows name the same one
- attn_gain: float32 [1024], replicated, may hold values from 0.1 to 1.9
- w_query: bfloat16 [1024, 1024], P(None, 'heads'), may hold values from -0.1875 to 0.1875
- w_key: bfloat16 [1024, 512], P(None, 'heads'), may hold values from -0.1875 to 0.1875
- w_value: bfloat16 [1024, 512], P(None, 'heads'), may hold values from -0.1875 to 0.1875
- w_out: bfloat16 [1024, 1024], P('heads'), may hold values from -1 to 1
- ffn_gain: float32 [1024], replicated, may hold values from 0.1 to 1.9
- router: bfloat16 [1024, 32], replicated, may hold values from -0.09375 to 0.09375
- w_gate: bfloat16 [32, 1024, 512], P('tokens'), may hold values from -0.1875 to 0.1875
- w_up: bfloat16 [32, 1024, 512], P('tokens'), may hold values from -0.1875 to 0.1875
- w_down: bfloat16 [32, 512, 1024], P('tokens'), may hold values from -1 to 1
- cotangent: bfloat16 [8192, 1024], P(('tokens', 'heads')), may hold values from -6 to 6
Outputs:
- output: bfloat16 [8192, 1024], P(('tokens', 'heads'))
- input_grad: float32 [8192, 1024], P(('tokens', 'heads'))
- attn_gain_grad: float32 [1024], replicated
- w_query_grad: float32 [1024, 1024], P('tokens', 'heads')
- w_key_grad: float32 [1024, 512], P('tokens', 'heads')
- w_value_grad: float32 [1024, 512], P('tokens', 'heads')
- w_out_grad: float32 [1024, 1024], P(('heads', 'tokens'))
- ffn_gain_grad: float32 [1024], replicated
- router_grad: float32 [1024, 32], replicated
- w_gate_grad: float32 [32, 1024, 512], P('tokens', 'heads')
- w_up_grad: float32 [32, 1024, 512], P('tokens', 'heads')
- w_down_grad: float32 [32, 512, 1024], P('tokens', 'heads')
The draws below stay inside these ranges and needn't reach their ends.
Inputs may be any that keep to these rules, and one draw needn't show every extreme that they name: `segment_ids`: document numbers never fall along a sequence; each document holds 1 to 512 positions. `routes`: each row names 8 different experts; within the rows of one device (256 aligned rows) no expert is named more than 96 times.
All inputs are finite; a program needn't handle non-finite values.
Results may differ from the reference program's by a relative error of at most 0.02.
Values may be sent and summed in bfloat16 or wider, within the bound.
No kernel may reach another device: no remote copies, remote signals or barrier semaphores. Data moves between devices by JAX's collectives and lax.ppermute only.
A program may use at most 192 MiB of HBM per device.

```python
import math
import jax
import jax.numpy as jnp
import numpy as np
from jax import lax

D = 1024
HEADS = 16
KV_HEADS = 8
HEAD_DIM = 64
FF = 512
EXPERTS = 32
TOP = 8
TOK_DEV = 256
DOCS = 8
SEQ = 1024
SEQS = 8
TOKENS = 8192
CAP = 96


def block_scale(rng, dims, shards, least, largest):
    def one(position, parts):
        steps = jax.random.uniform(jax.random.fold_in(jax.random.fold_in(rng, 6), position), (parts,), jnp.float32, least / len(shards), largest / len(shards))
        return jnp.repeat(jnp.exp(steps), dims[position] // parts).reshape((-1,) + (1,) * (len(dims) - position - 1))

    level = one(*shards[0])
    for cut in shards[1:]:
        level = level * one(*cut)
    return level


def length_profile(number_of, total, reach, slope):
    loads = [(1 << 20) // math.isqrt(grade ** slope) + 1 for grade in range(2, number_of + 1)]
    rest, counts = total - reach - (number_of - 1), [1] * (number_of - 1)
    while rest > 0:
        free = [i for i in range(number_of - 1) if counts[i] < reach]
        whole, remaining = sum([loads[i] for i in free]), rest
        for i in free:
            addition = min(reach - counts[i], max(1, remaining * loads[i] // whole), rest)
            counts[i] = counts[i] + addition
            rest = rest - addition
    return np.array([reach] + counts)


def ragged(own_key, count, total, most, lean):
    if count == 2:
        one = jax.random.randint(own_key, (), max(1, total - most), min(most, total - 1) + 1)
        return jnp.stack([one, total - one])
    sizes = jnp.asarray(length_profile(count, total, most, lean), jnp.int32)
    twos = (count - 1) // 2
    giver, receiver = sizes[1:1 + 2 * twos:2], sizes[2:2 + 2 * twos:2]
    margin = jnp.minimum(giver - 1, most - receiver)
    shifted = jax.random.randint(jax.random.fold_in(own_key, 1), (twos,), 0, 1 << 20) % (margin + 1)
    sizes = sizes.at[1:1 + 2 * twos:2].set(giver - shifted).at[2:2 + 2 * twos:2].set(receiver + shifted)
    return sizes[jax.random.permutation(jax.random.fold_in(own_key, 2), count)]


def assign_block(own_key, own, number, rows, number_of, top, limit, skew):
    order = jax.random.permutation(own_key, number_of)
    heavy_load, common = shares(number_of, rows * top, limit, skew, True), shares(number_of, rows * top, limit, skew, False)
    places = jnp.arange(number_of)

    def named(tallies, rotation):
        used = int((tallies > 0).sum())
        fixed = max(1, used // 4)
        moved = fixed + (places - fixed + rotation * (used - fixed)) % max(1, number_of - fixed)
        return jnp.zeros((number_of,), jnp.int32).at[order[jnp.where(places < fixed, places, moved)]].set(jnp.asarray(tallies, jnp.int32))

    tallies = jnp.where(number % 4 == 0, named(heavy_load, number // 4), named(common, number - number // 4 - 1))
    mixed = jax.random.permutation(jax.random.fold_in(own, 3), number_of)
    giver, sink = mixed[0:number_of // 2 * 2:2], mixed[1:number_of // 2 * 2:2]
    slack = jnp.minimum(tallies[giver] - 1, limit - tallies[sink]) // 2
    slack = jnp.where((giver == order[0]) | (sink == order[0]) | (tallies[sink] == 0), 0, jnp.maximum(slack, 0))
    moved = jax.random.randint(jax.random.fold_in(own, 4), (number_of // 2,), 0, 1 << 20) % (slack + 1)
    tallies = tallies.at[giver].add(-moved).at[sink].add(moved)
    members = jnp.searchsorted(jnp.cumsum(tallies), jnp.arange(rows * top), side="right").astype(jnp.int32)
    table = members.reshape(top, rows).T
    table = table[jax.random.permutation(jax.random.fold_in(own, 1), rows)]
    rotation = jax.random.randint(jax.random.fold_in(own, 2), (rows, 1), 0, top)
    return jnp.take_along_axis(table, (jnp.arange(top)[None, :] + rotation) % top, axis=1)


def shares(amount, total, limit, lean, full):
    loads = [(1 << 20) // math.isqrt(grade ** lean) + 1 for grade in range(1, amount + 1)]
    largest = limit if full else min(limit, max(-(-total // amount), total * loads[0] // sum(loads)))
    least = 1 if total - largest >= amount - 1 else 0
    holding, spare = [largest] + [least] * (amount - 1), total - largest - least * (amount - 1)
    while spare > 0:
        candidates = [i for i in range(1, amount) if holding[i] < largest] or [i for i in range(1, amount) if holding[i] < limit]
        mass, left = sum([loads[i] for i in candidates]), spare
        for i in candidates:
            extra = min(limit - holding[i], max(1, left * loads[i] // mass), spare)
            holding[i] = holding[i] + extra
            spare = spare - extra
    return np.array(holding)


def bell_draw(stream_key, dims, deviation, reach, cuts=(), kind=jnp.bfloat16):
    result = deviation * jax.random.normal(stream_key, dims, jnp.float32)
    if cuts:
        result = result * block_scale(stream_key, dims, cuts, -0.22, 0.18)
    return jnp.clip(result, -reach, reach).astype(kind)


def setup_inputs(seed: int = 0) -> dict:
    keys = jax.random.split(jax.random.key(seed), 15)
    tokens = bell_draw(keys[0], (TOKENS, D), 1.0, 6.0, ((0, 32),))
    segment_ids = jax.vmap(lambda own: jnp.searchsorted(jnp.cumsum(ragged(own, DOCS, SEQ, SEQ // 2, 2)), jnp.arange(SEQ), side="right"))(jax.random.split(keys[1], SEQS)).reshape((SEQS, SEQ)).astype(jnp.int32)
    routes_keys = jax.random.split(jax.random.fold_in(keys[2], 1), TOKENS // TOK_DEV)
    routes_turns = jax.random.permutation(jax.random.fold_in(keys[2], 3), TOKENS // TOK_DEV)
    routes = jax.vmap(lambda own, number: assign_block(jax.random.fold_in(keys[2], 2), own, number, TOK_DEV, EXPERTS, TOP, CAP, 1))(routes_keys, routes_turns).reshape((TOKENS, TOP))
    attn_gain = jnp.clip(1.0 + 0.18 * jax.random.normal(keys[3], (D,), jnp.float32), 0.1, 1.9)
    w_query = bell_draw(keys[4], (D, HEADS * HEAD_DIM), D ** -0.5, 0.1875, ((1, 4),))
    w_key = bell_draw(keys[5], (D, KV_HEADS * HEAD_DIM), D ** -0.5, 0.1875, ((1, 4),))
    w_value = bell_draw(keys[6], (D, KV_HEADS * HEAD_DIM), D ** -0.5, 0.1875, ((1, 4),))
    w_out = bell_draw(keys[7], (HEADS * HEAD_DIM, D), (D // 32) ** -0.5, 1.0, ((0, 4),))
    ffn_gain = jnp.clip(1.0 + 0.18 * jax.random.normal(keys[8], (D,), jnp.float32), 0.1, 1.9)
    router = bell_draw(keys[9], (D, EXPERTS), (4 * D) ** -0.5, 0.09375)
    w_gate = bell_draw(keys[10], (EXPERTS, D, FF), D ** -0.5, 0.1875, ((0, 8),))
    w_up = bell_draw(keys[11], (EXPERTS, D, FF), D ** -0.5, 0.1875, ((0, 8),))
    w_down = bell_draw(keys[12], (EXPERTS, FF, D), (FF // 16) ** -0.5, 1.0, ((0, 8),))
    cotangent = bell_draw(keys[13], (TOKENS, D), 1.0, 6.0, ((0, 32),))
    return dict(tokens=tokens, segment_ids=segment_ids, routes=routes, attn_gain=attn_gain, w_query=w_query, w_key=w_key, w_value=w_value, w_out=w_out, ffn_gain=ffn_gain, router=router, w_gate=w_gate, w_up=w_up, w_down=w_down, cotangent=cotangent)


@jax.custom_vjp
def low(v):
    return lax.optimization_barrier(v.astype(jnp.bfloat16)).astype(jnp.float32)

@jax.custom_vjp
def low_back(v):
    return v

def low_keep(v):
    return (low(v), None)

def low_pass(kept, grad):
    return (grad,)

def back_keep(v):
    return (v, None)

def back_low(kept, grad):
    return (low(grad),)
low.defvjp(low_keep, low_pass)
low_back.defvjp(back_keep, back_low)
epsilon = 1e-06
theta_base = 10000.0
masked_value = -1e+30

def doc_positions(segments):
    axis_last = segments.ndim - 1
    place_ids = lax.broadcasted_iota(jnp.int32, segments.shape, axis_last)
    previous = jnp.concatenate([segments[..., :1] - 1, segments[..., :-1]], axis=axis_last)
    starts = jnp.where(segments != previous, place_ids, 0).astype(jnp.int32)
    return (place_ids - lax.cummax(starts, axis=axis_last)).astype(jnp.int32)

def rotary_tables(positions, half_size):
    frequency = theta_base ** (-(jnp.arange(half_size, dtype=jnp.float32) * 2.0) / (2.0 * half_size))
    angles = positions.astype(jnp.float32)[..., None] * frequency
    return (jnp.cos(angles), jnp.sin(angles))

def rotate(field, cosine_table, sine_table):
    half_size = field.shape[-1] // 2
    leading = field[..., :half_size]
    trailing = field[..., half_size:]
    cos_part = cosine_table[..., None, :]
    sin_part = sine_table[..., None, :]
    return jnp.concatenate([leading * cos_part - trailing * sin_part, trailing * cos_part + leading * sin_part], axis=-1)

def root_scale(values):
    return values * lax.rsqrt(lax.optimization_barrier(jnp.mean(values * values, axis=-1, keepdims=True)) + epsilon)

def matmul(left, right):
    return jnp.dot(left, right, precision=lax.Precision.HIGHEST, preferred_element_type=jnp.float32)

def attend_one(packed):
    queries_one, keys_one, values_one, segments = packed
    group_size = queries_one.shape[1] // keys_one.shape[1]
    keys_all = jnp.repeat(keys_one, group_size, axis=1)
    values_all = jnp.repeat(values_one, group_size, axis=1)
    length = queries_one.shape[0]
    scores = jnp.einsum('qhd,khd->hqk', queries_one, keys_all, precision=lax.Precision.HIGHEST) * HEAD_DIM ** (-0.5)
    scores = low_back(scores)
    row_ids = lax.broadcasted_iota(jnp.int32, (length, length), 0)
    col_ids = lax.broadcasted_iota(jnp.int32, (length, length), 1)
    allowed = (segments[:, None] == segments[None, :]) & (col_ids <= row_ids)
    scores = jnp.where(allowed[None], scores, masked_value)
    weights = low(jax.nn.softmax(scores, axis=-1))
    return jnp.einsum('hqk,khd->qhd', weights, values_all, precision=lax.Precision.HIGHEST).reshape(length, -1)

def reference(tokens, segment_ids, routes, attn_gain, w_query, w_key, w_value, w_out, ffn_gain, router, w_gate, w_up, w_down, cotangent):
    positions = doc_positions(segment_ids)
    cosine_table, sine_table = rotary_tables(positions, HEAD_DIM // 2)
    blocks_total = TOKENS // TOK_DEV
    flat_routes = routes.reshape(blocks_total, TOK_DEV * TOP)
    expert_ids = jnp.arange(EXPERTS, dtype=jnp.int32)
    one_hot = (flat_routes[:, :, None] == expert_ids).astype(jnp.int32)
    earlier = jnp.cumsum(one_hot, axis=1) - one_hot
    slot_ids = lax.optimization_barrier(jnp.sum(one_hot * earlier, axis=-1)).astype(jnp.int32)
    block_ids = jnp.arange(blocks_total, dtype=jnp.int32)[:, None]
    assign_ids = jnp.arange(TOKENS * TOP, dtype=jnp.int32).reshape(blocks_total, TOK_DEV * TOP)
    table = jnp.full((EXPERTS, blocks_total, CAP), TOKENS * TOP, jnp.int32)
    table = table.at[flat_routes, block_ids, slot_ids].set(assign_ids)
    source_rows = (table // TOP).reshape(EXPERTS, blocks_total * CAP).astype(jnp.int32)
    places = ((flat_routes * blocks_total + block_ids) * CAP + slot_ids).reshape(TOKENS, TOP).astype(jnp.int32)

    def forward(inputs, gain_one, query_w, key_w, value_w, out_w, gain_two, router_w, gate_w, up_w, down_w):
        normed_one = low(root_scale(inputs) * gain_one)
        query_raw = low_back(matmul(normed_one, query_w)).reshape(SEQS, SEQ, HEADS, HEAD_DIM)
        key_raw = low_back(matmul(normed_one, key_w)).reshape(SEQS, SEQ, KV_HEADS, HEAD_DIM)
        values = low(low_back(matmul(normed_one, value_w))).reshape(SEQS, SEQ, KV_HEADS, HEAD_DIM)
        queries = low(rotate(query_raw, cosine_table, sine_table))
        keys_rotated = low(rotate(key_raw, cosine_table, sine_table))
        attended = lax.map(jax.checkpoint(attend_one), (queries, keys_rotated, values, segment_ids))
        attended = low(low_back(attended.reshape(TOKENS, HEADS * HEAD_DIM)))
        residual = inputs + low_back(matmul(attended, out_w))
        normed_two = low(root_scale(residual) * gain_two)
        logits = low_back(matmul(normed_two, router_w))
        gate_weights = jax.nn.softmax(jnp.take_along_axis(logits, routes, axis=1), axis=-1)
        padded = jnp.concatenate([normed_two, jnp.zeros((1, D), jnp.float32)], axis=0)

        def expert_one(packed):
            rows_one, gate_one, up_one, down_one = packed
            expert_in = low_back(padded[rows_one])
            gate_pre = low_back(matmul(expert_in, gate_one))
            up_pre = low_back(matmul(expert_in, up_one))
            activated = low(jax.nn.silu(gate_pre) * up_pre)
            return low(low_back(matmul(activated, down_one)))
        produced = lax.map(jax.checkpoint(expert_one), (source_rows, gate_w, up_w, down_w)).reshape(-1, D)
        mixture = jnp.zeros_like(residual)
        for picked in range(TOP):
            mixture = mixture + gate_weights[:, picked:picked + 1] * produced[places[:, picked]]
        return residual + mixture
    result_value, pullback = jax.vjp(forward, tokens.astype(jnp.float32), attn_gain.astype(jnp.float32), w_query.astype(jnp.float32), w_key.astype(jnp.float32), w_value.astype(jnp.float32), w_out.astype(jnp.float32), ffn_gain.astype(jnp.float32), router.astype(jnp.float32), w_gate.astype(jnp.float32), w_up.astype(jnp.float32), w_down.astype(jnp.float32))
    gradients = pullback(cotangent.astype(jnp.float32))
    return (result_value.astype(jnp.bfloat16), gradients[0], gradients[1], gradients[2], gradients[3], gradients[4], gradients[5], gradients[6], gradients[7], gradients[8], gradients[9], gradients[10])
```

```python
import jax
import jax.numpy as jnp
from jax import lax
from jax.experimental import pallas as pl
from jax.experimental.pallas import tpu as pltpu
from jax.sharding import PartitionSpec as P

HEAD_DIM = 64
EXPERTS = 32
TOP = 8
CAP = 96


epsilon = 1e-06
theta_base = 10000.0
masked_value = -1e30


def doc_positions(segments):
    axis_last = segments.ndim - 1
    place_ids = lax.broadcasted_iota(jnp.int32, segments.shape, axis_last)
    previous = jnp.concatenate([segments[..., :1] - 1, segments[..., :-1]], axis=axis_last)
    starts = jnp.where(segments != previous, place_ids, 0)
    return place_ids - lax.cummax(starts, axis=axis_last)


def rotary_tables(positions, half_size):
    frequency = theta_base ** (
        -(jnp.arange(half_size, dtype=jnp.float32) * 2.0) / (2.0 * half_size)
    )
    angles = positions.astype(jnp.float32)[..., None] * frequency
    return (jnp.cos(angles), jnp.sin(angles))


def rotate(field, cosine_table, sine_table):
    half_size = field.shape[-1] // 2
    leading = field[..., :half_size]
    trailing = field[..., half_size:]
    cos_part = cosine_table[..., None, :]
    sin_part = sine_table[..., None, :]
    return jnp.concatenate(
        [leading * cos_part - trailing * sin_part, trailing * cos_part + leading * sin_part],
        axis=-1,
    )


f32 = jnp.float32
bf16 = jnp.bfloat16
i32 = jnp.int32
VMEM_LIMIT = 60 * 1024 * 1024


def swap(field, axis, bit):
    count = lax.axis_size(axis)
    return lax.ppermute(field, axis, [(i, i ^ bit) for i in range(count)])


def gather_tokens(field):
    count = lax.axis_size("tokens")
    held = {0: field}
    bit = count // 2
    while bit > 1:
        held.update({key | bit: swap(held[key], "tokens", bit) for key in list(held)})
        bit //= 2
    held.update({key | 1: swap(held[key], "tokens", 1) for key in list(held)})
    return [held[key] for key in range(count)]


def add_low(left, right):
    return (left.astype(f32) + right.astype(f32)).astype(bf16)


def scatter_chips(parts):
    count = len(parts)
    terms = {key: [parts[key]] for key in range(count)}
    bit = 1

    def total(key):
        result = terms[key][0]
        for other in terms[key][1:]:
            result = result.astype(f32) + other.astype(f32)
        return result

    while bit < count:
        for key in sorted((k for k in terms if k & bit), reverse=True):
            terms[key ^ bit].append(swap(total(key).astype(bf16), "tokens", 2 * bit))
            del terms[key]
        bit *= 2
    return total(0).astype(f32)


def scatter_tokens(field):
    count, rows, columns = field.shape
    place = lax.axis_index("tokens")
    chip, core = place // 2, place % 2
    paired = field.reshape(count // 2, 2, rows, columns)
    sent = lax.dynamic_index_in_dim(paired, 1 - core, axis=1, keepdims=False)
    kept = lax.dynamic_index_in_dim(paired, core, axis=1, keepdims=False)
    both = add_low(kept, swap(sent, "tokens", 1))
    parts = [
        lax.dynamic_index_in_dim(both, chip ^ key, axis=0, keepdims=False)
        for key in range(count // 2)
    ]
    return scatter_chips(parts)


def sum_all(field):
    for axis in ("heads", "tokens"):
        bit = 1
        while bit < lax.axis_size(axis):
            field = field + swap(field, axis, bit)
            bit *= 2
    return field


def xor_order(field, place):
    count = field.shape[0]
    rest = field.shape[1:]
    bit = 1
    while bit < count:
        split = field.reshape((count // (2 * bit), 2, bit) + rest)
        flipped = jnp.concatenate([split[:, 1:], split[:, :1]], axis=1)
        field = jnp.where((place & bit) != 0, flipped, split).reshape((count,) + rest)
        bit *= 2
    return field


def nn(left, right):
    return lax.dot_general(left, right, (((1,), (0,)), ((), ())), preferred_element_type=f32)


def nt(left, right):
    return lax.dot_general(left, right, (((1,), (1,)), ((), ())), preferred_element_type=f32)


def tn(left, right):
    return lax.dot_general(left, right, (((0,), (0,)), ((), ())), preferred_element_type=f32)


def expert_kernel(sources, first_source, first_expert, count, local, fresh, heads, *refs):
    refs = list(refs)
    where_ref = refs.pop(0)
    hn_refs = [refs.pop(0) for _ in range(sources)]
    g_hbm = refs.pop(0)
    slot_ref = refs.pop(0)
    if fresh:
        router_ref = refs.pop(0)
        mask_ref = refs.pop(0)
    else:
        gw_ref = refs.pop(0)
    gate_ref, up_ref, down_ref = refs.pop(0), refs.pop(0), refs.pop(0)
    ye_ref, dxe_ref, dgw_ref = refs.pop(0), refs.pop(0), refs.pop(0)
    sums = [(refs.pop(0), refs.pop(0)) for _ in range(count)]
    if fresh:
        gw_ref = refs.pop(0)
    h_ref, g_ref, x_ref, gx_ref, act_ref, dye_ref, dgu_ref, gws_ref, dcol_ref = refs[:9]
    h_sem, g_sem = refs[9:]
    step = pl.program_id(0)
    expert = first_expert + step
    place, head = where_ref[0], where_ref[1]
    rows = h_ref.shape[1]
    width = h_ref.shape[2]
    hidden = act_ref.shape[1]

    def copy_h(s):
        return pltpu.make_async_copy(hn_refs[s], h_ref.at[s], h_sem.at[s])

    def copy_g(s):
        return pltpu.make_async_copy(
            g_hbm.at[place ^ (first_source + s), pl.ds(0, rows)], g_ref.at[s], g_sem.at[s]
        )

    @pl.when(step == 0)
    def _():
        for s in range(sources):
            copy_h(s).start()
        for s in range(sources):
            copy_g(s).start()
        for s in range(sources):
            copy_h(s).wait()
            if fresh:
                logits = nt(router_ref[...], h_ref[s])
                mask = mask_ref[s] > 0
                top = jnp.max(jnp.where(mask, logits, -jnp.inf), axis=0, keepdims=True)
                exponent = jnp.where(mask, jnp.exp(logits - top), 0.0)
                gw_ref[s] = exponent / jnp.sum(exponent, axis=0, keepdims=True)
        for s in range(sources):
            copy_g(s).wait()

    def chosen(s):
        slots = slot_ref[s, pl.ds(expert, 1), :]
        return lax.broadcasted_iota(i32, (CAP, rows), 0) == slots

    for s in range(sources):
        same = chosen(s)
        select = jnp.where(same, 1.0, 0.0).astype(bf16)
        part = pl.ds(s * CAP, CAP)
        x_ref[part, :] = nn(select, h_ref[s]).astype(bf16)
        gx_ref[part, :] = nn(select, g_ref[s]).astype(bf16)
        weights = gw_ref[s, pl.ds(place * local + expert, 1), :]
        gws_ref[part, :] = jnp.sum(jnp.where(same, weights, 0.0), axis=1, keepdims=True)

    chunk = 4 * CAP
    while (sources * CAP) % chunk:
        chunk //= 2

    @pl.loop(0, sources * CAP // chunk)
    def _(number):
        part = pl.ds(pl.multiple_of(number * chunk, chunk), chunk)
        x = x_ref[part, :]
        gate = nn(x, gate_ref[0])
        up = nn(x, up_ref[0])
        sigma = 1.0 / (1.0 + jnp.exp(-gate))
        silu = gate * sigma
        act = (silu * up).astype(bf16)
        act_ref[part, :] = act
        gx = gx_ref[part, :].astype(f32)
        weights = gws_ref[part, :]
        dye = (gx * weights).astype(bf16)
        dye_ref[part, :] = dye
        ye = nn(act, down_ref[0]).astype(bf16).astype(f32)
        dcol_ref[part, :] = jnp.sum(gx * ye, axis=1, keepdims=True)
        ye_ref[0, part, :] = (ye * weights).astype(bf16)
        dact = nt(dye, down_ref[0])
        dgate = (dact * up * sigma * (1.0 + gate * (1.0 - sigma))).astype(bf16)
        dup = (dact * silu).astype(bf16)
        dgu_ref[part, pl.ds(0, hidden)] = dgate
        dgu_ref[part, pl.ds(hidden, hidden)] = dup
        dxe_ref[0, part, :] = (nt(dgate, gate_ref[0]) + nt(dup, up_ref[0])).astype(bf16)

    for s in range(sources):
        column = dcol_ref[pl.ds(s * CAP, CAP), :]
        dgw_ref[0, pl.ds(s, 1), :] = jnp.sum(
            jnp.where(chosen(s), column, 0.0), axis=0, keepdims=True
        )

    wide, narrow = width // heads, hidden // heads

    def weight_sums(target_ref, index, relative):
        owner = relative ^ head
        some = x_ref[:, pl.ds(pl.multiple_of(owner * wide, wide), wide)]
        both = tn(some, dgu_ref[...]).astype(bf16)
        target_ref[index, pl.ds(0, wide), :] = both[:, :hidden]
        target_ref[index, pl.ds(wide, wide), :] = both[:, hidden:]
        some = act_ref[:, pl.ds(pl.multiple_of(owner * narrow, narrow), narrow)]
        down = tn(some, dye_ref[...]).astype(bf16)
        target_ref[index, pl.ds(2 * wide, narrow), :] = down[:, :hidden]
        target_ref[index, pl.ds(2 * wide + narrow, narrow), :] = down[:, hidden:]

    for number, (sent_ref, kept_ref) in enumerate(sums):
        first = 1 + (first_expert + number) % 2

        @pl.when(step == number)
        def _():
            weight_sums(sent_ref, 0, first)
            weight_sums(sent_ref, 1, 3)
            weight_sums(kept_ref, 0, 0)
            weight_sums(kept_ref, 1, 3 - first)


def run_experts(
    where, hn_list, upstream_all, first_source, slots, router_t, mask, gate_weights,
    first_expert, count, w_gate, w_up, w_down, heads,
):
    sources = len(hn_list)
    rows, width = hn_list[0].shape
    local, _, hidden = w_gate.shape
    fresh = gate_weights is None
    experts = mask.shape[1]
    slots_all = sources * CAP
    block = 2 * (width // heads) + width // heads
    whole = pl.BlockSpec(memory_space=pltpu.VMEM)
    hbm = pl.BlockSpec(memory_space=pl.ANY)

    def of_expert(shape):
        return pl.BlockSpec(shape, lambda i: (first_expert + i, 0, 0))

    operands = [where, *hn_list, upstream_all, slots]
    in_specs = [pl.BlockSpec(memory_space=pltpu.SMEM)] + [hbm] * sources + [hbm, whole]
    if fresh:
        operands += [router_t, mask]
        in_specs += [whole, whole]
    else:
        operands += [gate_weights]
        in_specs += [whole]
    operands += [w_gate, w_up, w_down]
    in_specs += [
        of_expert((1, width, hidden)), of_expert((1, width, hidden)), of_expert((1, hidden, width))
    ]
    out_shape = [
        jax.ShapeDtypeStruct((count, slots_all, width), bf16),
        jax.ShapeDtypeStruct((count, slots_all, width), bf16),
        jax.ShapeDtypeStruct((count, sources, rows), f32),
    ]
    out_specs = [
        pl.BlockSpec((1, slots_all, width), lambda i: (i, 0, 0)),
        pl.BlockSpec((1, slots_all, width), lambda i: (i, 0, 0)),
        pl.BlockSpec((1, sources, rows), lambda i: (i, 0, 0)),
    ]
    for _ in range(count):
        for _ in range(2):
            out_shape.append(jax.ShapeDtypeStruct((2, block, hidden), bf16))
            out_specs.append(pl.BlockSpec((2, block, hidden), lambda i: (0, 0, 0)))
    if fresh:
        out_shape.append(jax.ShapeDtypeStruct((sources, experts, rows), f32))
        out_specs.append(whole)

    def body(*refs):
        expert_kernel(sources, first_source, first_expert, count, local, fresh, heads, *refs)

    flops = count * slots_all * width * hidden * 18
    return pl.pallas_call(
        body,
        grid=(count,),
        in_specs=in_specs,
        out_specs=out_specs,
        out_shape=out_shape,
        scratch_shapes=[
            pltpu.VMEM((sources, rows, width), bf16),
            pltpu.VMEM((sources, rows, width), bf16),
            pltpu.VMEM((slots_all, width), bf16),
            pltpu.VMEM((slots_all, width), bf16),
            pltpu.VMEM((slots_all, hidden), bf16),
            pltpu.VMEM((slots_all, width), bf16),
            pltpu.VMEM((slots_all, 2 * hidden), bf16),
            pltpu.VMEM((slots_all, 1), f32),
            pltpu.VMEM((slots_all, 1), f32),
            pltpu.SemaphoreType.DMA((sources,)),
            pltpu.SemaphoreType.DMA((sources,)),
        ],
        compiler_params=pltpu.CompilerParams(vmem_limit_bytes=VMEM_LIMIT),
        cost_estimate=pl.CostEstimate(
            flops=flops, bytes_accessed=30 * 1024 * 1024, transcendentals=0
        ),
        name="experts",
    )(*operands)


def combine_kernel(groups, slot_ref, *refs):
    part_refs = refs[:groups]
    odd_ref, even_ref = refs[groups:]
    source = pl.program_id(0)
    local, rows = slot_ref.shape[1:]
    slots = slot_ref[source]
    selects = []
    for expert in range(local):
        same = lax.broadcasted_iota(i32, (CAP, rows), 0) == slots[expert : expert + 1, :]
        selects.append(jnp.where(same, 1.0, 0.0).astype(bf16))
    select = jnp.concatenate(selects, axis=0)
    values = jnp.concatenate(
        [ref[e] for ref in part_refs for e in range(ref.shape[0])], axis=0
    )
    result = tn(select, values).astype(bf16)

    @pl.when(source % 2 == 1)
    def _():
        odd_ref[0] = result

    @pl.when(source % 2 == 0)
    def _():
        even_ref[0] = result


def combine(slots, parts):
    sources, _, rows = slots.shape
    width = parts[0].shape[2]
    shape = jax.ShapeDtypeStruct((sources // 2, rows, width), bf16)
    spec = pl.BlockSpec((1, rows, width), lambda i: (i // 2, 0, 0))
    return pl.pallas_call(
        lambda *refs: combine_kernel(len(parts), *refs),
        grid=(sources,),
        in_specs=[pl.BlockSpec(memory_space=pltpu.VMEM)]
        + [pl.BlockSpec((p.shape[0], CAP, width), lambda i: (0, i, 0)) for p in parts],
        out_specs=[spec, spec],
        out_shape=[shape, shape],
        compiler_params=pltpu.CompilerParams(vmem_limit_bytes=VMEM_LIMIT),
        cost_estimate=pl.CostEstimate(
            flops=sources * slots.shape[1] * CAP * rows * width * 2,
            bytes_accessed=12 * 1024 * 1024, transcendentals=0,
        ),
        name="combine",
    )(slots, *parts)


def scatter_rows(odd, even):
    arrived = swap(odd, "tokens", 1)
    return scatter_chips([add_low(even[k], arrived[k]) for k in range(even.shape[0])])


def place_rows(pieces, place):
    rows = pieces[0].shape[0]
    result = jnp.zeros((rows * len(pieces),) + pieces[0].shape[1:], pieces[0].dtype)
    for key, piece in enumerate(pieces):
        result = lax.dynamic_update_slice_in_dim(result, piece, (place ^ key) * rows, axis=0)
    return result


def exchange_rows(field, place):
    count = lax.axis_size("heads")
    rows = field.shape[0] // count
    pieces = []
    for key in range(count):
        piece = lax.dynamic_slice_in_dim(field, (place ^ key) * rows, rows, axis=0)
        pieces.append(swap(piece, "heads", key) if key else piece)
    return pieces


def gather_heads(field):
    return [field] + [swap(field, "heads", key) for key in range(1, lax.axis_size("heads"))]


def body(
    tokens,
    segment_ids,
    routes,
    attn_gain,
    w_query,
    w_key,
    w_value,
    w_out,
    ffn_gain,
    router,
    w_gate,
    w_up,
    w_down,
    cotangent,
):
    rows_here = tokens.shape[0]
    model_width = tokens.shape[1]
    local_heads = w_query.shape[1] // HEAD_DIM
    local_kv = w_key.shape[1] // HEAD_DIM
    group_size = local_heads // local_kv
    seq_len = segment_ids.shape[1]
    experts_here = w_gate.shape[0]
    hidden = w_gate.shape[2]
    token_groups = lax.axis_size("tokens")
    head_groups = lax.axis_size("heads")
    place = lax.axis_index("tokens")
    head = lax.axis_index("heads")
    scaling = HEAD_DIM ** (-0.5)
    inputs = tokens.astype(f32)
    scale_one = lax.rsqrt(jnp.mean(inputs * inputs, axis=-1, keepdims=True) + epsilon)
    normed_one = (inputs * scale_one * attn_gain).astype(bf16)
    normed_pieces = gather_heads(normed_one)
    normed_full = place_rows(normed_pieces, head)

    expert_ids = jnp.arange(EXPERTS, dtype=i32)
    own_mask = jnp.sum(
        (routes.T[:, None, :] == expert_ids[None, :, None]).astype(f32), axis=0
    ).astype(bf16)
    mask_rows = EXPERTS * rows_here // model_width
    extra = (-mask_rows) % 16
    packed = jnp.concatenate(
        [
            cotangent,
            own_mask.reshape(mask_rows, model_width),
            jnp.zeros((extra, model_width), bf16),
        ],
        axis=0,
    )
    upstream_all = lax.all_gather(packed, "tokens", axis=0, tiled=False)
    masks = upstream_all[:, rows_here : rows_here + mask_rows].reshape(
        token_groups, EXPERTS, rows_here
    )
    masks = xor_order(masks.astype(f32), place)
    before = jnp.triu(jnp.ones((rows_here, rows_here), bf16), 1)
    local_masks = lax.dynamic_slice_in_dim(masks, place * experts_here, experts_here, axis=1)
    slots = jnp.einsum(
        "set,tu->seu", local_masks.astype(bf16), before, preferred_element_type=f32
    )
    slots = jnp.where(local_masks > 0, slots, -1.0).astype(i32)

    query_raw = jnp.dot(normed_full, w_query, preferred_element_type=f32).reshape(
        seq_len, local_heads, HEAD_DIM
    )
    key_raw = jnp.dot(normed_full, w_key, preferred_element_type=f32).reshape(
        seq_len, local_kv, HEAD_DIM
    )
    value_raw = jnp.dot(normed_full, w_value, preferred_element_type=f32).reshape(
        seq_len, local_kv, HEAD_DIM
    )
    out_pieces = gather_heads(lax.optimization_barrier((w_out, normed_full))[0])
    w_out_all = jnp.concatenate(out_pieces, axis=0)
    segments = segment_ids[0]
    positions = doc_positions(segment_ids)[0]
    cosine_table, sine_table = rotary_tables(positions, HEAD_DIM // 2)
    queries = rotate(query_raw, cosine_table, sine_table).astype(bf16)
    keys_rotated = rotate(key_raw, cosine_table, sine_table).astype(bf16)
    values = value_raw.astype(bf16)
    query_grouped = queries.reshape(seq_len, local_kv, group_size, HEAD_DIM)
    block_rows = min(512, seq_len)
    block_count = seq_len // block_rows
    place_ids = jnp.arange(seq_len, dtype=i32)

    def block_scores(number, query_block):
        first_row = number * block_rows
        last_row = first_row + block_rows
        allowed = (segments[first_row:last_row, None] == segments[None, :last_row]) & (
            place_ids[None, :last_row] <= place_ids[first_row:last_row, None]
        )
        scores = (
            jnp.einsum(
                "qgrd,kgd->grqk", query_block, keys_rotated[:last_row], preferred_element_type=f32
            )
            * scaling
        )
        return jnp.where(allowed, scores, masked_value)

    outputs_list = []
    log_totals = []
    for number in range(block_count):
        first_row = number * block_rows
        last_row = first_row + block_rows
        scores = block_scores(number, query_grouped[first_row:last_row])
        maximum = jnp.max(scores, axis=-1, keepdims=True)
        exponent = jnp.exp(scores - maximum)
        denominator = jnp.sum(exponent, axis=-1, keepdims=True)
        weights = (exponent / denominator).astype(bf16)
        log_totals.append(maximum + jnp.log(denominator))
        out_block = jnp.einsum(
            "grqk,kgd->qgrd", weights, values[:last_row], preferred_element_type=f32
        )
        outputs_list.append(out_block.reshape(block_rows, local_heads * HEAD_DIM))
    attended = jnp.concatenate(outputs_list, axis=0).astype(bf16)
    attended_rows = jnp.concatenate(exchange_rows(attended, head), axis=1)
    residual = inputs + jnp.dot(attended_rows, w_out_all, preferred_element_type=f32)
    scale_two = lax.rsqrt(jnp.mean(residual * residual, axis=-1, keepdims=True) + epsilon)
    normed_two = (residual * scale_two * ffn_gain).astype(bf16)
    normed_list = gather_tokens(normed_two)
    weights_packed = jnp.concatenate([w_query, w_key, w_value], axis=1)
    weights_packed = lax.optimization_barrier((weights_packed, normed_two))[0]
    weight_pieces = gather_heads(weights_packed)

    where = jnp.stack([place, head]).astype(i32)
    router_t = router.T
    chunk_sources = min(8, token_groups)
    group = min(2, experts_here)
    mixed_parts, grad_parts, dgw_parts = [], [], []
    sent_sums, kept_sums = {}, {}
    own_gate_weights = None
    for first in range(0, token_groups, chunk_sources):
        part = slice(first, first + chunk_sources)
        gate_weights = None
        mixed_groups, grad_groups, dgw_groups = [], [], []
        for first_expert in range(0, experts_here, group):
            results = run_experts(
                where, normed_list[part], upstream_all, first, slots[part], router_t,
                masks[part], gate_weights, first_expert, group, w_gate, w_up, w_down, head_groups,
            )
            if gate_weights is None:
                gate_weights = results[-1]
                if own_gate_weights is None:
                    own_gate_weights = gate_weights[0]
            mixed_groups.append(results[0])
            grad_groups.append(results[1])
            dgw_groups.append(results[2])
            for number in range(group):
                expert = first_expert + number
                sent, kept = results[3 + 2 * number], results[4 + 2 * number]
                if expert in sent_sums:
                    sent = add_low(sent, sent_sums[expert])
                    kept = add_low(kept, kept_sums[expert])
                sent_sums[expert], kept_sums[expert] = sent, kept
        mixed_parts.append((slots[part], mixed_groups))
        grad_parts.append((slots[part], grad_groups))
        dgw_parts.append(jnp.concatenate(dgw_groups, axis=0))

    def combine_all(items):
        pairs = [combine(some_slots, parts) for some_slots, parts in items]
        return [
            pairs[0][side]
            if len(pairs) == 1
            else jnp.concatenate([pair[side] for pair in pairs], axis=0)
            for side in range(2)
        ]

    dgw_all = jnp.concatenate(dgw_parts, axis=1) if len(dgw_parts) > 1 else dgw_parts[0]
    dgw_all = xor_order(jnp.swapaxes(dgw_all, 0, 1), place)
    dgw = lax.all_to_all(dgw_all, "tokens", split_axis=0, concat_axis=0, tiled=True).reshape(
        EXPERTS, rows_here
    )
    normed_grad = scatter_rows(*combine_all(grad_parts))
    weighted_sum = jnp.sum(own_gate_weights * dgw, axis=0, keepdims=True)
    logit_grads = (own_gate_weights * (dgw - weighted_sum)).astype(bf16)
    upstream = cotangent.astype(f32)
    normed_grad = normed_grad + jnp.einsum(
        "er,de->rd", logit_grads, router, preferred_element_type=f32
    )
    router_grad = jnp.einsum("er,rd->ed", logit_grads, normed_two, preferred_element_type=f32)
    hatted_two = residual * scale_two
    ffn_gain_grad = jnp.sum(normed_grad * hatted_two, axis=0)
    scaled_two = normed_grad * ffn_gain
    residual_grad = upstream + scale_two * (
        scaled_two - hatted_two * jnp.mean(scaled_two * hatted_two, axis=-1, keepdims=True)
    )
    attn_grad = residual_grad.astype(bf16)
    group_width = local_heads * HEAD_DIM
    attended_pieces = []
    for key in range(head_groups):
        piece = jnp.einsum(
            "ld,hd->lh", attn_grad, out_pieces[key], preferred_element_type=f32
        ).astype(bf16)
        attended_pieces.append(swap(piece, "heads", key) if key else piece)
    attended_grad = place_rows(attended_pieces, head)

    mixture = scatter_rows(*combine_all(mixed_parts))
    output = (residual + mixture).astype(bf16)
    small = jnp.concatenate(
        [router_grad, ffn_gain_grad[None], jnp.zeros((7, model_width), f32)], axis=0
    )
    small = sum_all(small)
    router_grad, ffn_gain_grad = small[:EXPERTS].T, small[EXPERTS]

    out_w_grad = jnp.einsum("rh,rd->hd", attended_rows, attn_grad, preferred_element_type=f32)
    out_rows = group_width // token_groups
    out_w_grad = (
        out_w_grad.astype(bf16)
        .reshape(head_groups, token_groups, out_rows, model_width)
        .swapaxes(0, 1)
        .reshape(token_groups, head_groups * out_rows, model_width)
    )
    out_w_grad = scatter_tokens(out_w_grad).astype(bf16)
    out_w_grad = out_w_grad.reshape(head_groups, out_rows, model_width)
    out_w_grad = out_w_grad[0].astype(f32) + sum(
        swap(out_w_grad[key], "heads", key).astype(f32) for key in range(1, head_groups)
    )

    gate_w, up_w, down_w = [], [], []
    wide, narrow = model_width // head_groups, hidden // head_groups
    for expert in range(experts_here):
        bit = 1 + expert % 2
        arrived = swap(sent_sums[expert], "heads", bit)
        kept = kept_sums[expert]
        passed = swap(add_low(kept[1], arrived[1]), "heads", 3 - bit)
        total = kept[0].astype(f32) + arrived[0].astype(f32) + passed.astype(f32)
        gate_w.append(total[:wide])
        up_w.append(total[wide : 2 * wide])
        down_w.append(
            jnp.concatenate(
                [total[2 * wide : 2 * wide + narrow], total[2 * wide + narrow :]], axis=1
            )
        )
    gate_w_grad, up_w_grad, down_w_grad = jnp.stack(gate_w), jnp.stack(up_w), jnp.stack(down_w)

    out_grad_grouped = attended_grad.reshape(seq_len, local_kv, group_size, HEAD_DIM)
    key_acc = jnp.zeros((seq_len, local_kv, HEAD_DIM), f32)
    value_acc = jnp.zeros((seq_len, local_kv, HEAD_DIM), f32)
    query_parts = []
    for number in range(block_count):
        first_row = number * block_rows
        last_row = first_row + block_rows
        query_block = query_grouped[first_row:last_row]
        scores = block_scores(number, query_block)
        probs_float = jnp.exp(scores - log_totals[number])
        probs_low = probs_float.astype(bf16)
        out_grad_block = out_grad_grouped[first_row:last_row]
        prob_grads = jnp.einsum(
            "qgrd,kgd->grqk", out_grad_block, values[:last_row], preferred_element_type=f32
        )
        offset = jnp.sum(probs_float * prob_grads, axis=-1, keepdims=True)
        score_grads = (probs_float * (prob_grads - offset)).astype(bf16)
        query_parts.append(
            jnp.einsum(
                "grqk,kgd->qgrd", score_grads, keys_rotated[:last_row], preferred_element_type=f32
            )
            * scaling
        )
        key_acc = key_acc.at[:last_row].add(
            jnp.einsum("grqk,qgrd->kgd", score_grads, query_block, preferred_element_type=f32)
            * scaling
        )
        value_acc = value_acc.at[:last_row].add(
            jnp.einsum("grqk,qgrd->kgd", probs_low, out_grad_block, preferred_element_type=f32)
        )
    query_rot_grad = jnp.concatenate(query_parts, axis=0).reshape(seq_len, local_heads, HEAD_DIM)
    query_grad = (
        rotate(query_rot_grad, cosine_table, -sine_table)
        .astype(bf16)
        .reshape(seq_len, local_heads * HEAD_DIM)
    )
    key_grad = (
        rotate(key_acc, cosine_table, -sine_table)
        .astype(bf16)
        .reshape(seq_len, local_kv * HEAD_DIM)
    )
    value_grad = value_acc.astype(bf16).reshape(seq_len, local_kv * HEAD_DIM)
    packed_grad = jnp.concatenate([query_grad, key_grad, value_grad], axis=1)
    grad_pieces = exchange_rows(packed_grad, head)
    normed_one_grad = sum(
        jnp.einsum("lh,dh->ld", piece, weight, preferred_element_type=f32)
        for piece, weight in zip(grad_pieces, weight_pieces)
    )
    hatted_one = inputs * scale_one
    attn_gain_grad = jnp.sum(normed_one_grad * hatted_one, axis=0)
    attn_gain_grad = sum_all(attn_gain_grad.reshape(-1, 128)).reshape(model_width)
    scaled_one = normed_one_grad * attn_gain
    input_grad = residual_grad + scale_one * (
        scaled_one - hatted_one * jnp.mean(scaled_one * hatted_one, axis=-1, keepdims=True)
    )
    packed_w_grad = jnp.einsum("ld,lh->dh", normed_full, packed_grad, preferred_element_type=f32)
    packed_w_grad = scatter_tokens(
        packed_w_grad.astype(bf16).reshape(
            token_groups, model_width // token_groups, packed_grad.shape[1]
        )
    )
    key_start, value_start = group_width, group_width + local_kv * HEAD_DIM
    return (
        output,
        input_grad,
        attn_gain_grad,
        packed_w_grad[:, :key_start],
        packed_w_grad[:, key_start:value_start],
        packed_w_grad[:, value_start:],
        out_w_grad,
        ffn_gain_grad,
        router_grad,
        gate_w_grad,
        up_w_grad,
        down_w_grad,
    )


def solution(mesh):
    placed = (
        P(("tokens", "heads"), None),
        P("tokens", None),
        P(("tokens", "heads"), None),
        P(),
        P(None, "heads"),
        P(None, "heads"),
        P(None, "heads"),
        P("heads", None),
        P(),
        P(),
        P("tokens", None, None),
        P("tokens", None, None),
        P("tokens", None, None),
        P(("tokens", "heads"), None),
    )
    return jax.shard_map(
        body,
        mesh=mesh,
        in_specs=placed,
        out_specs=(
            P(("tokens", "heads"), None),
            P(("tokens", "heads"), None),
            P(),
            P("tokens", "heads"),
            P("tokens", "heads"),
            P("tokens", "heads"),
            P(("heads", "tokens"), None),
            P(),
            P(),
            P("tokens", "heads", None),
            P("tokens", "heads", None),
            P("tokens", "heads", None),
        ),
        check_vma=False,
    )
```

```python
import jax
import jax.numpy as jnp
from jax import lax
from jax.experimental import pallas as pl
from jax.experimental.pallas import tpu as pltpu
from jax.sharding import PartitionSpec as P

HEAD_DIM = 64
EXPERTS = 32
TOP = 8
CAP = 96


epsilon = 1e-06
theta_base = 10000.0
masked_value = -1e30


def doc_positions(segments):
    axis_last = segments.ndim - 1
    place_ids = lax.broadcasted_iota(jnp.int32, segments.shape, axis_last)
    previous = jnp.concatenate([segments[..., :1] - 1, segments[..., :-1]], axis=axis_last)
    starts = jnp.where(segments != previous, place_ids, 0)
    return place_ids - lax.cummax(starts, axis=axis_last)


def rotary_tables(positions, half_size):
    frequency = theta_base ** (
        -(jnp.arange(half_size, dtype=jnp.float32) * 2.0) / (2.0 * half_size)
    )
    angles = positions.astype(jnp.float32)[..., None] * frequency
    return (jnp.cos(angles), jnp.sin(angles))


def rotate(field, cosine_table, sine_table):
    half_size = field.shape[-1] // 2
    leading = field[..., :half_size]
    trailing = field[..., half_size:]
    cos_part = cosine_table[..., None, :]
    sin_part = sine_table[..., None, :]
    return jnp.concatenate(
        [leading * cos_part - trailing * sin_part, trailing * cos_part + leading * sin_part],
        axis=-1,
    )


f32 = jnp.float32
bf16 = jnp.bfloat16
i32 = jnp.int32
VMEM_LIMIT = 60 * 1024 * 1024
ATTENTION_LIMIT = 24 * 1024 * 1024
CHUNK = 4


def swap(field, axis, bit):
    count = lax.axis_size(axis)
    return lax.ppermute(field, axis, [(i, i ^ bit) for i in range(count)])


def gather_tokens(field, other):
    count = lax.axis_size("tokens")
    held = {0: field}
    early = swap(field, "tokens", 2) if count > 2 else field
    bit = count // 2
    while bit > 1:
        for key in list(held):
            source = after(held[key], other) if key else held[key]
            held[key | bit] = early if bit == 2 and not key else swap(source, "tokens", bit)
        bit //= 2
    held.update({key | 1: swap(held[key], "tokens", 1) for key in list(held)})
    return [held[key] for key in range(count)], early


def add_low(left, right):
    return (left.astype(f32) + right.astype(f32)).astype(bf16)


def scatter_chips(terms, one_by_one=True):
    terms = {key: list(some) for key, some in enumerate(terms)}
    count = len(terms)
    bit, marks = 1, []

    def total(key):
        result = terms[key][0].astype(f32)
        for other in terms[key][1:]:
            result = result + other.astype(f32)
        return result

    while bit < count:
        last = None
        for key in sorted((k for k in terms if k & bit), reverse=True):
            low = total(key).astype(bf16)
            marks.append(low)
            if one_by_one and last is not None:
                low = after(low, last)
            last = swap(low, "tokens", 2 * bit)
            terms[key ^ bit].append(last)
            del terms[key]
        bit *= 2
    return total(0), marks


def after(field, *others):
    return lax.optimization_barrier((field, *others))[0]


def scatter_tokens(field):
    count, rows, columns = field.shape
    place = lax.axis_index("tokens")
    chip, core = place // 2, place % 2
    paired = field.reshape(count // 2, 2, rows, columns)
    sent = lax.dynamic_index_in_dim(paired, 1 - core, axis=1, keepdims=False)
    kept = lax.dynamic_index_in_dim(paired, core, axis=1, keepdims=False)
    both = add_low(kept, swap(sent, "tokens", 1))
    parts = [
        [lax.dynamic_index_in_dim(both, chip ^ key, axis=0, keepdims=False)]
        for key in range(count // 2)
    ]
    return scatter_chips(parts)[0]


def sum_axis(field, axis):
    bit = 1
    while bit < lax.axis_size(axis):
        field = field + swap(field, axis, bit)
        bit *= 2
    return field


def xor_order(field, place):
    count = field.shape[0]
    rest = field.shape[1:]
    bit = 1
    while bit < count:
        split = field.reshape((count // (2 * bit), 2, bit) + rest)
        flipped = jnp.concatenate([split[:, 1:], split[:, :1]], axis=1)
        field = jnp.where((place & bit) != 0, flipped, split).reshape((count,) + rest)
        bit *= 2
    return field


def nn(left, right):
    return lax.dot_general(left, right, (((1,), (0,)), ((), ())), preferred_element_type=f32)


def nt(left, right):
    return lax.dot_general(left, right, (((1,), (1,)), ((), ())), preferred_element_type=f32)


def tn(left, right):
    return lax.dot_general(left, right, (((0,), (0,)), ((), ())), preferred_element_type=f32)


def select_columns(slots, local):
    rows = slots.shape[1]
    slots = jnp.transpose(slots)
    lanes = lax.broadcasted_iota(i32, (rows, local * CAP), 1)
    same = None
    for expert in range(local):
        column = slots[:, expert : expert + 1]
        term = lanes == jnp.where(column < 0, -1, column + expert * CAP)
        same = term if same is None else same | term
    return jnp.where(same, 1.0, 0.0).astype(bf16)


def turn(field, cosine, sine, sign):
    lanes = lax.broadcasted_iota(i32, field.shape, 1)
    partner = jnp.where(
        lanes % HEAD_DIM < HEAD_DIM // 2,
        -pltpu.roll(field, 128 - HEAD_DIM // 2, 1),
        pltpu.roll(field, HEAD_DIM // 2, 1),
    )
    return field * cosine + sign * (partner * sine)


def keep_half(field, side):
    lanes = lax.broadcasted_iota(i32, field.shape, 1)
    return jnp.where((lanes >= HEAD_DIM) == (side == 1), field, jnp.zeros_like(field))


def join_halves(low, high):
    lanes = lax.broadcasted_iota(i32, low.shape, 1)
    return jnp.where(lanes < HEAD_DIM, low, high)


def attention_forward_kernel(
    raw_ref, cosine_ref, sine_ref, start_ref, out_ref, turned_ref, log_ref, swapped_ref
):
    length = raw_ref.shape[0]
    rows = 256
    scaling = HEAD_DIM ** (-0.5)
    for first in range(0, length, rows):
        some = pl.ds(first, rows)
        cosine, sine = cosine_ref[some, :], sine_ref[some, :]
        for part in range(2):
            lanes = pl.ds(128 * part, 128)
            query = turn(raw_ref[some, lanes], cosine, sine, 1.0).astype(bf16)
            turned_ref[some, lanes] = (query.astype(f32) * scaling).astype(bf16)
        key = turn(raw_ref[some, pl.ds(256, 128)], cosine, sine, 1.0)
        value = raw_ref[some, pl.ds(384, 128)]
        turned_ref[some, pl.ds(256, 128)] = key.astype(bf16)
        turned_ref[some, pl.ds(384, 128)] = value.astype(bf16)
        swapped_ref[some, pl.ds(0, 128)] = pltpu.roll(key, HEAD_DIM, 1).astype(bf16)
        swapped_ref[some, pl.ds(128, 128)] = pltpu.roll(value, HEAD_DIM, 1).astype(bf16)
    for first in range(0, length, rows):
        some = pl.ds(first, rows)
        low = max(0, first - 512)
        span = pl.ds(low, first + rows - low)
        columns = first + rows - low
        keys = lax.broadcasted_iota(i32, (rows, columns), 1) + low
        queries = lax.broadcasted_iota(i32, (rows, columns), 0) + first
        allowed = (keys <= queries) & (keys >= start_ref[some, :])
        for pair in range(2):
            query = turned_ref[some, pl.ds(128 * pair, 128)]
            halves = []
            for side in range(2):
                if pair == side:
                    key, value = turned_ref[span, pl.ds(256, 128)], turned_ref[span, pl.ds(384, 128)]
                else:
                    key, value = swapped_ref[span, pl.ds(0, 128)], swapped_ref[span, pl.ds(128, 128)]
                scores = jnp.where(allowed, nt(keep_half(query, side), key), masked_value)
                top = jnp.max(scores, axis=1, keepdims=True)
                exponent = jnp.exp(scores - top)
                total = jnp.sum(exponent, axis=1, keepdims=True)
                weights = (exponent * (1.0 / total)).astype(bf16)
                halves.append(nn(weights, value))
                number = 2 * pair + side
                log_ref[some, pl.ds(number, 1)] = top + jnp.log(total)
            out_ref[some, pl.ds(128 * pair, 128)] = join_halves(*halves).astype(bf16)


def attention_backward_kernel(
    turned_ref, grad_ref, log_ref, start_ref, cosine_ref, sine_ref, out_ref,
    swapped_ref, key_acc, value_acc,
):
    length = turned_ref.shape[0]
    rows = 256
    scaling = HEAD_DIM ** (-0.5)
    key_acc[...] = jnp.zeros_like(key_acc)
    value_acc[...] = jnp.zeros_like(value_acc)
    for first in range(0, length, rows):
        some = pl.ds(first, rows)
        for part in range(2):
            field = turned_ref[some, pl.ds(256 + 128 * part, 128)].astype(f32)
            swapped_ref[some, pl.ds(128 * part, 128)] = pltpu.roll(field, HEAD_DIM, 1).astype(bf16)
    for first in range(0, length, rows):
        some = pl.ds(first, rows)
        low = max(0, first - 512)
        count = first + rows - low
        span = pl.ds(low, count)
        keys = lax.broadcasted_iota(i32, (count, rows), 0) + low
        queries = lax.broadcasted_iota(i32, (count, rows), 1) + first
        allowed = (keys <= queries) & (keys >= start_ref[:, some])
        for pair in range(2):
            query = turned_ref[some, pl.ds(128 * pair, 128)]
            grad = grad_ref[some, pl.ds(128 * pair, 128)]
            halves = []
            for side in range(2):
                if pair == side:
                    key, value = turned_ref[span, pl.ds(256, 128)], turned_ref[span, pl.ds(384, 128)]
                else:
                    key, value = swapped_ref[span, pl.ds(0, 128)], swapped_ref[span, pl.ds(128, 128)]
                mine, mine_grad = keep_half(query, side), keep_half(grad, side)
                scores = jnp.where(allowed, nt(key, mine), masked_value)
                number = 2 * pair + side
                probs = jnp.exp(scores - log_ref[pl.ds(number, 1), some])
                prob_grads = nt(value, mine_grad)
                offset = jnp.sum(probs * prob_grads, axis=0, keepdims=True)
                score_grads = (probs * (prob_grads - offset)).astype(bf16)
                halves.append(tn(score_grads, key) * scaling)
                kind = 0 if pair == side else 1
                key_acc[kind, span, :] += nn(score_grads, mine)
                value_acc[kind, span, :] += nn(probs.astype(bf16), mine_grad)
            cosine, sine = cosine_ref[some, :], sine_ref[some, :]
            out_ref[some, pl.ds(128 * pair, 128)] = turn(
                join_halves(*halves), cosine, sine, -1.0
            ).astype(bf16)
    for first in range(0, length, rows):
        some = pl.ds(first, rows)
        cosine, sine = cosine_ref[some, :], sine_ref[some, :]
        key = key_acc[0, some, :] + pltpu.roll(key_acc[1, some, :], HEAD_DIM, 1)
        value = value_acc[0, some, :] + pltpu.roll(value_acc[1, some, :], HEAD_DIM, 1)
        out_ref[some, pl.ds(256, 128)] = turn(key, cosine, sine, -1.0).astype(bf16)
        out_ref[some, pl.ds(384, 128)] = value.astype(bf16)


def small_cost():
    return pl.CostEstimate(flops=1000000, bytes_accessed=100000, transcendentals=0)


def attention_forward(raw, cosine, sine, starts):
    length = raw.shape[0]
    return pl.pallas_call(
        attention_forward_kernel,
        out_shape=[
            jax.ShapeDtypeStruct((length, 256), bf16),
            jax.ShapeDtypeStruct((length, 512), bf16),
            jax.ShapeDtypeStruct((length, 8), f32),
        ],
        scratch_shapes=[pltpu.VMEM((length, 256), bf16)],
        compiler_params=pltpu.CompilerParams(vmem_limit_bytes=ATTENTION_LIMIT),
        cost_estimate=small_cost(),
        name="attention_forward",
    )(raw, cosine, sine, starts)


def attention_backward(turned, grad, logs, starts, cosine, sine):
    length = turned.shape[0]
    return pl.pallas_call(
        attention_backward_kernel,
        out_shape=jax.ShapeDtypeStruct((length, 512), bf16),
        scratch_shapes=[
            pltpu.VMEM((length, 256), bf16),
            pltpu.VMEM((2, length, 128), f32),
            pltpu.VMEM((2, length, 128), f32),
        ],
        compiler_params=pltpu.CompilerParams(vmem_limit_bytes=ATTENTION_LIMIT),
        cost_estimate=small_cost(),
        name="attention_backward",
    )(turned, grad, logs, starts, cosine, sine)


def expert_kernel(sources, first_source, count, heads, chunk, absolute, *refs):
    refs = list(refs)
    where_ref = refs.pop(0)
    hn_refs = [refs.pop(0) for _ in range(sources)]
    g_hbm, slot_ref, gw_ref, gate_ref, up_ref, down_ref = refs[:6]
    ye_ref, even_ref, odd_ref, dgw_ref = refs[6:10]
    outs = [refs[10 + 4 * k : 14 + 4 * k] for k in range(count)]
    h_ref, g_ref, x_ref, xr_ref, gx_ref, act_ref, dye_ref, dgu_ref, gws_ref, dcol_ref = refs[
        10 + 4 * count : 20 + 4 * count
    ]
    dxe_ref, sum_ref, h_sem, g_sem, out_sem = refs[20 + 4 * count :]
    step = pl.program_id(0)
    expert = jnp.minimum(step, count - 1)
    place, head = where_ref[0], where_ref[1]
    rows = h_ref.shape[1]
    width = h_ref.shape[2]
    hidden = act_ref.shape[1]
    wide, narrow = width // heads, hidden // heads
    group = chunk // CAP

    def origin(s):
        return place ^ (first_source + s)

    def copy_h(s):
        return pltpu.make_async_copy(hn_refs[s], h_ref.at[s], h_sem.at[s])

    def copy_g(s):
        return pltpu.make_async_copy(g_hbm.at[origin(s)], g_ref.at[s], g_sem.at[s])

    def copy_out(number, side):
        slot = number % 2
        return pltpu.make_async_copy(
            sum_ref.at[slot, side],
            outs[number][side],
            out_sem.at[4 * slot + side],
        )

    @pl.when(step == 0)
    def _():
        for s in range(sources):
            copy_h(s).start()
        for s in range(sources):
            copy_g(s).start()
        for s in range(sources):
            copy_h(s).wait()

    def chosen(s):
        slots = slot_ref[origin(s), pl.ds(expert, 1), :]
        return lax.broadcasted_iota(i32, (CAP, rows), 0) == slots

    def pick(s):
        same = chosen(s)
        select = jnp.where(same, 1.0, 0.0).astype(bf16)
        mine = pl.ds(s * CAP, CAP)
        x = nn(select, h_ref[s]).astype(bf16)
        x_ref[mine, :] = x
        for owner in range(heads):
            target = pl.multiple_of((owner ^ head) * wide, wide)
            xr_ref[mine, pl.ds(target, wide)] = x[:, owner * wide : (owner + 1) * wide]
        row = gw_ref[origin(s), pl.ds(expert, 1), :]
        gws_ref[mine, :] = jnp.sum(jnp.where(same, row, 0.0), axis=1, keepdims=True)

    def pick_grad(s):
        select = jnp.where(chosen(s), 1.0, 0.0).astype(bf16)
        gx_ref[pl.ds(s * CAP, CAP), :] = nn(select, g_ref[s]).astype(bf16)

    def work(number):
        part = pl.ds(pl.multiple_of(number * chunk, chunk), chunk)
        some = pl.ds(number * group, group)
        x = x_ref[part, :]
        gate = nn(x, gate_ref[0])
        up = nn(x, up_ref[0])
        sigma = 1.0 / (1.0 + jnp.exp(-gate))
        silu = gate * sigma
        act = (silu * up).astype(bf16)
        for owner in range(heads):
            target = pl.multiple_of((owner ^ head) * narrow, narrow)
            act_ref[part, pl.ds(target, narrow)] = act[:, owner * narrow : (owner + 1) * narrow]
        gx = gx_ref[part, :].astype(f32)
        weights = gws_ref[part, :]
        dye = (gx * weights).astype(bf16)
        dye_ref[part, :] = dye
        ye = nn(act, down_ref[0]).astype(bf16).astype(f32)
        dcol_ref[part, :] = jnp.sum(gx * ye, axis=1, keepdims=True)
        ye_ref[some, 0] = (ye * weights).astype(bf16).reshape(group, CAP, width)
        dact = nt(dye, down_ref[0])
        dgate = (dact * up * sigma * (1.0 + gate * (1.0 - sigma))).astype(bf16)
        dup = (dact * silu).astype(bf16)
        dgu_ref[part, pl.ds(0, hidden)] = dgate
        dgu_ref[part, pl.ds(hidden, hidden)] = dup
        dxe = (nt(dgate, gate_ref[0]) + nt(dup, up_ref[0])).astype(bf16)
        dxe_ref[some, expert] = dxe.reshape(group, CAP, width)

    @pl.when(step < count)
    def _():
        for s in range(sources):
            pick(s)

        @pl.when(step == 0)
        def _():
            for s in range(sources):
                copy_g(s).wait()

        for s in range(sources):
            pick_grad(s)
        pl.loop(0, sources // group)(work)
        for s in range(sources):
            column = dcol_ref[pl.ds(s * CAP, CAP), :]
            index = origin(s) if absolute else s
            dgw_ref[index, pl.ds(expert, 1), :] = jnp.sum(
                jnp.where(chosen(s), column, 0.0), axis=0, keepdims=True
            )

        down = tn(act_ref[...], dye_ref[...]).astype(bf16)
        for number in range(2, count):

            @pl.when(step == number)
            def _():
                for side in range(4):
                    copy_out(number - 2, side).wait()

        slot = lax.rem(step, 2)
        for relative, position in ((0, 3), (1, 2 * slot), (2, 2 - 2 * slot), (3, 1)):
            both = tn(xr_ref[:, pl.ds(relative * wide, wide)], dgu_ref[...]).astype(bf16)
            target_ref = sum_ref.at[slot, position]
            target_ref[pl.ds(0, wide), :] = both[:, :hidden]
            target_ref[pl.ds(wide, wide), :] = both[:, hidden:]
            low = down[relative * narrow : (relative + 1) * narrow]
            target_ref[pl.ds(2 * wide, narrow), :] = low[:, :hidden]
            target_ref[pl.ds(2 * wide + narrow, narrow), :] = low[:, hidden:]
        for number in range(count):

            @pl.when(step == number)
            def _():
                for side in range(4):
                    copy_out(number, side).start()

    @pl.when(step >= count)
    def _():
        pair = step - count
        for side, out_ref in enumerate((even_ref, odd_ref)):
            select = select_columns(slot_ref[place ^ (first_source + 2 * pair + side)], count)
            values = dxe_ref[2 * pair + side].reshape(count * CAP, width)
            out_ref[0] = nn(select, values).astype(bf16)

        @pl.when(pair == sources // 2 - 1)
        def _():
            for number in range(max(0, count - 2), count):
                for side in range(4):
                    copy_out(number, side).wait()


def run_experts(
    where, hn_list, upstream_all, first_source, slots, gate_weights, w_gate, w_up, w_down, heads,
):
    sources = len(hn_list)
    rows, width = hn_list[0].shape
    count, _, hidden = w_gate.shape
    slots_all = sources * CAP
    block = 3 * (width // heads)
    whole = pl.BlockSpec(memory_space=pltpu.VMEM)
    hbm = pl.BlockSpec(memory_space=pl.ANY)
    chunk = CHUNK * CAP
    absolute = sources == slots.shape[0]

    def of_expert(shape):
        return pl.BlockSpec(shape, lambda i: (jnp.minimum(i, count - 1), 0, 0))

    def of_pair(i):
        return (jnp.maximum(i - count, 0), 0, 0)

    half = jax.ShapeDtypeStruct((sources // 2, rows, width), bf16)
    out_shape = [
        jax.ShapeDtypeStruct((sources, count, CAP, width), bf16),
        half,
        half,
        jax.ShapeDtypeStruct((sources, count, rows), f32),
    ]
    out_specs = [
        pl.BlockSpec((sources, 1, CAP, width), lambda i: (0, jnp.minimum(i, count - 1), 0, 0)),
        pl.BlockSpec((1, rows, width), of_pair),
        pl.BlockSpec((1, rows, width), of_pair),
        whole,
    ]
    one = jax.ShapeDtypeStruct((block, hidden), bf16)
    out_shape += [one] * (4 * count)
    out_specs += [hbm] * (4 * count)

    def kernel(*refs):
        expert_kernel(sources, first_source, count, heads, chunk, absolute, *refs)

    return pl.pallas_call(
        kernel,
        grid=(count + sources // 2,),
        in_specs=[pl.BlockSpec(memory_space=pltpu.SMEM)]
        + [hbm] * sources
        + [hbm, whole, whole]
        + [
            of_expert((1, width, hidden)),
            of_expert((1, width, hidden)),
            of_expert((1, hidden, width)),
        ],
        out_specs=out_specs,
        out_shape=out_shape,
        scratch_shapes=[
            pltpu.VMEM((sources, rows, width), bf16),
            pltpu.VMEM((sources, rows, width), bf16),
            pltpu.VMEM((slots_all, width), bf16),
            pltpu.VMEM((slots_all, width), bf16),
            pltpu.VMEM((slots_all, width), bf16),
            pltpu.VMEM((slots_all, hidden), bf16),
            pltpu.VMEM((slots_all, width), bf16),
            pltpu.VMEM((slots_all, 2 * hidden), bf16),
            pltpu.VMEM((slots_all, 1), f32),
            pltpu.VMEM((slots_all, 1), f32),
            pltpu.VMEM((sources, count, CAP, width), bf16),
            pltpu.VMEM((2, 4, block, hidden), bf16),
            pltpu.SemaphoreType.DMA((sources,)),
            pltpu.SemaphoreType.DMA((sources,)),
            pltpu.SemaphoreType.DMA((8,)),
        ],
        compiler_params=pltpu.CompilerParams(vmem_limit_bytes=VMEM_LIMIT),
        cost_estimate=small_cost(),
        name="experts",
    )(where, *hn_list, upstream_all, slots, gate_weights, w_gate, w_up, w_down)


def combine_kernel(first_source, where_ref, slot_ref, part_ref, even_ref, odd_ref):
    pair = pl.program_id(0)
    place = where_ref[0]
    count, cap, width = part_ref.shape[1:]
    for side, out_ref in enumerate((even_ref, odd_ref)):
        select = select_columns(slot_ref[place ^ (first_source + 2 * pair + side)], count)
        out_ref[0] = nn(select, part_ref[side].reshape(count * cap, width)).astype(bf16)


def combine(where, slots, part, first_source):
    sources, count, cap, width = part.shape
    rows = slots.shape[2]
    shape = jax.ShapeDtypeStruct((sources // 2, rows, width), bf16)
    spec = pl.BlockSpec((1, rows, width), lambda i: (i, 0, 0))
    return pl.pallas_call(
        lambda *refs: combine_kernel(first_source, *refs),
        grid=(sources // 2,),
        in_specs=[
            pl.BlockSpec(memory_space=pltpu.SMEM),
            pl.BlockSpec(memory_space=pltpu.VMEM),
            pl.BlockSpec((2, count, cap, width), lambda i: (i, 0, 0, 0)),
        ],
        out_specs=[spec, spec],
        out_shape=[shape, shape],
        compiler_params=pltpu.CompilerParams(vmem_limit_bytes=VMEM_LIMIT),
        cost_estimate=small_cost(),
        name="combine",
    )(where, slots, part)


def finish_kernel(*refs):
    in_ref, pair_ref, down_ref, in_sem, out_sem = refs[-5:]
    outs = refs[-8:-5]
    fields = refs[:-8]
    count = len(fields) // 3
    wide, hidden = pair_ref.shape[2:]
    narrow = down_ref.shape[1]

    def arrive(number):
        return pltpu.make_async_copy(fields[number], in_ref.at[number], in_sem.at[number])

    def leave(e, kind):
        source = pair_ref.at[e, kind] if kind < 2 else down_ref.at[e]
        return pltpu.make_async_copy(source, outs[kind].at[e], out_sem.at[3 * e + kind])

    for e in range(count):
        for kind in range(3):
            arrive(kind * count + e).start()
    for e in range(count):
        for kind in range(3):
            arrive(kind * count + e).wait()

        def total(first, rows):
            part = pl.ds(first, rows)
            return (
                in_ref[e, part, :].astype(f32)
                + in_ref[count + e, part, :].astype(f32)
                + in_ref[2 * count + e, part, :].astype(f32)
            )

        for kind in range(2):
            pair_ref[e, kind] = total(kind * wide, wide)
        down_ref[e, :, pl.ds(0, hidden)] = total(2 * wide, narrow)
        down_ref[e, :, pl.ds(hidden, hidden)] = total(2 * wide + narrow, narrow)
        for kind in range(3):
            leave(e, kind).start()
    for e in range(count):
        for kind in range(3):
            leave(e, kind).wait()


def scatter_rows(odd, even, one_by_one=True):
    arrived = swap(odd, "tokens", 1)
    return scatter_chips([[even[k], arrived[k]] for k in range(even.shape[0])], one_by_one)


def place_rows(pieces, place):
    rows = pieces[0].shape[0]
    result = jnp.concatenate([pieces[0]] * (len(pieces) - 1), axis=0)
    for key, piece in list(enumerate(pieces))[1:]:
        start = (place ^ key) * rows if key < 4 else (place ^ 3) * rows + rows // 2
        result = lax.dynamic_update_slice_in_dim(result, piece, start, axis=0)
    return result


def place_small(pieces, place):
    count = len(pieces)
    blocks = []
    for block in range(count):
        chosen = pieces[0]
        for key in range(1, count):
            chosen = jnp.where((place ^ key) == block, pieces[key], chosen)
        blocks.append(chosen)
    return jnp.concatenate(blocks, axis=0)


def exchange_rows(field, place):
    count = lax.axis_size("heads")
    rows = field.shape[0] // count
    pieces = []
    for key in range(count):
        piece = lax.dynamic_slice_in_dim(field, (place ^ key) * rows, rows, axis=0)
        pieces.append(swap(piece, "heads", key) if key else piece)
    return pieces


def gather_heads(field):
    half = field.shape[0] // 2
    one, two = swap(field, "heads", 1), swap(field, "heads", 2)
    return [field, one, two, swap(two[:half], "heads", 1), swap(one[half:], "heads", 2)]


def body(
    tokens,
    segment_ids,
    routes,
    attn_gain,
    w_query,
    w_key,
    w_value,
    w_out,
    ffn_gain,
    router,
    w_gate,
    w_up,
    w_down,
    cotangent,
):
    rows_here = tokens.shape[0]
    model_width = tokens.shape[1]
    local_heads = w_query.shape[1] // HEAD_DIM
    local_kv = w_key.shape[1] // HEAD_DIM
    group_size = local_heads // local_kv
    seq_len = segment_ids.shape[1]
    experts_here = w_gate.shape[0]
    hidden = w_gate.shape[2]
    token_groups = lax.axis_size("tokens")
    head_groups = lax.axis_size("heads")
    place = lax.axis_index("tokens")
    head = lax.axis_index("heads")
    scaling = HEAD_DIM ** (-0.5)
    inputs = tokens.astype(f32)
    scale_one = lax.rsqrt(jnp.mean(inputs * inputs, axis=-1, keepdims=True) + epsilon)
    normed_one = (inputs * scale_one * attn_gain).astype(bf16)
    normed_pieces = gather_heads(normed_one)
    weights_packed = jnp.concatenate([w_query, w_key, w_value], axis=1)

    expert_ids = jnp.arange(EXPERTS, dtype=i32)
    own_mask = jnp.sum(
        (routes.T[:, None, :] == expert_ids[None, :, None]).astype(f32), axis=0
    )

    def to_experts(field):
        return lax.all_to_all(
            field, "tokens", split_axis=0, concat_axis=0, tiled=True
        ).reshape(token_groups, experts_here, rows_here)

    masks = to_experts(own_mask)
    normed_full = place_rows([after(normed_one, masks), *normed_pieces[1:]], head)
    upstream_all = lax.all_gather(cotangent, "tokens", axis=0, tiled=False)
    before = jnp.triu(jnp.ones((rows_here, rows_here), bf16), 1)
    slots = jnp.einsum("set,tu->seu", masks.astype(bf16), before, preferred_element_type=f32)
    slots = jnp.where(masks > 0, slots, -1.0).astype(i32)
    slots = jnp.pad(slots, ((0, 0), (0, (-experts_here) % 8), (0, 0)), constant_values=-1)
    positions = doc_positions(segment_ids)[0]
    starts = jnp.arange(seq_len, dtype=i32) - positions
    cosine_table, sine_table = rotary_tables(positions, HEAD_DIM // 2)
    cosine_table = jnp.tile(cosine_table, (1, 4))
    sine_table = jnp.tile(sine_table, (1, 4))
    start_column, start_row = starts[:, None], starts[None]
    normed_full, slots, cosine_table, sine_table, weights_packed, start_column, start_row = (
        lax.optimization_barrier(
            (
                normed_full, slots, cosine_table, sine_table, weights_packed, start_column,
                start_row,
            )
        )
    )
    out_pieces = gather_heads(after(w_out, *normed_pieces[3:]))
    w_out_all = jnp.concatenate(out_pieces, axis=0)

    group_width = local_heads * HEAD_DIM
    key_start, value_start = group_width, group_width + local_kv * HEAD_DIM
    raw = jnp.dot(normed_full, weights_packed, preferred_element_type=f32)
    attended, turned, logs = attention_forward(raw, cosine_table, sine_table, start_column)
    attended_rows = jnp.concatenate(exchange_rows(attended, head), axis=1)
    residual = inputs + jnp.dot(attended_rows, w_out_all, preferred_element_type=f32)
    scale_two = lax.rsqrt(jnp.mean(residual * residual, axis=-1, keepdims=True) + epsilon)
    normed_two = (residual * scale_two * ffn_gain).astype(bf16)
    logits = jnp.einsum("de,rd->er", router, normed_two, preferred_element_type=f32)
    top = jnp.max(jnp.where(own_mask > 0, logits, masked_value), axis=0, keepdims=True)
    exponent = jnp.where(own_mask > 0, jnp.exp(logits - top), 0.0)
    own_gate_weights = exponent / jnp.sum(exponent, axis=0, keepdims=True)
    gate_weights = to_experts(own_gate_weights)
    normed_list, early = gather_tokens(normed_two, gate_weights)
    weights_sent = after(weights_packed, early)
    weight_pieces = [weights_packed] + [
        swap(weights_sent, "heads", key) for key in range(1, head_groups)
    ]
    weights_all = jnp.concatenate(weight_pieces, axis=1)

    where = jnp.stack([place, head]).astype(i32)
    chunk_sources = min(8, token_groups)
    results = []
    for first in range(0, token_groups, chunk_sources):
        results.append(
            run_experts(
                where, normed_list[first : first + chunk_sources], upstream_all, first, slots,
                gate_weights, w_gate, w_up, w_down, head_groups,
            )
        )

    def joined(parts):
        return parts[0] if len(parts) == 1 else jnp.concatenate(parts, axis=0)

    grad_even, grad_odd, dgw_all = (joined([r[k] for r in results]) for k in (1, 2, 3))
    weight_sums = results[0][4:]
    for other in results[1:]:
        weight_sums = [add_low(mine, more) for mine, more in zip(weight_sums, other[4:])]
    if len(results) > 1:
        dgw_all = xor_order(dgw_all, place)
    grad_odd = after(grad_odd, *weight_pieces[1:])
    normed_grad, marks = scatter_rows(grad_odd, grad_even)
    own_gate_weights = after(own_gate_weights, marks[-1])
    dgw = lax.all_to_all(
        after(dgw_all, marks[0]), "tokens", split_axis=0, concat_axis=0, tiled=True
    ).reshape(EXPERTS, rows_here)
    mixed = [
        combine(where, slots, after(r[0], marks[-1]), chunk_sources * number)
        for number, r in enumerate(results)
    ]
    mixed_even, mixed_odd = (joined([pair[k] for pair in mixed]) for k in (0, 1))

    def send(expert, number, *anchors):
        part = weight_sums[4 * expert + number]
        part = after(part, *anchors) if anchors else part
        return swap(part, "heads", 1 + expert % 2)

    pair = min(2, experts_here)
    arrived = {(e, number): send(e, number) for e in range(pair) for number in (1, 0)}

    def passed_on(expert, anchor):
        kept = after(weight_sums[4 * expert + 2], anchor)
        return add_low(kept, arrived[expert, 1])

    middle = {e: passed_on(e, marks[-1]) for e in range(pair)}
    normed_grad = after(normed_grad, *middle.values())
    passed = {e: swap(middle[e], "heads", 2 - e % 2) for e in middle}
    weighted_sum = jnp.sum(own_gate_weights * dgw, axis=0, keepdims=True)
    logit_grads = (own_gate_weights * (dgw - weighted_sum)).astype(bf16)
    upstream = cotangent.astype(f32)
    normed_grad = normed_grad + jnp.einsum(
        "er,de->rd", logit_grads, router, preferred_element_type=f32
    )
    router_grad = jnp.einsum("er,rd->ed", logit_grads, normed_two, preferred_element_type=f32)
    hatted_two = residual * scale_two
    ffn_gain_grad = jnp.sum(normed_grad * hatted_two, axis=0)
    scaled_two = normed_grad * ffn_gain
    residual_grad = upstream + scale_two * (
        scaled_two - hatted_two * jnp.mean(scaled_two * hatted_two, axis=-1, keepdims=True)
    )
    attn_grad = residual_grad.astype(bf16)
    out_bounds = [0, group_width, 2 * group_width, 3 * group_width]
    out_full = jnp.concatenate(out_pieces, axis=0)
    attended_rel = jnp.einsum(
        "ld,hd->lh", attn_grad, out_full, preferred_element_type=f32
    ).astype(bf16)
    attended_pieces = []
    for key in range(head_groups):
        piece = attended_rel[:, out_bounds[key] : out_bounds[key] + group_width]
        attended_pieces.append(swap(piece, "heads", key) if key else piece)
    attended_grad = place_small(attended_pieces, head)

    mixed_even = after(mixed_even, attended_rel)
    mixture, marks = scatter_rows(mixed_odd, mixed_even, False)
    out_w_grad = jnp.einsum("rh,rd->hd", attended_rows, attn_grad, preferred_element_type=f32)
    out_rows = group_width // token_groups
    out_w_grad = (
        out_w_grad.astype(bf16)
        .reshape(head_groups, token_groups, out_rows, model_width)
        .swapaxes(0, 1)
        .reshape(token_groups * head_groups * out_rows, model_width)
    )
    attended_grad = after(attended_grad, out_w_grad, *marks[:-1], *passed.values())
    arrived.update({(e, 1): send(e, 1, attended_grad) for e in range(pair, experts_here)})
    out_w_grad = lax.psum_scatter(out_w_grad, "tokens", scatter_dimension=0, tiled=True)
    packed_grad = attention_backward(
        turned, attended_grad, logs.T, start_row, cosine_table, sine_table
    )
    packed_grad = after(packed_grad, marks[-1])
    out_w_grad = after(out_w_grad, packed_grad).reshape(head_groups, out_rows, model_width)
    out_w_grad = out_w_grad[0].astype(f32) + sum(
        swap(out_w_grad[key], "heads", key).astype(f32) for key in range(1, head_groups)
    )
    middle.update({e: passed_on(e, packed_grad) for e in range(pair, experts_here)})
    grad_pieces = exchange_rows(packed_grad, head)
    output = (after(residual, packed_grad) + mixture).astype(bf16)
    packed_w_grad = jnp.einsum("ld,lh->dh", normed_full, packed_grad, preferred_element_type=f32)
    attn_gain_grad = jnp.sum(packed_w_grad * weights_packed.astype(f32), axis=1) / attn_gain
    small = jnp.concatenate(
        [
            router_grad,
            ffn_gain_grad[None],
            attn_gain_grad[None],
            jnp.zeros((6, model_width), f32),
        ],
        axis=0,
    )
    small = sum_axis(small, "heads")
    grad_pieces[-1] = after(grad_pieces[-1], small)
    small = sum_axis(small, "tokens")
    router_grad = small[:EXPERTS].T
    ffn_gain_grad, attn_gain_grad = small[EXPERTS], small[EXPERTS + 1]
    packed_w_grad = scatter_tokens(
        packed_w_grad.astype(bf16).reshape(
            token_groups, model_width // token_groups, packed_grad.shape[1]
        )
    )
    grad_rows = jnp.concatenate(grad_pieces, axis=1)
    later = range(pair, experts_here)
    grad_rows = after(grad_rows, out_w_grad, *[middle[e] for e in later])
    for e in later:
        arrived[e, 0] = send(e, 0, grad_rows)
        passed[e] = swap(after(middle[e], grad_rows), "heads", 2 - e % 2)
    normed_one_grad = jnp.einsum("lh,dh->ld", grad_rows, weights_all, preferred_element_type=f32)
    hatted_one = inputs * scale_one
    scaled_one = normed_one_grad * attn_gain
    input_grad = residual_grad + scale_one * (
        scaled_one - hatted_one * jnp.mean(scaled_one * hatted_one, axis=-1, keepdims=True)
    )
    wide, narrow = model_width // head_groups, hidden // head_groups
    block = 3 * wide
    gate_w_grad, up_w_grad, down_w_grad = pl.pallas_call(
        finish_kernel,
        in_specs=[pl.BlockSpec(memory_space=pl.ANY)] * (3 * experts_here),
        out_specs=[pl.BlockSpec(memory_space=pl.ANY)] * 3,
        out_shape=[
            jax.ShapeDtypeStruct((experts_here, wide, hidden), f32),
            jax.ShapeDtypeStruct((experts_here, wide, hidden), f32),
            jax.ShapeDtypeStruct((experts_here, narrow, model_width), f32),
        ],
        scratch_shapes=[
            pltpu.VMEM((3 * experts_here, block, hidden), bf16),
            pltpu.VMEM((experts_here, 2, wide, hidden), f32),
            pltpu.VMEM((experts_here, narrow, model_width), f32),
            pltpu.SemaphoreType.DMA((3 * experts_here,)),
            pltpu.SemaphoreType.DMA((3 * experts_here,)),
        ],
        compiler_params=pltpu.CompilerParams(vmem_limit_bytes=ATTENTION_LIMIT),
        cost_estimate=small_cost(),
        name="finish",
    )(
        *[after(weight_sums[4 * e + 3], input_grad) for e in range(experts_here)],
        *[arrived[e, 0] for e in range(experts_here)],
        *[passed[e] for e in range(experts_here)],
    )
    return (
        output,
        input_grad,
        attn_gain_grad,
        packed_w_grad[:, :key_start],
        packed_w_grad[:, key_start:value_start],
        packed_w_grad[:, value_start:],
        out_w_grad,
        ffn_gain_grad,
        router_grad,
        gate_w_grad,
        up_w_grad,
        down_w_grad,
    )


def solution(mesh):
    placed = (
        P(("tokens", "heads"), None),
        P("tokens", None),
        P(("tokens", "heads"), None),
        P(),
        P(None, "heads"),
        P(None, "heads"),
        P(None, "heads"),
        P("heads", None),
        P(),
        P(),
        P("tokens", None, None),
        P("tokens", None, None),
        P("tokens", None, None),
        P(("tokens", "heads"), None),
    )
    return jax.shard_map(
        body,
        mesh=mesh,
        in_specs=placed,
        out_specs=(
            P(("tokens", "heads"), None),
            P(("tokens", "heads"), None),
            P(),
            P("tokens", "heads"),
            P("tokens", "heads"),
            P("tokens", "heads"),
            P(("heads", "tokens"), None),
            P(),
            P(),
            P("tokens", "heads", None),
            P("tokens", "heads", None),
            P("tokens", "heads", None),
        ),
        check_vma=False,
    )
```

```python
import jax
import jax.numpy as jnp
from jax import lax
from jax.experimental import pallas as pl
from jax.experimental.pallas import tpu as pltpu
from jax.sharding import PartitionSpec as P

HEAD_DIM = 64
EXPERTS = 32
TOP = 8
CAP = 96


epsilon = 1e-06
theta_base = 10000.0
masked_value = -1e30


def doc_positions(segments):
    axis_last = segments.ndim - 1
    place_ids = lax.broadcasted_iota(jnp.int32, segments.shape, axis_last)
    previous = jnp.concatenate([segments[..., :1] - 1, segments[..., :-1]], axis=axis_last)
    starts = jnp.where(segments != previous, place_ids, 0)
    return place_ids - lax.cummax(starts, axis=axis_last)


def rotary_tables(positions, half_size):
    frequency = theta_base ** (
        -(jnp.arange(half_size, dtype=jnp.float32) * 2.0) / (2.0 * half_size)
    )
    angles = positions.astype(jnp.float32)[..., None] * frequency
    return (jnp.cos(angles), jnp.sin(angles))


def rotate(field, cosine_table, sine_table):
    half_size = field.shape[-1] // 2
    leading = field[..., :half_size]
    trailing = field[..., half_size:]
    cos_part = cosine_table[..., None, :]
    sin_part = sine_table[..., None, :]
    return jnp.concatenate(
        [leading * cos_part - trailing * sin_part, trailing * cos_part + leading * sin_part],
        axis=-1,
    )


f32 = jnp.float32
bf16 = jnp.bfloat16
i32 = jnp.int32
VMEM_LIMIT = 60 * 1024 * 1024
ATTENTION_LIMIT = 24 * 1024 * 1024
CHUNK = 4


def wide_tables(positions):
    half_size = HEAD_DIM // 2
    lanes = jnp.arange(128, dtype=i32) % half_size
    frequency = theta_base ** (-(lanes.astype(f32) * 2.0) / (2.0 * half_size))
    angles = positions.astype(f32) * frequency
    return jnp.cos(angles), jnp.sin(angles)


def swap(field, axis, bit):
    count = lax.axis_size(axis)
    return lax.ppermute(field, axis, [(i, i ^ bit) for i in range(count)])


def gather_tokens(field, other):
    count = lax.axis_size("tokens")
    held = {0: field}
    early = swap(field, "tokens", 2) if count > 2 else field
    bit = count // 2
    while bit > 1:
        for key in list(held):
            source = after(held[key], other) if key else held[key]
            held[key | bit] = early if bit == 2 and not key else swap(source, "tokens", bit)
        bit //= 2
    held.update({key | 1: swap(held[key], "tokens", 1) for key in list(held)})
    return [held[key] for key in range(count)], early


def add_low(left, right):
    return (left.astype(f32) + right.astype(f32)).astype(bf16)


def total(terms):
    result = terms[0].astype(f32)
    for other in terms[1:]:
        result = result + other.astype(f32)
    return result


def scatter_step(terms, bit, one_by_one, *anchors):
    sent, last = [], anchors
    for key in sorted((k for k in terms if k & bit), reverse=True):
        low = total(terms.pop(key)).astype(bf16)
        sent.append(low)
        arrived = swap(after(low, *last) if last else low, "tokens", 2 * bit)
        if one_by_one:
            last = (arrived,)
        terms[key ^ bit].append(arrived)
    return sent


def scatter_rest(terms, *anchors):
    bit, sent = 2, []
    while len(terms) > 1:
        sent += scatter_step(terms, bit, True, *anchors)
        bit *= 2
    return total(terms[0]), sent


def scatter_chips(parts, one_by_one=True):
    terms = {key: list(some) for key, some in enumerate(parts)}
    sent = scatter_step(terms, 1, one_by_one)
    result, more = scatter_rest(terms)
    return result, sent + more


def after(field, *others):
    return lax.optimization_barrier((field, *others))[0]


def scatter_tokens(field):
    count, rows, columns = field.shape
    place = lax.axis_index("tokens")
    chip, core = place // 2, place % 2
    paired = field.reshape(count // 2, 2, rows, columns)
    sent = lax.dynamic_index_in_dim(paired, 1 - core, axis=1, keepdims=False)
    kept = lax.dynamic_index_in_dim(paired, core, axis=1, keepdims=False)
    both = add_low(kept, swap(sent, "tokens", 1))
    parts = [
        [lax.dynamic_index_in_dim(both, chip ^ key, axis=0, keepdims=False)]
        for key in range(count // 2)
    ]
    return scatter_chips(parts)[0]


def sum_axis(field, axis):
    bit = 1
    while bit < lax.axis_size(axis):
        field = field + swap(field, axis, bit)
        bit *= 2
    return field


def xor_order(field, place):
    count = field.shape[0]
    rest = field.shape[1:]
    bit = 1
    while bit < count:
        split = field.reshape((count // (2 * bit), 2, bit) + rest)
        flipped = jnp.concatenate([split[:, 1:], split[:, :1]], axis=1)
        field = jnp.where((place & bit) != 0, flipped, split).reshape((count,) + rest)
        bit *= 2
    return field


def nn(left, right):
    return lax.dot_general(left, right, (((1,), (0,)), ((), ())), preferred_element_type=f32)


def nt(left, right):
    return lax.dot_general(left, right, (((1,), (1,)), ((), ())), preferred_element_type=f32)


def tn(left, right):
    return lax.dot_general(left, right, (((0,), (0,)), ((), ())), preferred_element_type=f32)


def select_columns(slots, local):
    rows = slots.shape[1]
    slots = jnp.transpose(slots)
    lanes = lax.broadcasted_iota(i32, (rows, local * CAP), 1)
    same = None
    for expert in range(local):
        column = slots[:, expert : expert + 1]
        term = lanes == jnp.where(column < 0, -1, column + expert * CAP)
        same = term if same is None else same | term
    return jnp.where(same, 1.0, 0.0).astype(bf16)


def turn(field, cosine, sine, sign):
    lanes = lax.broadcasted_iota(i32, field.shape, 1)
    partner = jnp.where(
        lanes % HEAD_DIM < HEAD_DIM // 2,
        -pltpu.roll(field, 128 - HEAD_DIM // 2, 1),
        pltpu.roll(field, HEAD_DIM // 2, 1),
    )
    return field * cosine + sign * (partner * sine)


def keep_half(field, side):
    lanes = lax.broadcasted_iota(i32, field.shape, 1)
    return jnp.where((lanes >= HEAD_DIM) == (side == 1), field, jnp.zeros_like(field))


def join_halves(low, high):
    lanes = lax.broadcasted_iota(i32, low.shape, 1)
    return jnp.where(lanes < HEAD_DIM, low, high)


def attention_forward_kernel(
    raw_ref, cosine_ref, sine_ref, start_ref, out_ref, turned_ref, log_ref, swapped_ref
):
    length = raw_ref.shape[0]
    rows = 256
    scaling = HEAD_DIM ** (-0.5)
    for first in range(0, length, rows):
        some = pl.ds(first, rows)
        cosine, sine = cosine_ref[some, :], sine_ref[some, :]
        for part in range(2):
            lanes = pl.ds(128 * part, 128)
            query = turn(raw_ref[some, lanes], cosine, sine, 1.0).astype(bf16)
            turned_ref[some, lanes] = (query.astype(f32) * scaling).astype(bf16)
        key = turn(raw_ref[some, pl.ds(256, 128)], cosine, sine, 1.0)
        value = raw_ref[some, pl.ds(384, 128)]
        turned_ref[some, pl.ds(256, 128)] = key.astype(bf16)
        turned_ref[some, pl.ds(384, 128)] = value.astype(bf16)
        swapped_ref[some, pl.ds(0, 128)] = pltpu.roll(key, HEAD_DIM, 1).astype(bf16)
        swapped_ref[some, pl.ds(128, 128)] = pltpu.roll(value, HEAD_DIM, 1).astype(bf16)
    for first in range(0, length, rows):
        some = pl.ds(first, rows)
        low = max(0, first - 512)
        span = pl.ds(low, first + rows - low)
        columns = first + rows - low
        keys = lax.broadcasted_iota(i32, (rows, columns), 1) + low
        queries = lax.broadcasted_iota(i32, (rows, columns), 0) + first
        allowed = (keys <= queries) & (keys >= start_ref[some, :])
        for pair in range(2):
            query = turned_ref[some, pl.ds(128 * pair, 128)]
            halves = []
            for side in range(2):
                if pair == side:
                    key, value = turned_ref[span, pl.ds(256, 128)], turned_ref[span, pl.ds(384, 128)]
                else:
                    key, value = swapped_ref[span, pl.ds(0, 128)], swapped_ref[span, pl.ds(128, 128)]
                scores = jnp.where(allowed, nt(keep_half(query, side), key), masked_value)
                top = jnp.max(scores, axis=1, keepdims=True)
                exponent = jnp.exp(scores - top)
                total = jnp.sum(exponent, axis=1, keepdims=True)
                weights = (exponent * (1.0 / total)).astype(bf16)
                halves.append(nn(weights, value))
                number = 2 * pair + side
                log_ref[some, pl.ds(number, 1)] = top + jnp.log(total)
            out_ref[some, pl.ds(128 * pair, 128)] = join_halves(*halves).astype(bf16)


def attention_backward_kernel(
    turned_ref, grad_ref, log_ref, start_ref, cosine_ref, sine_ref, out_ref,
    swapped_ref, key_acc, value_acc,
):
    length = turned_ref.shape[0]
    rows = 256
    scaling = HEAD_DIM ** (-0.5)
    key_acc[...] = jnp.zeros_like(key_acc)
    value_acc[...] = jnp.zeros_like(value_acc)
    for first in range(0, length, rows):
        some = pl.ds(first, rows)
        for part in range(2):
            field = turned_ref[some, pl.ds(256 + 128 * part, 128)].astype(f32)
            swapped_ref[some, pl.ds(128 * part, 128)] = pltpu.roll(field, HEAD_DIM, 1).astype(bf16)
    for first in range(0, length, rows):
        some = pl.ds(first, rows)
        low = max(0, first - 512)
        count = first + rows - low
        span = pl.ds(low, count)
        keys = lax.broadcasted_iota(i32, (count, rows), 0) + low
        queries = lax.broadcasted_iota(i32, (count, rows), 1) + first
        allowed = (keys <= queries) & (keys >= start_ref[:, some])
        for pair in range(2):
            query = turned_ref[some, pl.ds(128 * pair, 128)]
            grad = grad_ref[some, pl.ds(128 * pair, 128)]
            halves = []
            for side in range(2):
                if pair == side:
                    key, value = turned_ref[span, pl.ds(256, 128)], turned_ref[span, pl.ds(384, 128)]
                else:
                    key, value = swapped_ref[span, pl.ds(0, 128)], swapped_ref[span, pl.ds(128, 128)]
                mine, mine_grad = keep_half(query, side), keep_half(grad, side)
                scores = jnp.where(allowed, nt(key, mine), masked_value)
                number = 2 * pair + side
                probs = jnp.exp(scores - log_ref[pl.ds(number, 1), some])
                prob_grads = nt(value, mine_grad)
                offset = jnp.sum(probs * prob_grads, axis=0, keepdims=True)
                score_grads = (probs * (prob_grads - offset)).astype(bf16)
                halves.append(tn(score_grads, key) * scaling)
                kind = 0 if pair == side else 1
                key_acc[kind, span, :] += nn(score_grads, mine)
                value_acc[kind, span, :] += nn(probs.astype(bf16), mine_grad)
            cosine, sine = cosine_ref[some, :], sine_ref[some, :]
            out_ref[some, pl.ds(128 * pair, 128)] = turn(
                join_halves(*halves), cosine, sine, -1.0
            ).astype(bf16)
    for first in range(0, length, rows):
        some = pl.ds(first, rows)
        cosine, sine = cosine_ref[some, :], sine_ref[some, :]
        key = key_acc[0, some, :] + pltpu.roll(key_acc[1, some, :], HEAD_DIM, 1)
        value = value_acc[0, some, :] + pltpu.roll(value_acc[1, some, :], HEAD_DIM, 1)
        out_ref[some, pl.ds(256, 128)] = turn(key, cosine, sine, -1.0).astype(bf16)
        out_ref[some, pl.ds(384, 128)] = value.astype(bf16)


def small_cost():
    return pl.CostEstimate(flops=1000000, bytes_accessed=100000, transcendentals=0)


def attention_forward(raw, cosine, sine, starts):
    length = raw.shape[0]
    return pl.pallas_call(
        attention_forward_kernel,
        out_shape=[
            jax.ShapeDtypeStruct((length, 256), bf16),
            jax.ShapeDtypeStruct((length, 512), bf16),
            jax.ShapeDtypeStruct((length, 8), f32),
        ],
        scratch_shapes=[pltpu.VMEM((length, 256), bf16)],
        compiler_params=pltpu.CompilerParams(vmem_limit_bytes=ATTENTION_LIMIT),
        cost_estimate=small_cost(),
        name="attention_forward",
    )(raw, cosine, sine, starts)


def attention_backward(turned, grad, logs, starts, cosine, sine):
    length = turned.shape[0]
    return pl.pallas_call(
        attention_backward_kernel,
        out_shape=jax.ShapeDtypeStruct((length, 512), bf16),
        scratch_shapes=[
            pltpu.VMEM((length, 256), bf16),
            pltpu.VMEM((2, length, 128), f32),
            pltpu.VMEM((2, length, 128), f32),
        ],
        compiler_params=pltpu.CompilerParams(vmem_limit_bytes=ATTENTION_LIMIT),
        cost_estimate=small_cost(),
        name="attention_backward",
    )(turned, grad, logs, starts, cosine, sine)


def expert_kernel(sources, first_source, count, heads, chunk, absolute, *refs):
    refs = list(refs)
    where_ref = refs.pop(0)
    hn_refs = [refs.pop(0) for _ in range(sources)]
    g_hbm, slot_ref, gw_ref, gate_ref, up_ref, down_ref = refs[:6]
    even_ref, odd_ref, mixed_even_ref, mixed_odd_ref, dgw_ref = refs[6:11]
    outs = [refs[11 + 4 * k : 15 + 4 * k] for k in range(count)]
    h_ref, g_ref, x_ref, xr_ref, gx_ref, act_ref, dye_ref, dgu_ref, gws_ref, dcol_ref = refs[
        11 + 4 * count : 21 + 4 * count
    ]
    dxe_ref, ye_ref, sum_ref, h_sem, g_sem, out_sem = refs[21 + 4 * count :]
    step = pl.program_id(0)
    expert = jnp.minimum(step, count - 1)
    place, head = where_ref[0], where_ref[1]
    rows = h_ref.shape[1]
    width = h_ref.shape[2]
    hidden = act_ref.shape[1]
    wide, narrow = width // heads, hidden // heads
    group = chunk // CAP

    def origin(s):
        return place ^ (first_source + s)

    def copy_h(s):
        return pltpu.make_async_copy(hn_refs[s], h_ref.at[s], h_sem.at[s])

    def copy_g(s):
        return pltpu.make_async_copy(g_hbm.at[origin(s)], g_ref.at[s], g_sem.at[s])

    def copy_out(number, side):
        slot = number % 2
        return pltpu.make_async_copy(
            sum_ref.at[slot, side],
            outs[number][side],
            out_sem.at[4 * slot + side],
        )

    @pl.when(step == 0)
    def _():
        for s in range(sources):
            copy_h(s).start()
        for s in range(sources):
            copy_g(s).start()
        for s in range(sources):
            copy_h(s).wait()

    def chosen(s):
        slots = slot_ref[origin(s), pl.ds(expert, 1), :]
        return lax.broadcasted_iota(i32, (CAP, rows), 0) == slots

    def pick(s):
        same = chosen(s)
        select = jnp.where(same, 1.0, 0.0).astype(bf16)
        mine = pl.ds(s * CAP, CAP)
        x = nn(select, h_ref[s]).astype(bf16)
        x_ref[mine, :] = x
        for owner in range(heads):
            target = pl.multiple_of((owner ^ head) * wide, wide)
            xr_ref[mine, pl.ds(target, wide)] = x[:, owner * wide : (owner + 1) * wide]
        row = gw_ref[origin(s), pl.ds(expert, 1), :]
        gws_ref[mine, :] = jnp.sum(jnp.where(same, row, 0.0), axis=1, keepdims=True)

    def pick_grad(s):
        select = jnp.where(chosen(s), 1.0, 0.0).astype(bf16)
        gx_ref[pl.ds(s * CAP, CAP), :] = nn(select, g_ref[s]).astype(bf16)

    def work(number):
        part = pl.ds(pl.multiple_of(number * chunk, chunk), chunk)
        some = pl.ds(number * group, group)
        x = x_ref[part, :]
        gate = nn(x, gate_ref[0])
        up = nn(x, up_ref[0])
        sigma = 1.0 / (1.0 + jnp.exp(-gate))
        silu = gate * sigma
        act = (silu * up).astype(bf16)
        for owner in range(heads):
            target = pl.multiple_of((owner ^ head) * narrow, narrow)
            act_ref[part, pl.ds(target, narrow)] = act[:, owner * narrow : (owner + 1) * narrow]
        gx = gx_ref[part, :].astype(f32)
        weights = gws_ref[part, :]
        dye = (gx * weights).astype(bf16)
        dye_ref[part, :] = dye
        ye = nn(act, down_ref[0]).astype(bf16).astype(f32)
        dcol_ref[part, :] = jnp.sum(gx * ye, axis=1, keepdims=True)
        ye_ref[some, expert] = (ye * weights).astype(bf16).reshape(group, CAP, width)
        dact = nt(dye, down_ref[0])
        dgate = (dact * up * sigma * (1.0 + gate * (1.0 - sigma))).astype(bf16)
        dup = (dact * silu).astype(bf16)
        dgu_ref[part, pl.ds(0, hidden)] = dgate
        dgu_ref[part, pl.ds(hidden, hidden)] = dup
        dxe = (nt(dgate, gate_ref[0]) + nt(dup, up_ref[0])).astype(bf16)
        dxe_ref[some, expert] = dxe.reshape(group, CAP, width)

    @pl.when(step < count)
    def _():
        for s in range(sources):
            pick(s)

        @pl.when(step == 0)
        def _():
            for s in range(sources):
                copy_g(s).wait()

        for s in range(sources):
            pick_grad(s)
        pl.loop(0, sources // group)(work)
        for s in range(sources):
            column = dcol_ref[pl.ds(s * CAP, CAP), :]
            index = origin(s) if absolute else s
            dgw_ref[index, pl.ds(expert, 1), :] = jnp.sum(
                jnp.where(chosen(s), column, 0.0), axis=0, keepdims=True
            )

        down = tn(act_ref[...], dye_ref[...]).astype(bf16)
        for number in range(2, count):

            @pl.when(step == number)
            def _():
                for side in range(4):
                    copy_out(number - 2, side).wait()

        slot = lax.rem(step, 2)
        for relative, position in ((0, 3), (1, 2 * slot), (2, 2 - 2 * slot), (3, 1)):
            both = tn(xr_ref[:, pl.ds(relative * wide, wide)], dgu_ref[...]).astype(bf16)
            target_ref = sum_ref.at[slot, position]
            target_ref[pl.ds(0, wide), :] = both[:, :hidden]
            target_ref[pl.ds(wide, wide), :] = both[:, hidden:]
            low = down[relative * narrow : (relative + 1) * narrow]
            target_ref[pl.ds(2 * wide, narrow), :] = low[:, :hidden]
            target_ref[pl.ds(2 * wide + narrow, narrow), :] = low[:, hidden:]
        for number in range(count):

            @pl.when(step == number)
            def _():
                for side in range(4):
                    copy_out(number, side).start()

    @pl.when(step >= count)
    def _():
        pair = step - count
        for side, targets in enumerate(((even_ref, mixed_even_ref), (odd_ref, mixed_odd_ref))):
            select = select_columns(slot_ref[place ^ (first_source + 2 * pair + side)], count)
            for source_ref, out_ref in zip((dxe_ref, ye_ref), targets):
                values = source_ref[2 * pair + side].reshape(count * CAP, width)
                out_ref[0] = nn(select, values).astype(bf16)

        @pl.when(pair == sources // 2 - 1)
        def _():
            for number in range(max(0, count - 2), count):
                for side in range(4):
                    copy_out(number, side).wait()


def run_experts(
    where, hn_list, upstream_all, first_source, slots, gate_weights, w_gate, w_up, w_down, heads,
):
    sources = len(hn_list)
    rows, width = hn_list[0].shape
    count, _, hidden = w_gate.shape
    slots_all = sources * CAP
    block = 3 * (width // heads)
    whole = pl.BlockSpec(memory_space=pltpu.VMEM)
    hbm = pl.BlockSpec(memory_space=pl.ANY)
    chunk = CHUNK * CAP
    absolute = sources == slots.shape[0]

    def of_expert(shape):
        return pl.BlockSpec(shape, lambda i: (jnp.minimum(i, count - 1), 0, 0))

    def of_pair(i):
        return (jnp.maximum(i - count, 0), 0, 0)

    half = jax.ShapeDtypeStruct((sources // 2, rows, width), bf16)
    out_shape = [
        half,
        half,
        half,
        half,
        jax.ShapeDtypeStruct((sources, count, rows), f32),
    ]
    out_specs = [
        pl.BlockSpec((1, rows, width), of_pair),
        pl.BlockSpec((1, rows, width), of_pair),
        pl.BlockSpec((1, rows, width), of_pair),
        pl.BlockSpec((1, rows, width), of_pair),
        whole,
    ]
    one = jax.ShapeDtypeStruct((block, hidden), bf16)
    out_shape += [one] * (4 * count)
    out_specs += [hbm] * (4 * count)

    def kernel(*refs):
        expert_kernel(sources, first_source, count, heads, chunk, absolute, *refs)

    return pl.pallas_call(
        kernel,
        grid=(count + sources // 2,),
        in_specs=[pl.BlockSpec(memory_space=pltpu.SMEM)]
        + [hbm] * sources
        + [hbm, whole, whole]
        + [
            of_expert((1, width, hidden)),
            of_expert((1, width, hidden)),
            of_expert((1, hidden, width)),
        ],
        out_specs=out_specs,
        out_shape=out_shape,
        scratch_shapes=[
            pltpu.VMEM((sources, rows, width), bf16),
            pltpu.VMEM((sources, rows, width), bf16),
            pltpu.VMEM((slots_all, width), bf16),
            pltpu.VMEM((slots_all, width), bf16),
            pltpu.VMEM((slots_all, width), bf16),
            pltpu.VMEM((slots_all, hidden), bf16),
            pltpu.VMEM((slots_all, width), bf16),
            pltpu.VMEM((slots_all, 2 * hidden), bf16),
            pltpu.VMEM((slots_all, 1), f32),
            pltpu.VMEM((slots_all, 1), f32),
            pltpu.VMEM((sources, count, CAP, width), bf16),
            pltpu.VMEM((sources, count, CAP, width), bf16),
            pltpu.VMEM((2, 4, block, hidden), bf16),
            pltpu.SemaphoreType.DMA((sources,)),
            pltpu.SemaphoreType.DMA((sources,)),
            pltpu.SemaphoreType.DMA((8,)),
        ],
        compiler_params=pltpu.CompilerParams(vmem_limit_bytes=VMEM_LIMIT),
        cost_estimate=small_cost(),
        name="experts",
    )(where, *hn_list, upstream_all, slots, gate_weights, w_gate, w_up, w_down)


def finish_kernel(*refs):
    in_ref, pair_ref, down_ref, in_sem, out_sem = refs[-5:]
    outs = refs[-8:-5]
    fields = refs[:-8]
    count = len(fields) // 3
    wide, hidden = pair_ref.shape[2:]
    narrow = down_ref.shape[1]

    def arrive(number):
        return pltpu.make_async_copy(fields[number], in_ref.at[number], in_sem.at[number])

    def leave(e, kind):
        source = pair_ref.at[e, kind] if kind < 2 else down_ref.at[e]
        return pltpu.make_async_copy(source, outs[kind].at[e], out_sem.at[3 * e + kind])

    for e in range(count):
        for kind in range(3):
            arrive(kind * count + e).start()
    for e in range(count):
        for kind in range(3):
            arrive(kind * count + e).wait()

        def total(first, rows):
            part = pl.ds(first, rows)
            return (
                in_ref[e, part, :].astype(f32)
                + in_ref[count + e, part, :].astype(f32)
                + in_ref[2 * count + e, part, :].astype(f32)
            )

        for kind in range(2):
            pair_ref[e, kind] = total(kind * wide, wide)
        down_ref[e, :, pl.ds(0, hidden)] = total(2 * wide, narrow)
        down_ref[e, :, pl.ds(hidden, hidden)] = total(2 * wide + narrow, narrow)
        for kind in range(3):
            leave(e, kind).start()
    for e in range(count):
        for kind in range(3):
            leave(e, kind).wait()


def scatter_rows(odd, even):
    arrived = swap(odd, "tokens", 1)
    return scatter_chips([[even[k], arrived[k]] for k in range(even.shape[0])], False)


def place_rows(pieces, place):
    rows = pieces[0].shape[0]
    result = jnp.concatenate([pieces[0]] * (len(pieces) - 1), axis=0)
    for key, piece in list(enumerate(pieces))[1:]:
        start = (place ^ key) * rows if key < 4 else (place ^ 3) * rows + rows // 2
        result = lax.dynamic_update_slice_in_dim(result, piece, start, axis=0)
    return result


def place_small(pieces, place):
    count = len(pieces)
    blocks = []
    for block in range(count):
        chosen = pieces[0]
        for key in range(1, count):
            chosen = jnp.where((place ^ key) == block, pieces[key], chosen)
        blocks.append(chosen)
    return jnp.concatenate(blocks, axis=0)


def exchange_rows(field, place):
    count = lax.axis_size("heads")
    rows = field.shape[0] // count
    pieces = []
    for key in range(count):
        piece = lax.dynamic_slice_in_dim(field, (place ^ key) * rows, rows, axis=0)
        pieces.append(swap(piece, "heads", key) if key else piece)
    return pieces


def gather_heads(field):
    half = field.shape[0] // 2
    one, two = swap(field, "heads", 1), swap(field, "heads", 2)
    return [field, one, two, swap(two[:half], "heads", 1), swap(one[half:], "heads", 2)]


def body(
    tokens,
    segment_ids,
    routes,
    attn_gain,
    w_query,
    w_key,
    w_value,
    w_out,
    ffn_gain,
    router,
    w_gate,
    w_up,
    w_down,
    cotangent,
):
    rows_here = tokens.shape[0]
    model_width = tokens.shape[1]
    local_heads = w_query.shape[1] // HEAD_DIM
    local_kv = w_key.shape[1] // HEAD_DIM
    group_size = local_heads // local_kv
    seq_len = segment_ids.shape[1]
    experts_here = w_gate.shape[0]
    hidden = w_gate.shape[2]
    token_groups = lax.axis_size("tokens")
    head_groups = lax.axis_size("heads")
    place = lax.axis_index("tokens")
    head = lax.axis_index("heads")
    scaling = HEAD_DIM ** (-0.5)
    inputs = tokens.astype(f32)
    scale_one = lax.rsqrt(jnp.mean(inputs * inputs, axis=-1, keepdims=True) + epsilon)
    normed_one = (inputs * scale_one * attn_gain).astype(bf16)
    normed_pieces = gather_heads(normed_one)
    weights_packed = jnp.concatenate([w_query, w_key, w_value], axis=1)

    expert_ids = jnp.arange(EXPERTS, dtype=i32)
    own_mask = jnp.sum(
        (routes.T[:, None, :] == expert_ids[None, :, None]).astype(f32), axis=0
    )

    def to_experts(field):
        return lax.all_to_all(
            field, "tokens", split_axis=0, concat_axis=0, tiled=True
        ).reshape(token_groups, experts_here, rows_here)

    masks = to_experts(own_mask)
    normed_full = place_rows([after(normed_one, masks), *normed_pieces[1:]], head)
    upstream_all = lax.all_gather(cotangent, "tokens", axis=0, tiled=False)
    before = jnp.triu(jnp.ones((rows_here, rows_here), bf16), 1)
    slots = jnp.einsum("set,tu->seu", masks.astype(bf16), before, preferred_element_type=f32)
    slots = jnp.where(masks > 0, slots, -1.0).astype(i32)
    slots = jnp.pad(slots, ((0, 0), (0, (-experts_here) % 8), (0, 0)), constant_values=-1)
    positions = doc_positions(segment_ids)[0]
    starts = jnp.arange(seq_len, dtype=i32) - positions
    wide_positions = jnp.broadcast_to(positions[:, None], (seq_len, 128))
    cosine_table, sine_table = wide_tables(wide_positions)
    start_column, start_row = starts[:, None], starts[None]
    normed_full, slots, cosine_table, sine_table, weights_packed, start_column, start_row = (
        lax.optimization_barrier(
            (
                normed_full, slots, cosine_table, sine_table, weights_packed, start_column,
                start_row,
            )
        )
    )
    core = place % 2
    half_rows = w_out.shape[0] // 2
    out_half = lax.dynamic_slice_in_dim(w_out, core * half_rows, half_rows, axis=0)
    out_half = after(after(out_half, slots, cosine_table, sine_table), *normed_pieces[3:])
    out_halves = [swap(out_half, "heads", key) for key in range(1, head_groups)]

    group_width = local_heads * HEAD_DIM
    key_start, value_start = group_width, group_width + local_kv * HEAD_DIM
    raw = jnp.dot(normed_full, weights_packed, preferred_element_type=f32)
    attended, turned, logs = attention_forward(raw, cosine_table, sine_table, start_column)
    out_halves = lax.optimization_barrier((*out_halves, attended))[:-1]
    out_pieces = [w_out]
    for mine in out_halves:
        other = swap(mine, "tokens", 1)
        out_pieces.append(jnp.where(core == 0, mine, other))
        out_pieces.append(jnp.where(core == 0, other, mine))
    w_out_all = jnp.concatenate(out_pieces, axis=0)
    attended_rows = jnp.concatenate(exchange_rows(attended, head), axis=1)
    residual = inputs + jnp.dot(attended_rows, w_out_all, preferred_element_type=f32)
    scale_two = lax.rsqrt(jnp.mean(residual * residual, axis=-1, keepdims=True) + epsilon)
    normed_two = (residual * scale_two * ffn_gain).astype(bf16)
    logits = jnp.einsum("de,rd->er", router, normed_two, preferred_element_type=f32)
    top = jnp.max(jnp.where(own_mask > 0, logits, masked_value), axis=0, keepdims=True)
    exponent = jnp.where(own_mask > 0, jnp.exp(logits - top), 0.0)
    own_gate_weights = exponent / jnp.sum(exponent, axis=0, keepdims=True)
    gate_weights = to_experts(own_gate_weights)
    normed_list, early = gather_tokens(normed_two, gate_weights)
    weights_sent = after(weights_packed, early)
    weight_pieces = [weights_packed] + [
        swap(weights_sent, "heads", key) for key in range(1, head_groups)
    ]
    weights_all = jnp.concatenate(weight_pieces, axis=1)

    where = jnp.stack([place, head]).astype(i32)
    chunk_sources = min(8, token_groups)
    results = []
    for first in range(0, token_groups, chunk_sources):
        results.append(
            run_experts(
                where, normed_list[first : first + chunk_sources], upstream_all, first, slots,
                gate_weights, w_gate, w_up, w_down, head_groups,
            )
        )

    def joined(parts):
        return parts[0] if len(parts) == 1 else jnp.concatenate(parts, axis=0)

    grad_even, grad_odd, mixed_even, mixed_odd, dgw_all = (
        joined([r[k] for r in results]) for k in range(5)
    )
    weight_sums = results[0][5:]
    for other in results[1:]:
        weight_sums = [add_low(mine, more) for mine, more in zip(weight_sums, other[5:])]
    if len(results) > 1:
        dgw_all = xor_order(dgw_all, place)
    grad_odd = after(grad_odd, *weight_pieces[1:])
    normed_grad, marks = scatter_rows(grad_odd, grad_even)
    own_gate_weights = after(own_gate_weights, marks[0])
    dgw = lax.all_to_all(
        dgw_all, "tokens", split_axis=0, concat_axis=0, tiled=True
    ).reshape(EXPERTS, rows_here)
    def send(expert, number, *anchors):
        part = weight_sums[4 * expert + number]
        part = after(part, *anchors) if anchors else part
        return swap(part, "heads", 1 + expert % 2)

    pair = min(2, experts_here)
    arrived = {(e, number): send(e, number) for e in range(pair) for number in (1, 0)}

    def passed_on(expert, anchor):
        kept = after(weight_sums[4 * expert + 2], anchor)
        return add_low(kept, arrived[expert, 1])

    middle = {e: passed_on(e, marks[-1]) for e in range(pair)}
    normed_grad = after(normed_grad, *middle.values(), *[arrived[e, 0] for e in range(pair)])
    passed = {e: swap(middle[e], "heads", 2 - e % 2) for e in middle}
    weighted_sum = jnp.sum(own_gate_weights * dgw, axis=0, keepdims=True)
    logit_grads = (own_gate_weights * (dgw - weighted_sum)).astype(bf16)
    upstream = cotangent.astype(f32)
    normed_grad = normed_grad + jnp.einsum(
        "er,de->rd", logit_grads, router, preferred_element_type=f32
    )
    router_grad = jnp.einsum("er,rd->ed", logit_grads, normed_two, preferred_element_type=f32)
    hatted_two = residual * scale_two
    ffn_gain_grad = jnp.sum(normed_grad * hatted_two, axis=0)
    scaled_two = normed_grad * ffn_gain
    residual_grad = upstream + scale_two * (
        scaled_two - hatted_two * jnp.mean(scaled_two * hatted_two, axis=-1, keepdims=True)
    )
    attn_grad = residual_grad.astype(bf16)
    out_bounds = [0, group_width, 2 * group_width, 3 * group_width]
    attended_rel = jnp.einsum(
        "ld,hd->lh", attn_grad, w_out_all, preferred_element_type=f32
    ).astype(bf16)
    attended_pieces = []
    for key in range(head_groups):
        piece = attended_rel[:, out_bounds[key] : out_bounds[key] + group_width]
        attended_pieces.append(swap(piece, "heads", key) if key else piece)
    attended_grad = place_small(attended_pieces, head)

    mixed_even = after(mixed_even, attended_rel)
    mixed_arrived = swap(mixed_odd, "tokens", 1)
    mixed_terms = {k: [mixed_even[k], mixed_arrived[k]] for k in range(mixed_even.shape[0])}
    mixed_sent = scatter_step(mixed_terms, 1, False)

    out_w_grad = jnp.einsum("rh,rd->hd", attended_rows, attn_grad, preferred_element_type=f32)
    out_rows = group_width // token_groups
    out_w_grad = (
        out_w_grad.astype(bf16)
        .reshape(head_groups, token_groups, out_rows, model_width)
        .swapaxes(0, 1)
        .reshape(token_groups * head_groups * out_rows, model_width)
    )
    attended_grad = after(attended_grad, out_w_grad, *mixed_sent, *passed.values())
    arrived.update({(e, 1): send(e, 1, attended_grad) for e in range(pair, experts_here)})
    out_w_grad = lax.psum_scatter(out_w_grad, "tokens", scatter_dimension=0, tiled=True)
    packed_grad = attention_backward(
        turned, attended_grad, logs.T, start_row, cosine_table, sine_table
    )
    mixture, sent = scatter_rest(mixed_terms, attended_grad)
    packed_grad = after(packed_grad, *sent)
    middle.update({e: passed_on(e, packed_grad) for e in range(pair, experts_here)})
    grad_pieces = exchange_rows(packed_grad, head)
    packed_w_grad = jnp.einsum("ld,lh->dh", normed_full, packed_grad, preferred_element_type=f32)
    attn_gain_grad = jnp.sum(packed_w_grad * weights_packed.astype(f32), axis=1) / attn_gain
    small = jnp.concatenate(
        [
            router_grad,
            ffn_gain_grad[None],
            attn_gain_grad[None],
            jnp.zeros((6, model_width), f32),
        ],
        axis=0,
    )
    packed_w_grad = scatter_tokens(
        packed_w_grad.astype(bf16).reshape(
            token_groups, model_width // token_groups, packed_grad.shape[1]
        )
    )
    grad_rows = jnp.concatenate(grad_pieces, axis=1)
    later = range(pair, experts_here)
    passed.update(
        {e: swap(after(middle[e], grad_rows), "heads", 2 - e % 2) for e in later}
    )
    out_w_grad = after(out_w_grad, grad_rows).reshape(head_groups, out_rows, model_width)
    out_w_grad = out_w_grad[0].astype(f32) + sum(
        swap(out_w_grad[key], "heads", key).astype(f32) for key in range(1, head_groups)
    )
    arrived.update({(e, 0): send(e, 0, grad_rows) for e in later})
    grad_rows = after(grad_rows, *[middle[e] for e in later])
    normed_one_grad = jnp.einsum("lh,dh->ld", grad_rows, weights_all, preferred_element_type=f32)
    hatted_one = inputs * scale_one
    scaled_one = normed_one_grad * attn_gain
    input_grad = residual_grad + scale_one * (
        scaled_one - hatted_one * jnp.mean(scaled_one * hatted_one, axis=-1, keepdims=True)
    )
    output = (after(residual, input_grad) + mixture).astype(bf16)
    small = after(small, output, out_w_grad, *[passed[e] for e in later])
    small = sum_axis(small, "tokens")
    small = after(small, *[arrived[e, 0] for e in later])
    small = sum_axis(small, "heads")
    router_grad = small[:EXPERTS].T
    ffn_gain_grad, attn_gain_grad = small[EXPERTS], small[EXPERTS + 1]
    wide, narrow = model_width // head_groups, hidden // head_groups
    block = 3 * wide
    gate_w_grad, up_w_grad, down_w_grad = pl.pallas_call(
        finish_kernel,
        in_specs=[pl.BlockSpec(memory_space=pl.ANY)] * (3 * experts_here),
        out_specs=[pl.BlockSpec(memory_space=pl.ANY)] * 3,
        out_shape=[
            jax.ShapeDtypeStruct((experts_here, wide, hidden), f32),
            jax.ShapeDtypeStruct((experts_here, wide, hidden), f32),
            jax.ShapeDtypeStruct((experts_here, narrow, model_width), f32),
        ],
        scratch_shapes=[
            pltpu.VMEM((3 * experts_here, block, hidden), bf16),
            pltpu.VMEM((experts_here, 2, wide, hidden), f32),
            pltpu.VMEM((experts_here, narrow, model_width), f32),
            pltpu.SemaphoreType.DMA((3 * experts_here,)),
            pltpu.SemaphoreType.DMA((3 * experts_here,)),
        ],
        compiler_params=pltpu.CompilerParams(vmem_limit_bytes=ATTENTION_LIMIT),
        cost_estimate=small_cost(),
        name="finish",
    )(
        *[after(weight_sums[4 * e + 3], input_grad) for e in range(experts_here)],
        *[arrived[e, 0] for e in range(experts_here)],
        *[passed[e] for e in range(experts_here)],
    )
    return (
        output,
        input_grad,
        attn_gain_grad,
        packed_w_grad[:, :key_start],
        packed_w_grad[:, key_start:value_start],
        packed_w_grad[:, value_start:],
        out_w_grad,
        ffn_gain_grad,
        router_grad,
        gate_w_grad,
        up_w_grad,
        down_w_grad,
    )


def solution(mesh):
    placed = (
        P(("tokens", "heads"), None),
        P("tokens", None),
        P(("tokens", "heads"), None),
        P(),
        P(None, "heads"),
        P(None, "heads"),
        P(None, "heads"),
        P("heads", None),
        P(),
        P(),
        P("tokens", None, None),
        P("tokens", None, None),
        P("tokens", None, None),
        P(("tokens", "heads"), None),
    )
    return jax.shard_map(
        body,
        mesh=mesh,
        in_specs=placed,
        out_specs=(
            P(("tokens", "heads"), None),
            P(("tokens", "heads"), None),
            P(),
            P("tokens", "heads"),
            P("tokens", "heads"),
            P("tokens", "heads"),
            P(("heads", "tokens"), None),
            P(),
            P(),
            P("tokens", "heads", None),
            P("tokens", "heads", None),
            P("tokens", "heads", None),
        ),
        check_vma=False,
    )
```

```python
import jax
import jax.numpy as jnp
from jax import lax
from jax.experimental import pallas as pl
from jax.experimental.pallas import tpu as pltpu
from jax.sharding import PartitionSpec as P

HEAD_DIM = 64
EXPERTS = 32
TOP = 8
CAP = 96


epsilon = 1e-06
theta_base = 10000.0
masked_value = -1e30


def doc_positions(segments):
    axis_last = segments.ndim - 1
    place_ids = lax.broadcasted_iota(jnp.int32, segments.shape, axis_last)
    previous = jnp.concatenate([segments[..., :1] - 1, segments[..., :-1]], axis=axis_last)
    starts = jnp.where(segments != previous, place_ids, 0)
    return place_ids - lax.cummax(starts, axis=axis_last)


def rotary_tables(positions, half_size):
    frequency = theta_base ** (
        -(jnp.arange(half_size, dtype=jnp.float32) * 2.0) / (2.0 * half_size)
    )
    angles = positions.astype(jnp.float32)[..., None] * frequency
    return (jnp.cos(angles), jnp.sin(angles))


def rotate(field, cosine_table, sine_table):
    half_size = field.shape[-1] // 2
    leading = field[..., :half_size]
    trailing = field[..., half_size:]
    cos_part = cosine_table[..., None, :]
    sin_part = sine_table[..., None, :]
    return jnp.concatenate(
        [leading * cos_part - trailing * sin_part, trailing * cos_part + leading * sin_part],
        axis=-1,
    )


f32 = jnp.float32
bf16 = jnp.bfloat16
i32 = jnp.int32
VMEM_LIMIT = 60 * 1024 * 1024
ATTENTION_LIMIT = 24 * 1024 * 1024
CHUNK = 4


def wide_tables(positions):
    half_size = HEAD_DIM // 2
    lanes = jnp.arange(128, dtype=i32) % half_size
    frequency = theta_base ** (-(lanes.astype(f32) * 2.0) / (2.0 * half_size))
    angles = positions.astype(f32) * frequency
    return jnp.cos(angles), jnp.sin(angles)


def swap(field, axis, bit):
    count = lax.axis_size(axis)
    return lax.ppermute(field, axis, [(i, i ^ bit) for i in range(count)])


def gather_tokens(field, other):
    count = lax.axis_size("tokens")
    held = {0: field}
    early = swap(field, "tokens", 2) if count > 2 else field
    bit = count // 2
    while bit > 1:
        for key in list(held):
            source = after(held[key], other) if key else held[key]
            held[key | bit] = early if bit == 2 and not key else swap(source, "tokens", bit)
        bit //= 2
    held.update({key | 1: swap(held[key], "tokens", 1) for key in list(held)})
    return [held[key] for key in range(count)], early


def add_low(left, right):
    return (left.astype(f32) + right.astype(f32)).astype(bf16)


def total(terms):
    result = terms[0].astype(f32)
    for other in terms[1:]:
        result = result + other.astype(f32)
    return result


def scatter_step(terms, bit, one_by_one, *anchors):
    sent, last = [], anchors
    for key in sorted((k for k in terms if k & bit), reverse=True):
        low = total(terms.pop(key)).astype(bf16)
        sent.append(low)
        arrived = swap(after(low, *last) if last else low, "tokens", 2 * bit)
        if one_by_one:
            last = (arrived,)
        terms[key ^ bit].append(arrived)
    return sent


def scatter_rest(terms, *anchors):
    bit, sent = 2, []
    while len(terms) > 1:
        sent += scatter_step(terms, bit, True, *anchors)
        bit *= 2
    return total(terms[0]), sent


def scatter_chips(parts, one_by_one=True):
    terms = {key: list(some) for key, some in enumerate(parts)}
    sent = scatter_step(terms, 1, one_by_one)
    result, more = scatter_rest(terms)
    return result, sent + more


def after(field, *others):
    return lax.optimization_barrier((field, *others))[0]


def scatter_tokens(field):
    count, rows, columns = field.shape
    place = lax.axis_index("tokens")
    chip, core = place // 2, place % 2
    paired = field.reshape(count // 2, 2, rows, columns)
    sent = lax.dynamic_index_in_dim(paired, 1 - core, axis=1, keepdims=False)
    kept = lax.dynamic_index_in_dim(paired, core, axis=1, keepdims=False)
    both = add_low(kept, swap(sent, "tokens", 1))
    parts = [
        [lax.dynamic_index_in_dim(both, chip ^ key, axis=0, keepdims=False)]
        for key in range(count // 2)
    ]
    return scatter_chips(parts)[0], both


def sum_axis(field, axis):
    bit = 1
    while bit < lax.axis_size(axis):
        field = field + swap(field, axis, bit)
        bit *= 2
    return field


def sum_heads(field):
    one, two, three = (swap(field, "heads", key) for key in (1, 2, 3))
    return (field + one) + (two + three)


def xor_order(field, place):
    count = field.shape[0]
    rest = field.shape[1:]
    bit = 1
    while bit < count:
        split = field.reshape((count // (2 * bit), 2, bit) + rest)
        flipped = jnp.concatenate([split[:, 1:], split[:, :1]], axis=1)
        field = jnp.where((place & bit) != 0, flipped, split).reshape((count,) + rest)
        bit *= 2
    return field


def nn(left, right):
    return lax.dot_general(left, right, (((1,), (0,)), ((), ())), preferred_element_type=f32)


def nt(left, right):
    return lax.dot_general(left, right, (((1,), (1,)), ((), ())), preferred_element_type=f32)


def tn(left, right):
    return lax.dot_general(left, right, (((0,), (0,)), ((), ())), preferred_element_type=f32)


def select_columns(slots, local):
    rows = slots.shape[1]
    slots = jnp.transpose(slots)
    lanes = lax.broadcasted_iota(i32, (rows, local * CAP), 1)
    same = None
    for expert in range(local):
        column = slots[:, expert : expert + 1]
        term = lanes == jnp.where(column < 0, -1, column + expert * CAP)
        same = term if same is None else same | term
    return jnp.where(same, 1.0, 0.0).astype(bf16)


def turn(field, cosine, sine, sign):
    lanes = lax.broadcasted_iota(i32, field.shape, 1)
    partner = jnp.where(
        lanes % HEAD_DIM < HEAD_DIM // 2,
        -pltpu.roll(field, 128 - HEAD_DIM // 2, 1),
        pltpu.roll(field, HEAD_DIM // 2, 1),
    )
    return field * cosine + sign * (partner * sine)


def keep_half(field, side):
    lanes = lax.broadcasted_iota(i32, field.shape, 1)
    return jnp.where((lanes >= HEAD_DIM) == (side == 1), field, jnp.zeros_like(field))


def join_halves(low, high):
    lanes = lax.broadcasted_iota(i32, low.shape, 1)
    return jnp.where(lanes < HEAD_DIM, low, high)


def attention_forward_kernel(
    raw_ref, cosine_ref, sine_ref, start_ref, out_ref, turned_ref, log_ref, swapped_ref
):
    length = raw_ref.shape[0]
    rows = 256
    scaling = HEAD_DIM ** (-0.5)
    for first in range(0, length, rows):
        some = pl.ds(first, rows)
        cosine, sine = cosine_ref[some, :], sine_ref[some, :]
        for part in range(2):
            lanes = pl.ds(128 * part, 128)
            query = turn(raw_ref[some, lanes], cosine, sine, 1.0).astype(bf16)
            turned_ref[some, lanes] = (query.astype(f32) * scaling).astype(bf16)
        key = turn(raw_ref[some, pl.ds(256, 128)], cosine, sine, 1.0)
        value = raw_ref[some, pl.ds(384, 128)]
        turned_ref[some, pl.ds(256, 128)] = key.astype(bf16)
        turned_ref[some, pl.ds(384, 128)] = value.astype(bf16)
        swapped_ref[some, pl.ds(0, 128)] = pltpu.roll(key, HEAD_DIM, 1).astype(bf16)
        swapped_ref[some, pl.ds(128, 128)] = pltpu.roll(value, HEAD_DIM, 1).astype(bf16)
    for first in range(0, length, rows):
        some = pl.ds(first, rows)
        low = max(0, first - 512)
        span = pl.ds(low, first + rows - low)
        columns = first + rows - low
        keys = lax.broadcasted_iota(i32, (rows, columns), 1) + low
        queries = lax.broadcasted_iota(i32, (rows, columns), 0) + first
        allowed = (keys <= queries) & (keys >= start_ref[some, :])
        for pair in range(2):
            query = turned_ref[some, pl.ds(128 * pair, 128)]
            halves = []
            for side in range(2):
                if pair == side:
                    key, value = turned_ref[span, pl.ds(256, 128)], turned_ref[span, pl.ds(384, 128)]
                else:
                    key, value = swapped_ref[span, pl.ds(0, 128)], swapped_ref[span, pl.ds(128, 128)]
                scores = jnp.where(allowed, nt(keep_half(query, side), key), masked_value)
                top = jnp.max(scores, axis=1, keepdims=True)
                exponent = jnp.exp(scores - top)
                total = jnp.sum(exponent, axis=1, keepdims=True)
                weights = (exponent * (1.0 / total)).astype(bf16)
                halves.append(nn(weights, value))
                number = 2 * pair + side
                log_ref[some, pl.ds(number, 1)] = top + jnp.log(total)
            out_ref[some, pl.ds(128 * pair, 128)] = join_halves(*halves).astype(bf16)


def attention_backward_kernel(
    turned_ref, grad_ref, log_ref, start_ref, cosine_ref, sine_ref, out_ref,
    swapped_ref, key_acc, value_acc,
):
    length = turned_ref.shape[0]
    rows = 256
    scaling = HEAD_DIM ** (-0.5)
    key_acc[...] = jnp.zeros_like(key_acc)
    value_acc[...] = jnp.zeros_like(value_acc)
    for first in range(0, length, rows):
        some = pl.ds(first, rows)
        for part in range(2):
            field = turned_ref[some, pl.ds(256 + 128 * part, 128)].astype(f32)
            swapped_ref[some, pl.ds(128 * part, 128)] = pltpu.roll(field, HEAD_DIM, 1).astype(bf16)
    for first in range(0, length, rows):
        some = pl.ds(first, rows)
        low = max(0, first - 512)
        count = first + rows - low
        span = pl.ds(low, count)
        keys = lax.broadcasted_iota(i32, (count, rows), 0) + low
        queries = lax.broadcasted_iota(i32, (count, rows), 1) + first
        allowed = (keys <= queries) & (keys >= start_ref[:, some])
        for pair in range(2):
            query = turned_ref[some, pl.ds(128 * pair, 128)]
            grad = grad_ref[some, pl.ds(128 * pair, 128)]
            halves = []
            for side in range(2):
                if pair == side:
                    key, value = turned_ref[span, pl.ds(256, 128)], turned_ref[span, pl.ds(384, 128)]
                else:
                    key, value = swapped_ref[span, pl.ds(0, 128)], swapped_ref[span, pl.ds(128, 128)]
                mine, mine_grad = keep_half(query, side), keep_half(grad, side)
                scores = jnp.where(allowed, nt(key, mine), masked_value)
                number = 2 * pair + side
                probs = jnp.exp(scores - log_ref[pl.ds(number, 1), some])
                prob_grads = nt(value, mine_grad)
                offset = jnp.sum(probs * prob_grads, axis=0, keepdims=True)
                score_grads = (probs * (prob_grads - offset)).astype(bf16)
                halves.append(tn(score_grads, key) * scaling)
                kind = 0 if pair == side else 1
                key_acc[kind, span, :] += nn(score_grads, mine)
                value_acc[kind, span, :] += nn(probs.astype(bf16), mine_grad)
            cosine, sine = cosine_ref[some, :], sine_ref[some, :]
            out_ref[some, pl.ds(128 * pair, 128)] = turn(
                join_halves(*halves), cosine, sine, -1.0
            ).astype(bf16)
    for first in range(0, length, rows):
        some = pl.ds(first, rows)
        cosine, sine = cosine_ref[some, :], sine_ref[some, :]
        key = key_acc[0, some, :] + pltpu.roll(key_acc[1, some, :], HEAD_DIM, 1)
        value = value_acc[0, some, :] + pltpu.roll(value_acc[1, some, :], HEAD_DIM, 1)
        out_ref[some, pl.ds(256, 128)] = turn(key, cosine, sine, -1.0).astype(bf16)
        out_ref[some, pl.ds(384, 128)] = value.astype(bf16)


def small_cost():
    return pl.CostEstimate(flops=1000000, bytes_accessed=100000, transcendentals=0)


def attention_forward(raw, cosine, sine, starts):
    length = raw.shape[0]
    return pl.pallas_call(
        attention_forward_kernel,
        out_shape=[
            jax.ShapeDtypeStruct((length, 256), bf16),
            jax.ShapeDtypeStruct((length, 512), bf16),
            jax.ShapeDtypeStruct((length, 8), f32),
        ],
        scratch_shapes=[pltpu.VMEM((length, 256), bf16)],
        compiler_params=pltpu.CompilerParams(vmem_limit_bytes=ATTENTION_LIMIT),
        cost_estimate=small_cost(),
        name="attention_forward",
    )(raw, cosine, sine, starts)


def attention_backward(turned, grad, logs, starts, cosine, sine):
    length = turned.shape[0]
    return pl.pallas_call(
        attention_backward_kernel,
        out_shape=jax.ShapeDtypeStruct((length, 512), bf16),
        scratch_shapes=[
            pltpu.VMEM((length, 256), bf16),
            pltpu.VMEM((2, length, 128), f32),
            pltpu.VMEM((2, length, 128), f32),
        ],
        compiler_params=pltpu.CompilerParams(vmem_limit_bytes=ATTENTION_LIMIT),
        cost_estimate=small_cost(),
        name="attention_backward",
    )(turned, grad, logs, starts, cosine, sine)


def expert_kernel(sources, first_source, count, heads, chunk, absolute, *refs):
    refs = list(refs)
    where_ref = refs.pop(0)
    hn_refs = [refs.pop(0) for _ in range(sources)]
    g_hbm, slot_ref, gw_ref, gate_ref, up_ref, down_ref = refs[:6]
    even_ref, odd_ref, mixed_even_ref, mixed_odd_ref, dgw_ref = refs[6:11]
    outs = [refs[11 + 4 * k : 15 + 4 * k] for k in range(count)]
    h_ref, g_ref, x_ref, xr_ref, gx_ref, act_ref, dye_ref, dgu_ref, gws_ref, dcol_ref = refs[
        11 + 4 * count : 21 + 4 * count
    ]
    dxe_ref, ye_ref, sum_ref, h_sem, g_sem, out_sem = refs[21 + 4 * count :]
    step = pl.program_id(0)
    expert = jnp.minimum(step, count - 1)
    place, head = where_ref[0], where_ref[1]
    rows = h_ref.shape[1]
    width = h_ref.shape[2]
    hidden = act_ref.shape[1]
    wide, narrow = width // heads, hidden // heads
    group = chunk // CAP

    def origin(s):
        return place ^ (first_source + s)

    def copy_h(s):
        return pltpu.make_async_copy(hn_refs[s], h_ref.at[s], h_sem.at[s])

    def copy_g(s):
        return pltpu.make_async_copy(g_hbm.at[origin(s)], g_ref.at[s], g_sem.at[s])

    def copy_out(number, side):
        slot = number % 2
        return pltpu.make_async_copy(
            sum_ref.at[slot, side],
            outs[number][side],
            out_sem.at[4 * slot + side],
        )

    @pl.when(step == 0)
    def _():
        for s in range(sources):
            copy_h(s).start()
        for s in range(sources):
            copy_g(s).start()
        for s in range(sources):
            copy_h(s).wait()

    def chosen(s):
        slots = slot_ref[origin(s), pl.ds(expert, 1), :]
        return lax.broadcasted_iota(i32, (CAP, rows), 0) == slots

    def pick(s):
        same = chosen(s)
        select = jnp.where(same, 1.0, 0.0).astype(bf16)
        mine = pl.ds(s * CAP, CAP)
        x = nn(select, h_ref[s]).astype(bf16)
        x_ref[mine, :] = x
        for owner in range(heads):
            target = pl.multiple_of((owner ^ head) * wide, wide)
            xr_ref[mine, pl.ds(target, wide)] = x[:, owner * wide : (owner + 1) * wide]
        row = gw_ref[origin(s), pl.ds(expert, 1), :]
        gws_ref[mine, :] = jnp.sum(jnp.where(same, row, 0.0), axis=1, keepdims=True)

    def pick_grad(s):
        select = jnp.where(chosen(s), 1.0, 0.0).astype(bf16)
        gx_ref[pl.ds(s * CAP, CAP), :] = nn(select, g_ref[s]).astype(bf16)

    def work(number):
        part = pl.ds(pl.multiple_of(number * chunk, chunk), chunk)
        some = pl.ds(number * group, group)
        x = x_ref[part, :]
        gate = nn(x, gate_ref[0])
        up = nn(x, up_ref[0])
        sigma = 1.0 / (1.0 + jnp.exp(-gate))
        silu = gate * sigma
        act = (silu * up).astype(bf16)
        for owner in range(heads):
            target = pl.multiple_of((owner ^ head) * narrow, narrow)
            act_ref[part, pl.ds(target, narrow)] = act[:, owner * narrow : (owner + 1) * narrow]
        gx = gx_ref[part, :].astype(f32)
        weights = gws_ref[part, :]
        dye = (gx * weights).astype(bf16)
        dye_ref[part, :] = dye
        ye = nn(act, down_ref[0]).astype(bf16).astype(f32)
        dcol_ref[part, :] = jnp.sum(gx * ye, axis=1, keepdims=True)
        ye_ref[some, expert] = (ye * weights).astype(bf16).reshape(group, CAP, width)
        dact = nt(dye, down_ref[0])
        dgate = (dact * up * sigma * (1.0 + gate * (1.0 - sigma))).astype(bf16)
        dup = (dact * silu).astype(bf16)
        dgu_ref[part, pl.ds(0, hidden)] = dgate
        dgu_ref[part, pl.ds(hidden, hidden)] = dup
        dxe = (nt(dgate, gate_ref[0]) + nt(dup, up_ref[0])).astype(bf16)
        dxe_ref[some, expert] = dxe.reshape(group, CAP, width)

    @pl.when(step < count)
    def _():
        for s in range(sources):
            pick(s)

        @pl.when(step == 0)
        def _():
            for s in range(sources):
                copy_g(s).wait()

        for s in range(sources):
            pick_grad(s)
        pl.loop(0, sources // group)(work)
        for s in range(sources):
            column = dcol_ref[pl.ds(s * CAP, CAP), :]
            index = origin(s) if absolute else s
            dgw_ref[index, pl.ds(expert, 1), :] = jnp.sum(
                jnp.where(chosen(s), column, 0.0), axis=0, keepdims=True
            )

        down = tn(act_ref[...], dye_ref[...]).astype(bf16)
        for number in range(2, count):

            @pl.when(step == number)
            def _():
                for side in range(4):
                    copy_out(number - 2, side).wait()

        slot = lax.rem(step, 2)
        for relative, position in ((0, 3), (1, 2 * slot), (2, 2 - 2 * slot), (3, 1)):
            both = tn(xr_ref[:, pl.ds(relative * wide, wide)], dgu_ref[...]).astype(bf16)
            target_ref = sum_ref.at[slot, position]
            target_ref[pl.ds(0, wide), :] = both[:, :hidden]
            target_ref[pl.ds(wide, wide), :] = both[:, hidden:]
            low = down[relative * narrow : (relative + 1) * narrow]
            target_ref[pl.ds(2 * wide, narrow), :] = low[:, :hidden]
            target_ref[pl.ds(2 * wide + narrow, narrow), :] = low[:, hidden:]
        for number in range(count):

            @pl.when(step == number)
            def _():
                for side in range(4):
                    copy_out(number, side).start()

    @pl.when(step >= count)
    def _():
        pair = step - count
        for side, targets in enumerate(((even_ref, mixed_even_ref), (odd_ref, mixed_odd_ref))):
            select = select_columns(slot_ref[place ^ (first_source + 2 * pair + side)], count)
            for source_ref, out_ref in zip((dxe_ref, ye_ref), targets):
                values = source_ref[2 * pair + side].reshape(count * CAP, width)
                out_ref[0] = nn(select, values).astype(bf16)

        @pl.when(pair == sources // 2 - 1)
        def _():
            for number in range(max(0, count - 2), count):
                for side in range(4):
                    copy_out(number, side).wait()


def run_experts(
    where, hn_list, upstream_all, first_source, slots, gate_weights, w_gate, w_up, w_down, heads,
):
    sources = len(hn_list)
    rows, width = hn_list[0].shape
    count, _, hidden = w_gate.shape
    slots_all = sources * CAP
    block = 3 * (width // heads)
    whole = pl.BlockSpec(memory_space=pltpu.VMEM)
    hbm = pl.BlockSpec(memory_space=pl.ANY)
    chunk = CHUNK * CAP
    absolute = sources == slots.shape[0]

    def of_expert(shape):
        return pl.BlockSpec(shape, lambda i: (jnp.minimum(i, count - 1), 0, 0))

    def of_pair(i):
        return (jnp.maximum(i - count, 0), 0, 0)

    half = jax.ShapeDtypeStruct((sources // 2, rows, width), bf16)
    out_shape = [
        half,
        half,
        half,
        half,
        jax.ShapeDtypeStruct((sources, count, rows), f32),
    ]
    out_specs = [
        pl.BlockSpec((1, rows, width), of_pair),
        pl.BlockSpec((1, rows, width), of_pair),
        pl.BlockSpec((1, rows, width), of_pair),
        pl.BlockSpec((1, rows, width), of_pair),
        whole,
    ]
    one = jax.ShapeDtypeStruct((block, hidden), bf16)
    out_shape += [one] * (4 * count)
    out_specs += [hbm] * (4 * count)

    def kernel(*refs):
        expert_kernel(sources, first_source, count, heads, chunk, absolute, *refs)

    return pl.pallas_call(
        kernel,
        grid=(count + sources // 2,),
        in_specs=[pl.BlockSpec(memory_space=pltpu.SMEM)]
        + [hbm] * sources
        + [hbm, whole, whole]
        + [
            of_expert((1, width, hidden)),
            of_expert((1, width, hidden)),
            of_expert((1, hidden, width)),
        ],
        out_specs=out_specs,
        out_shape=out_shape,
        scratch_shapes=[
            pltpu.VMEM((sources, rows, width), bf16),
            pltpu.VMEM((sources, rows, width), bf16),
            pltpu.VMEM((slots_all, width), bf16),
            pltpu.VMEM((slots_all, width), bf16),
            pltpu.VMEM((slots_all, width), bf16),
            pltpu.VMEM((slots_all, hidden), bf16),
            pltpu.VMEM((slots_all, width), bf16),
            pltpu.VMEM((slots_all, 2 * hidden), bf16),
            pltpu.VMEM((slots_all, 1), f32),
            pltpu.VMEM((slots_all, 1), f32),
            pltpu.VMEM((sources, count, CAP, width), bf16),
            pltpu.VMEM((sources, count, CAP, width), bf16),
            pltpu.VMEM((2, 4, block, hidden), bf16),
            pltpu.SemaphoreType.DMA((sources,)),
            pltpu.SemaphoreType.DMA((sources,)),
            pltpu.SemaphoreType.DMA((8,)),
        ],
        compiler_params=pltpu.CompilerParams(vmem_limit_bytes=VMEM_LIMIT),
        cost_estimate=small_cost(),
        name="experts",
    )(where, *hn_list, upstream_all, slots, gate_weights, w_gate, w_up, w_down)


def finish_kernel(*refs):
    in_ref, pair_ref, down_ref, in_sem, out_sem = refs[-5:]
    outs = refs[-8:-5]
    fields = refs[:-8]
    count = len(fields) // 3
    wide, hidden = pair_ref.shape[2:]
    narrow = down_ref.shape[1]

    def arrive(number):
        return pltpu.make_async_copy(fields[number], in_ref.at[number], in_sem.at[number])

    def leave(e, kind):
        source = pair_ref.at[e, kind] if kind < 2 else down_ref.at[e]
        return pltpu.make_async_copy(source, outs[kind].at[e], out_sem.at[3 * e + kind])

    for e in range(count):
        for kind in range(3):
            arrive(kind * count + e).start()
    for e in range(count):
        for kind in range(3):
            arrive(kind * count + e).wait()

        def total(first, rows):
            part = pl.ds(first, rows)
            return (
                in_ref[e, part, :].astype(f32)
                + in_ref[count + e, part, :].astype(f32)
                + in_ref[2 * count + e, part, :].astype(f32)
            )

        for kind in range(2):
            pair_ref[e, kind] = total(kind * wide, wide)
        down_ref[e, :, pl.ds(0, hidden)] = total(2 * wide, narrow)
        down_ref[e, :, pl.ds(hidden, hidden)] = total(2 * wide + narrow, narrow)
        for kind in range(3):
            leave(e, kind).start()
    for e in range(count):
        for kind in range(3):
            leave(e, kind).wait()


def scatter_rows(odd, even):
    arrived = swap(odd, "tokens", 1)
    return scatter_chips([[even[k], arrived[k]] for k in range(even.shape[0])], False)


def place_rows(pieces, place):
    rows = pieces[0].shape[0]
    result = jnp.concatenate([pieces[0]] * (len(pieces) - 1), axis=0)
    for key, piece in list(enumerate(pieces))[1:]:
        start = (place ^ key) * rows if key < 4 else (place ^ 3) * rows + rows // 2
        result = lax.dynamic_update_slice_in_dim(result, piece, start, axis=0)
    return result


def place_small(pieces, place):
    count = len(pieces)
    blocks = []
    for block in range(count):
        chosen = pieces[0]
        for key in range(1, count):
            chosen = jnp.where((place ^ key) == block, pieces[key], chosen)
        blocks.append(chosen)
    return jnp.concatenate(blocks, axis=0)


def exchange_rows(field, place):
    count = lax.axis_size("heads")
    rows = field.shape[0] // count
    pieces = []
    for key in range(count):
        piece = lax.dynamic_slice_in_dim(field, (place ^ key) * rows, rows, axis=0)
        pieces.append(swap(piece, "heads", key) if key else piece)
    return pieces


def gather_heads(field):
    half = field.shape[0] // 2
    one, two = swap(field, "heads", 1), swap(field, "heads", 2)
    return [field, one, two, swap(two[:half], "heads", 1), swap(one[half:], "heads", 2)]


def body(
    tokens,
    segment_ids,
    routes,
    attn_gain,
    w_query,
    w_key,
    w_value,
    w_out,
    ffn_gain,
    router,
    w_gate,
    w_up,
    w_down,
    cotangent,
):
    rows_here = tokens.shape[0]
    model_width = tokens.shape[1]
    local_heads = w_query.shape[1] // HEAD_DIM
    local_kv = w_key.shape[1] // HEAD_DIM
    group_size = local_heads // local_kv
    seq_len = segment_ids.shape[1]
    experts_here = w_gate.shape[0]
    hidden = w_gate.shape[2]
    token_groups = lax.axis_size("tokens")
    head_groups = lax.axis_size("heads")
    place = lax.axis_index("tokens")
    head = lax.axis_index("heads")
    scaling = HEAD_DIM ** (-0.5)
    inputs = tokens.astype(f32)
    scale_one = lax.rsqrt(jnp.mean(inputs * inputs, axis=-1, keepdims=True) + epsilon)
    normed_one = (inputs * scale_one * attn_gain).astype(bf16)
    normed_pieces = gather_heads(normed_one)
    weights_packed = jnp.concatenate([w_query, w_key, w_value], axis=1)

    expert_ids = jnp.arange(EXPERTS, dtype=i32)
    own_mask = jnp.sum(
        (routes.T[:, None, :] == expert_ids[None, :, None]).astype(f32), axis=0
    )

    def to_experts(field):
        return lax.all_to_all(
            field, "tokens", split_axis=0, concat_axis=0, tiled=True
        ).reshape(token_groups, experts_here, rows_here)

    masks = to_experts(own_mask)
    normed_full = place_rows([after(normed_one, masks), *normed_pieces[1:]], head)
    upstream_all = lax.all_gather(cotangent, "tokens", axis=0, tiled=False)
    before = jnp.triu(jnp.ones((rows_here, rows_here), bf16), 1)
    slots = jnp.einsum("set,tu->seu", masks.astype(bf16), before, preferred_element_type=f32)
    slots = jnp.where(masks > 0, slots, -1.0).astype(i32)
    slots = jnp.pad(slots, ((0, 0), (0, (-experts_here) % 8), (0, 0)), constant_values=-1)
    positions = doc_positions(segment_ids)[0]
    starts = jnp.arange(seq_len, dtype=i32) - positions
    wide_positions = jnp.broadcast_to(positions[:, None], (seq_len, 128))
    cosine_table, sine_table = wide_tables(wide_positions)
    start_column, start_row = starts[:, None], starts[None]
    normed_full, slots, cosine_table, sine_table, weights_packed, start_column, start_row = (
        lax.optimization_barrier(
            (
                normed_full, slots, cosine_table, sine_table, weights_packed, start_column,
                start_row,
            )
        )
    )
    core = place % 2
    half_rows = w_out.shape[0] // 2
    out_half = lax.dynamic_slice_in_dim(w_out, core * half_rows, half_rows, axis=0)
    out_half = after(after(out_half, slots, cosine_table, sine_table), *normed_pieces[3:])
    out_halves = [swap(out_half, "heads", key) for key in range(1, head_groups)]

    group_width = local_heads * HEAD_DIM
    key_start, value_start = group_width, group_width + local_kv * HEAD_DIM
    raw = jnp.dot(normed_full, weights_packed, preferred_element_type=f32)
    attended, turned, logs = attention_forward(raw, cosine_table, sine_table, start_column)
    out_halves = lax.optimization_barrier((*out_halves, attended))[:-1]
    out_pieces = [w_out]
    for mine in out_halves:
        other = swap(mine, "tokens", 1)
        out_pieces.append(jnp.where(core == 0, mine, other))
        out_pieces.append(jnp.where(core == 0, other, mine))
    w_out_all = jnp.concatenate(out_pieces, axis=0)
    attended_rows = jnp.concatenate(exchange_rows(attended, head), axis=1)
    residual = inputs + jnp.dot(attended_rows, w_out_all, preferred_element_type=f32)
    scale_two = lax.rsqrt(jnp.mean(residual * residual, axis=-1, keepdims=True) + epsilon)
    normed_two = (residual * scale_two * ffn_gain).astype(bf16)
    logits = jnp.einsum("de,rd->er", router, normed_two, preferred_element_type=f32)
    top = jnp.max(jnp.where(own_mask > 0, logits, masked_value), axis=0, keepdims=True)
    exponent = jnp.where(own_mask > 0, jnp.exp(logits - top), 0.0)
    own_gate_weights = exponent / jnp.sum(exponent, axis=0, keepdims=True)
    gate_weights = to_experts(own_gate_weights)
    normed_list, early = gather_tokens(normed_two, gate_weights)
    weights_sent = after(weights_packed, early)
    weight_pieces = [weights_packed] + [
        swap(weights_sent, "heads", key) for key in range(1, head_groups)
    ]
    weights_all = jnp.concatenate(weight_pieces, axis=1)

    where = jnp.stack([place, head]).astype(i32)
    chunk_sources = min(8, token_groups)
    results = []
    for first in range(0, token_groups, chunk_sources):
        results.append(
            run_experts(
                where, normed_list[first : first + chunk_sources], upstream_all, first, slots,
                gate_weights, w_gate, w_up, w_down, head_groups,
            )
        )

    def joined(parts):
        return parts[0] if len(parts) == 1 else jnp.concatenate(parts, axis=0)

    grad_even, grad_odd, mixed_even, mixed_odd, dgw_all = (
        joined([r[k] for r in results]) for k in range(5)
    )
    weight_sums = results[0][5:]
    for other in results[1:]:
        weight_sums = [add_low(mine, more) for mine, more in zip(weight_sums, other[5:])]
    if len(results) > 1:
        dgw_all = xor_order(dgw_all, place)
    grad_odd = after(grad_odd, *weight_pieces[1:])
    normed_grad, marks = scatter_rows(grad_odd, grad_even)
    own_gate_weights = after(own_gate_weights, marks[0])
    dgw = lax.all_to_all(
        dgw_all, "tokens", split_axis=0, concat_axis=0, tiled=True
    ).reshape(EXPERTS, rows_here)
    def send(expert, number, *anchors):
        part = weight_sums[4 * expert + number]
        part = after(part, *anchors) if anchors else part
        return swap(part, "heads", 1 + expert % 2)

    pair = min(2, experts_here)
    arrived = {(e, number): send(e, number) for e in range(pair) for number in (1, 0)}

    def passed_on(expert, anchor):
        kept = after(weight_sums[4 * expert + 2], anchor)
        return add_low(kept, arrived[expert, 1])

    middle = {e: passed_on(e, marks[-1]) for e in range(pair)}
    normed_grad = after(normed_grad, *middle.values(), *[arrived[e, 0] for e in range(pair)])
    passed = {e: swap(middle[e], "heads", 2 - e % 2) for e in middle}
    weighted_sum = jnp.sum(own_gate_weights * dgw, axis=0, keepdims=True)
    logit_grads = (own_gate_weights * (dgw - weighted_sum)).astype(bf16)
    upstream = cotangent.astype(f32)
    normed_grad = normed_grad + jnp.einsum(
        "er,de->rd", logit_grads, router, preferred_element_type=f32
    )
    router_grad = jnp.einsum("er,rd->ed", logit_grads, normed_two, preferred_element_type=f32)
    hatted_two = residual * scale_two
    ffn_gain_grad = jnp.sum(normed_grad * hatted_two, axis=0)
    scaled_two = normed_grad * ffn_gain
    residual_grad = upstream + scale_two * (
        scaled_two - hatted_two * jnp.mean(scaled_two * hatted_two, axis=-1, keepdims=True)
    )
    attn_grad = residual_grad.astype(bf16)
    out_bounds = [0, group_width, 2 * group_width, 3 * group_width]
    attended_rel = jnp.einsum(
        "ld,hd->lh", attn_grad, w_out_all, preferred_element_type=f32
    ).astype(bf16)
    attended_pieces = []
    for key in range(head_groups):
        piece = attended_rel[:, out_bounds[key] : out_bounds[key] + group_width]
        attended_pieces.append(swap(piece, "heads", key) if key else piece)
    attended_grad = place_small(attended_pieces, head)

    mixed_even = after(mixed_even, attended_rel)
    mixed_arrived = swap(mixed_odd, "tokens", 1)
    mixed_terms = {k: [mixed_even[k], mixed_arrived[k]] for k in range(mixed_even.shape[0])}
    mixed_sent = scatter_step(mixed_terms, 1, False)

    out_w_grad = jnp.einsum("rh,rd->hd", attended_rows, attn_grad, preferred_element_type=f32)
    out_rows = group_width // token_groups
    out_w_grad = (
        out_w_grad.astype(bf16)
        .reshape(head_groups, token_groups, out_rows, model_width)
        .swapaxes(0, 1)
        .reshape(token_groups * head_groups * out_rows, model_width)
    )
    attended_grad = after(attended_grad, out_w_grad, *mixed_sent, *passed.values())
    arrived.update({(e, 1): send(e, 1, attended_grad) for e in range(pair, experts_here)})
    out_w_grad = lax.psum_scatter(out_w_grad, "tokens", scatter_dimension=0, tiled=True)
    packed_grad = attention_backward(
        turned, attended_grad, logs.T, start_row, cosine_table, sine_table
    )
    mixture, sent = scatter_rest(mixed_terms, attended_grad)
    packed_grad = after(packed_grad, *sent)
    middle.update({e: passed_on(e, packed_grad) for e in range(pair, experts_here)})
    grad_pieces = exchange_rows(packed_grad, head)
    packed_w_grad = jnp.einsum("ld,lh->dh", normed_full, packed_grad, preferred_element_type=f32)
    attn_gain_grad = jnp.sum(packed_w_grad * weights_packed.astype(f32), axis=1) / attn_gain
    small = jnp.concatenate(
        [
            router_grad,
            ffn_gain_grad[None],
            attn_gain_grad[None],
            jnp.zeros((6, model_width), f32),
        ],
        axis=0,
    )
    packed_w_grad, packed_w_both = scatter_tokens(
        packed_w_grad.astype(bf16).reshape(
            token_groups, model_width // token_groups, packed_grad.shape[1]
        )
    )
    grad_rows = jnp.concatenate(grad_pieces, axis=1)
    later = range(pair, experts_here)
    passed.update(
        {e: swap(after(middle[e], grad_rows), "heads", 2 - e % 2) for e in later}
    )
    out_w_grad = after(out_w_grad, grad_rows).reshape(head_groups, out_rows, model_width)
    out_w_grad = out_w_grad[0].astype(f32) + sum(
        swap(out_w_grad[key], "heads", key).astype(f32) for key in range(1, head_groups)
    )
    arrived.update({(e, 0): send(e, 0, grad_rows) for e in later})
    grad_rows = after(grad_rows, packed_w_both, *[middle[e] for e in later])
    normed_one_grad = jnp.einsum("lh,dh->ld", grad_rows, weights_all, preferred_element_type=f32)
    hatted_one = inputs * scale_one
    scaled_one = normed_one_grad * attn_gain
    input_grad = residual_grad + scale_one * (
        scaled_one - hatted_one * jnp.mean(scaled_one * hatted_one, axis=-1, keepdims=True)
    )
    output = (after(residual, input_grad) + mixture).astype(bf16)
    small = after(small, output, out_w_grad, *[passed[e] for e in later])
    small = sum_axis(small, "tokens")
    small = after(small, *[arrived[e, 0] for e in later])
    small = sum_heads(small)
    router_grad = small[:EXPERTS].T
    ffn_gain_grad, attn_gain_grad = small[EXPERTS], small[EXPERTS + 1]
    wide, narrow = model_width // head_groups, hidden // head_groups
    block = 3 * wide
    gate_w_grad, up_w_grad, down_w_grad = pl.pallas_call(
        finish_kernel,
        in_specs=[pl.BlockSpec(memory_space=pl.ANY)] * (3 * experts_here),
        out_specs=[pl.BlockSpec(memory_space=pl.ANY)] * 3,
        out_shape=[
            jax.ShapeDtypeStruct((experts_here, wide, hidden), f32),
            jax.ShapeDtypeStruct((experts_here, wide, hidden), f32),
            jax.ShapeDtypeStruct((experts_here, narrow, model_width), f32),
        ],
        scratch_shapes=[
            pltpu.VMEM((3 * experts_here, block, hidden), bf16),
            pltpu.VMEM((experts_here, 2, wide, hidden), f32),
            pltpu.VMEM((experts_here, narrow, model_width), f32),
            pltpu.SemaphoreType.DMA((3 * experts_here,)),
            pltpu.SemaphoreType.DMA((3 * experts_here,)),
        ],
        compiler_params=pltpu.CompilerParams(vmem_limit_bytes=ATTENTION_LIMIT),
        cost_estimate=small_cost(),
        name="finish",
    )(
        *[after(weight_sums[4 * e + 3], input_grad) for e in range(experts_here)],
        *[arrived[e, 0] for e in range(experts_here)],
        *[passed[e] for e in range(experts_here)],
    )
    return (
        output,
        input_grad,
        attn_gain_grad,
        packed_w_grad[:, :key_start],
        packed_w_grad[:, key_start:value_start],
        packed_w_grad[:, value_start:],
        out_w_grad,
        ffn_gain_grad,
        router_grad,
        gate_w_grad,
        up_w_grad,
        down_w_grad,
    )


def solution(mesh):
    placed = (
        P(("tokens", "heads"), None),
        P("tokens", None),
        P(("tokens", "heads"), None),
        P(),
        P(None, "heads"),
        P(None, "heads"),
        P(None, "heads"),
        P("heads", None),
        P(),
        P(),
        P("tokens", None, None),
        P("tokens", None, None),
        P("tokens", None, None),
        P(("tokens", "heads"), None),
    )
    return jax.shard_map(
        body,
        mesh=mesh,
        in_specs=placed,
        out_specs=(
            P(("tokens", "heads"), None),
            P(("tokens", "heads"), None),
            P(),
            P("tokens", "heads"),
            P("tokens", "heads"),
            P("tokens", "heads"),
            P(("heads", "tokens"), None),
            P(),
            P(),
            P("tokens", "heads", None),
            P("tokens", "heads", None),
            P("tokens", "heads", None),
        ),
        check_vma=False,
    )
```

```python
import jax
import jax.numpy as jnp
from jax import lax
from jax.experimental import pallas as pl
from jax.experimental.pallas import tpu as pltpu
from jax.sharding import PartitionSpec as P

HEAD_DIM = 64
EXPERTS = 32
TOP = 8
CAP = 96


epsilon = 1e-06
theta_base = 10000.0
masked_value = -1e30


def doc_positions(segments):
    axis_last = segments.ndim - 1
    place_ids = lax.broadcasted_iota(jnp.int32, segments.shape, axis_last)
    previous = jnp.concatenate([segments[..., :1] - 1, segments[..., :-1]], axis=axis_last)
    starts = jnp.where(segments != previous, place_ids, 0)
    return place_ids - lax.cummax(starts, axis=axis_last)


def rotary_tables(positions, half_size):
    frequency = theta_base ** (
        -(jnp.arange(half_size, dtype=jnp.float32) * 2.0) / (2.0 * half_size)
    )
    angles = positions.astype(jnp.float32)[..., None] * frequency
    return (jnp.cos(angles), jnp.sin(angles))


def rotate(field, cosine_table, sine_table):
    half_size = field.shape[-1] // 2
    leading = field[..., :half_size]
    trailing = field[..., half_size:]
    cos_part = cosine_table[..., None, :]
    sin_part = sine_table[..., None, :]
    return jnp.concatenate(
        [leading * cos_part - trailing * sin_part, trailing * cos_part + leading * sin_part],
        axis=-1,
    )


f32 = jnp.float32
bf16 = jnp.bfloat16
i32 = jnp.int32
VMEM_LIMIT = 60 * 1024 * 1024
ATTENTION_LIMIT = 24 * 1024 * 1024
CHUNK = 8


def wide_tables(positions):
    half_size = HEAD_DIM // 2
    lanes = jnp.arange(128, dtype=i32) % half_size
    frequency = theta_base ** (-(lanes.astype(f32) * 2.0) / (2.0 * half_size))
    angles = positions.astype(f32) * frequency
    return jnp.cos(angles), jnp.sin(angles)


def swap(field, axis, bit):
    count = lax.axis_size(axis)
    return lax.ppermute(field, axis, [(i, i ^ bit) for i in range(count)])


def gather_tokens(field, other):
    count = lax.axis_size("tokens")
    held = {0: field}
    early = swap(field, "tokens", 2) if count > 2 else field
    bit = count // 2
    while bit > 1:
        for key in list(held):
            source = after(held[key], other) if key else held[key]
            held[key | bit] = early if bit == 2 and not key else swap(source, "tokens", bit)
        bit //= 2
    held.update({key | 1: swap(held[key], "tokens", 1) for key in list(held)})
    return [held[key] for key in range(count)], early


def add_low(left, right):
    return (left.astype(f32) + right.astype(f32)).astype(bf16)


def total(terms):
    result = terms[0].astype(f32)
    for other in terms[1:]:
        result = result + other.astype(f32)
    return result


def scatter_step(terms, bit, one_by_one, *anchors):
    sent, last = [], anchors
    for key in sorted((k for k in terms if k & bit), reverse=True):
        low = total(terms.pop(key)).astype(bf16)
        sent.append(low)
        arrived = swap(after(low, *last) if last else low, "tokens", 2 * bit)
        if one_by_one:
            last = (arrived,)
        terms[key ^ bit].append(arrived)
    return sent


def scatter_rest(terms, *anchors):
    bit, sent = 2, []
    while len(terms) > 1:
        sent += scatter_step(terms, bit, True, *anchors)
        bit *= 2
    return total(terms[0]), sent


def scatter_chips(parts, one_by_one=True):
    terms = {key: list(some) for key, some in enumerate(parts)}
    sent = scatter_step(terms, 1, one_by_one)
    result, more = scatter_rest(terms)
    return result, sent + more


def after(field, *others):
    return lax.optimization_barrier((field, *others))[0]


def scatter_tokens(field):
    count, rows, columns = field.shape
    place = lax.axis_index("tokens")
    chip, core = place // 2, place % 2
    paired = field.reshape(count // 2, 2, rows, columns)
    sent = lax.dynamic_index_in_dim(paired, 1 - core, axis=1, keepdims=False)
    kept = lax.dynamic_index_in_dim(paired, core, axis=1, keepdims=False)
    both = add_low(kept, swap(sent, "tokens", 1))
    parts = [
        [lax.dynamic_index_in_dim(both, chip ^ key, axis=0, keepdims=False)]
        for key in range(count // 2)
    ]
    return scatter_chips(parts)[0], both


def sum_axis(field, axis):
    bit = 1
    while bit < lax.axis_size(axis):
        field = field + swap(field, axis, bit)
        bit *= 2
    return field


def sum_heads(field):
    one, two, three = (swap(field, "heads", key) for key in (1, 2, 3))
    return (field + one) + (two + three)


def xor_order(field, place):
    count = field.shape[0]
    rest = field.shape[1:]
    bit = 1
    while bit < count:
        split = field.reshape((count // (2 * bit), 2, bit) + rest)
        flipped = jnp.concatenate([split[:, 1:], split[:, :1]], axis=1)
        field = jnp.where((place & bit) != 0, flipped, split).reshape((count,) + rest)
        bit *= 2
    return field


def nn(left, right):
    return lax.dot_general(left, right, (((1,), (0,)), ((), ())), preferred_element_type=f32)


def nt(left, right):
    return lax.dot_general(left, right, (((1,), (1,)), ((), ())), preferred_element_type=f32)


def tn(left, right):
    return lax.dot_general(left, right, (((0,), (0,)), ((), ())), preferred_element_type=f32)


def select_columns(slots, local):
    rows = slots.shape[1]
    slots = jnp.transpose(slots)
    lanes = lax.broadcasted_iota(i32, (rows, local * CAP), 1)
    same = None
    for expert in range(local):
        column = slots[:, expert : expert + 1]
        term = lanes == jnp.where(column < 0, -1, column + expert * CAP)
        same = term if same is None else same | term
    return jnp.where(same, 1.0, 0.0).astype(bf16)


def turn(field, cosine, sine, sign):
    lanes = lax.broadcasted_iota(i32, field.shape, 1)
    partner = jnp.where(
        lanes % HEAD_DIM < HEAD_DIM // 2,
        -pltpu.roll(field, 128 - HEAD_DIM // 2, 1),
        pltpu.roll(field, HEAD_DIM // 2, 1),
    )
    return field * cosine + sign * (partner * sine)


def keep_half(field, side):
    lanes = lax.broadcasted_iota(i32, field.shape, 1)
    return jnp.where((lanes >= HEAD_DIM) == (side == 1), field, jnp.zeros_like(field))


def join_halves(low, high):
    lanes = lax.broadcasted_iota(i32, low.shape, 1)
    return jnp.where(lanes < HEAD_DIM, low, high)


def attention_forward_kernel(
    raw_ref, cosine_ref, sine_ref, start_ref, out_ref, turned_ref, log_ref, swapped_ref
):
    length = raw_ref.shape[0]
    rows = 256
    scaling = HEAD_DIM ** (-0.5)
    for first in range(0, length, rows):
        some = pl.ds(first, rows)
        cosine, sine = cosine_ref[some, :], sine_ref[some, :]
        for part in range(2):
            lanes = pl.ds(128 * part, 128)
            query = turn(raw_ref[some, lanes], cosine, sine, 1.0).astype(bf16)
            turned_ref[some, lanes] = (query.astype(f32) * scaling).astype(bf16)
        key = turn(raw_ref[some, pl.ds(256, 128)], cosine, sine, 1.0)
        value = raw_ref[some, pl.ds(384, 128)]
        turned_ref[some, pl.ds(256, 128)] = key.astype(bf16)
        turned_ref[some, pl.ds(384, 128)] = value.astype(bf16)
        swapped_ref[some, pl.ds(0, 128)] = pltpu.roll(key, HEAD_DIM, 1).astype(bf16)
        swapped_ref[some, pl.ds(128, 128)] = pltpu.roll(value, HEAD_DIM, 1).astype(bf16)
    for first in range(0, length, rows):
        some = pl.ds(first, rows)
        low = max(0, first - 512)
        span = pl.ds(low, first + rows - low)
        columns = first + rows - low
        keys = lax.broadcasted_iota(i32, (rows, columns), 1) + low
        queries = lax.broadcasted_iota(i32, (rows, columns), 0) + first
        allowed = (keys <= queries) & (keys >= start_ref[some, :])
        for pair in range(2):
            query = turned_ref[some, pl.ds(128 * pair, 128)]
            halves = []
            for side in range(2):
                if pair == side:
                    key, value = turned_ref[span, pl.ds(256, 128)], turned_ref[span, pl.ds(384, 128)]
                else:
                    key, value = swapped_ref[span, pl.ds(0, 128)], swapped_ref[span, pl.ds(128, 128)]
                scores = jnp.where(allowed, nt(keep_half(query, side), key), masked_value)
                top = jnp.max(scores, axis=1, keepdims=True)
                exponent = jnp.exp(scores - top)
                total = jnp.sum(exponent, axis=1, keepdims=True)
                weights = (exponent * (1.0 / total)).astype(bf16)
                halves.append(nn(weights, value))
                number = 2 * pair + side
                log_ref[some, pl.ds(number, 1)] = top + jnp.log(total)
            out_ref[some, pl.ds(128 * pair, 128)] = join_halves(*halves).astype(bf16)


def attention_backward_kernel(
    turned_ref, grad_ref, log_ref, start_ref, cosine_ref, sine_ref, out_ref,
    swapped_ref, key_acc, value_acc,
):
    length = turned_ref.shape[0]
    rows = 256
    scaling = HEAD_DIM ** (-0.5)
    key_acc[...] = jnp.zeros_like(key_acc)
    value_acc[...] = jnp.zeros_like(value_acc)
    for first in range(0, length, rows):
        some = pl.ds(first, rows)
        for part in range(2):
            field = turned_ref[some, pl.ds(256 + 128 * part, 128)].astype(f32)
            swapped_ref[some, pl.ds(128 * part, 128)] = pltpu.roll(field, HEAD_DIM, 1).astype(bf16)
    for first in range(0, length, rows):
        some = pl.ds(first, rows)
        low = max(0, first - 512)
        count = first + rows - low
        span = pl.ds(low, count)
        keys = lax.broadcasted_iota(i32, (count, rows), 0) + low
        queries = lax.broadcasted_iota(i32, (count, rows), 1) + first
        allowed = (keys <= queries) & (keys >= start_ref[:, some])
        for pair in range(2):
            query = turned_ref[some, pl.ds(128 * pair, 128)]
            grad = grad_ref[some, pl.ds(128 * pair, 128)]
            halves = []
            for side in range(2):
                if pair == side:
                    key, value = turned_ref[span, pl.ds(256, 128)], turned_ref[span, pl.ds(384, 128)]
                else:
                    key, value = swapped_ref[span, pl.ds(0, 128)], swapped_ref[span, pl.ds(128, 128)]
                mine, mine_grad = keep_half(query, side), keep_half(grad, side)
                scores = jnp.where(allowed, nt(key, mine), masked_value)
                number = 2 * pair + side
                probs = jnp.exp(scores - log_ref[pl.ds(number, 1), some])
                prob_grads = nt(value, mine_grad)
                offset = jnp.sum(probs * prob_grads, axis=0, keepdims=True)
                score_grads = (probs * (prob_grads - offset)).astype(bf16)
                halves.append(tn(score_grads, key) * scaling)
                kind = 0 if pair == side else 1
                key_acc[kind, span, :] += nn(score_grads, mine)
                value_acc[kind, span, :] += nn(probs.astype(bf16), mine_grad)
            cosine, sine = cosine_ref[some, :], sine_ref[some, :]
            out_ref[some, pl.ds(128 * pair, 128)] = turn(
                join_halves(*halves), cosine, sine, -1.0
            ).astype(bf16)
    for first in range(0, length, rows):
        some = pl.ds(first, rows)
        cosine, sine = cosine_ref[some, :], sine_ref[some, :]
        key = key_acc[0, some, :] + pltpu.roll(key_acc[1, some, :], HEAD_DIM, 1)
        value = value_acc[0, some, :] + pltpu.roll(value_acc[1, some, :], HEAD_DIM, 1)
        out_ref[some, pl.ds(256, 128)] = turn(key, cosine, sine, -1.0).astype(bf16)
        out_ref[some, pl.ds(384, 128)] = value.astype(bf16)


def small_cost():
    return pl.CostEstimate(flops=1000000, bytes_accessed=100000, transcendentals=0)


def attention_forward(raw, cosine, sine, starts):
    length = raw.shape[0]
    return pl.pallas_call(
        attention_forward_kernel,
        out_shape=[
            jax.ShapeDtypeStruct((length, 256), bf16),
            jax.ShapeDtypeStruct((length, 512), bf16),
            jax.ShapeDtypeStruct((length, 8), f32),
        ],
        scratch_shapes=[pltpu.VMEM((length, 256), bf16)],
        compiler_params=pltpu.CompilerParams(vmem_limit_bytes=ATTENTION_LIMIT),
        cost_estimate=small_cost(),
        name="attention_forward",
    )(raw, cosine, sine, starts)


def attention_backward(turned, grad, logs, starts, cosine, sine):
    length = turned.shape[0]
    return pl.pallas_call(
        attention_backward_kernel,
        out_shape=jax.ShapeDtypeStruct((length, 512), bf16),
        scratch_shapes=[
            pltpu.VMEM((length, 256), bf16),
            pltpu.VMEM((2, length, 128), f32),
            pltpu.VMEM((2, length, 128), f32),
        ],
        compiler_params=pltpu.CompilerParams(vmem_limit_bytes=ATTENTION_LIMIT),
        cost_estimate=small_cost(),
        name="attention_backward",
    )(turned, grad, logs, starts, cosine, sine)


def expert_kernel(sources, first_source, count, heads, chunk, absolute, *refs):
    refs = list(refs)
    where_ref = refs.pop(0)
    hn_refs = [refs.pop(0) for _ in range(sources)]
    g_hbm, slot_ref, gw_ref, gate_ref, up_ref, down_ref = refs[:6]
    even_ref, odd_ref, mixed_even_ref, mixed_odd_ref, dgw_ref = refs[6:11]
    outs = [refs[11 + 4 * k : 15 + 4 * k] for k in range(count)]
    h_ref, g_ref, x_ref, xr_ref, gx_ref, act_ref, dye_ref, dgu_ref, gws_ref, dcol_ref = refs[
        11 + 4 * count : 21 + 4 * count
    ]
    dxe_ref, ye_ref, sum_ref, h_sem, g_sem, out_sem = refs[21 + 4 * count :]
    step = pl.program_id(0)
    expert = jnp.minimum(step, count - 1)
    place, head = where_ref[0], where_ref[1]
    rows = h_ref.shape[1]
    width = h_ref.shape[2]
    hidden = act_ref.shape[1]
    wide, narrow = width // heads, hidden // heads
    group = chunk // CAP

    def origin(s):
        return place ^ (first_source + s)

    def copy_h(s):
        return pltpu.make_async_copy(hn_refs[s], h_ref.at[s], h_sem.at[s])

    def copy_g(s):
        return pltpu.make_async_copy(g_hbm.at[origin(s)], g_ref.at[s], g_sem.at[s])

    def copy_out(number, side):
        slot = number % 2
        return pltpu.make_async_copy(
            sum_ref.at[slot, side],
            outs[number][side],
            out_sem.at[4 * slot + side],
        )

    @pl.when(step == 0)
    def _():
        for s in range(sources):
            copy_h(s).start()
        for s in range(sources):
            copy_g(s).start()
        for s in range(sources):
            copy_h(s).wait()

    def chosen(s):
        slots = slot_ref[origin(s), pl.ds(expert, 1), :]
        return lax.broadcasted_iota(i32, (CAP, rows), 0) == slots

    def pick(s):
        same = chosen(s)
        select = jnp.where(same, 1.0, 0.0).astype(bf16)
        mine = pl.ds(s * CAP, CAP)
        x = nn(select, h_ref[s]).astype(bf16)
        x_ref[mine, :] = x
        for owner in range(heads):
            target = pl.multiple_of((owner ^ head) * wide, wide)
            xr_ref[mine, pl.ds(target, wide)] = x[:, owner * wide : (owner + 1) * wide]
        row = gw_ref[origin(s), pl.ds(expert, 1), :]
        gws_ref[mine, :] = jnp.sum(jnp.where(same, row, 0.0), axis=1, keepdims=True)

    def pick_grad(s):
        select = jnp.where(chosen(s), 1.0, 0.0).astype(bf16)
        gx_ref[pl.ds(s * CAP, CAP), :] = nn(select, g_ref[s]).astype(bf16)

    def work(number):
        part = pl.ds(pl.multiple_of(number * chunk, chunk), chunk)
        some = pl.ds(number * group, group)
        x = x_ref[part, :]
        gate = nn(x, gate_ref[0])
        up = nn(x, up_ref[0])
        sigma = 1.0 / (1.0 + jnp.exp(-gate))
        silu = gate * sigma
        act = (silu * up).astype(bf16)
        for owner in range(heads):
            target = pl.multiple_of((owner ^ head) * narrow, narrow)
            act_ref[part, pl.ds(target, narrow)] = act[:, owner * narrow : (owner + 1) * narrow]
        gx = gx_ref[part, :].astype(f32)
        weights = gws_ref[part, :]
        dye = (gx * weights).astype(bf16)
        dye_ref[part, :] = dye
        ye = nn(act, down_ref[0]).astype(bf16).astype(f32)
        dcol_ref[part, :] = jnp.sum(gx * ye, axis=1, keepdims=True)
        ye_ref[some, expert] = (ye * weights).astype(bf16).reshape(group, CAP, width)
        dact = nt(dye, down_ref[0])
        dgate = (dact * up * sigma * (1.0 + gate * (1.0 - sigma))).astype(bf16)
        dup = (dact * silu).astype(bf16)
        dgu_ref[part, pl.ds(0, hidden)] = dgate
        dgu_ref[part, pl.ds(hidden, hidden)] = dup
        dxe = (nt(dgate, gate_ref[0]) + nt(dup, up_ref[0])).astype(bf16)
        dxe_ref[some, expert] = dxe.reshape(group, CAP, width)

    @pl.when(step < count)
    def _():
        for s in range(sources):
            pick(s)

        @pl.when(step == 0)
        def _():
            for s in range(sources):
                copy_g(s).wait()

        for s in range(sources):
            pick_grad(s)
        pl.loop(0, sources // group)(work)
        for s in range(sources):
            column = dcol_ref[pl.ds(s * CAP, CAP), :]
            index = origin(s) if absolute else s
            dgw_ref[index, pl.ds(expert, 1), :] = jnp.sum(
                jnp.where(chosen(s), column, 0.0), axis=0, keepdims=True
            )

        down = tn(act_ref[...], dye_ref[...]).astype(bf16)
        for number in range(2, count):

            @pl.when(step == number)
            def _():
                for side in range(4):
                    copy_out(number - 2, side).wait()

        slot = lax.rem(step, 2)
        for relative, position in ((0, 3), (1, 2 * slot), (2, 2 - 2 * slot), (3, 1)):
            both = tn(xr_ref[:, pl.ds(relative * wide, wide)], dgu_ref[...]).astype(bf16)
            target_ref = sum_ref.at[slot, position]
            target_ref[pl.ds(0, wide), :] = both[:, :hidden]
            target_ref[pl.ds(wide, wide), :] = both[:, hidden:]
            low = down[relative * narrow : (relative + 1) * narrow]
            target_ref[pl.ds(2 * wide, narrow), :] = low[:, :hidden]
            target_ref[pl.ds(2 * wide + narrow, narrow), :] = low[:, hidden:]
        for number in range(count):

            @pl.when(step == number)
            def _():
                for side in range(4):
                    copy_out(number, side).start()

    @pl.when(step >= count)
    def _():
        pair = step - count
        for side, targets in enumerate(((even_ref, mixed_even_ref), (odd_ref, mixed_odd_ref))):
            select = select_columns(slot_ref[place ^ (first_source + 2 * pair + side)], count)
            for source_ref, out_ref in zip((dxe_ref, ye_ref), targets):
                values = source_ref[2 * pair + side].reshape(count * CAP, width)
                out_ref[0] = nn(select, values).astype(bf16)

        @pl.when(pair == sources // 2 - 1)
        def _():
            for number in range(max(0, count - 2), count):
                for side in range(4):
                    copy_out(number, side).wait()


def run_experts(
    where, hn_list, upstream_all, first_source, slots, gate_weights, w_gate, w_up, w_down, heads,
):
    sources = len(hn_list)
    rows, width = hn_list[0].shape
    count, _, hidden = w_gate.shape
    slots_all = sources * CAP
    block = 3 * (width // heads)
    whole = pl.BlockSpec(memory_space=pltpu.VMEM)
    hbm = pl.BlockSpec(memory_space=pl.ANY)
    chunk = CHUNK * CAP
    absolute = sources == slots.shape[0]

    def of_expert(shape):
        return pl.BlockSpec(shape, lambda i: (jnp.minimum(i, count - 1), 0, 0))

    def of_pair(i):
        return (jnp.maximum(i - count, 0), 0, 0)

    half = jax.ShapeDtypeStruct((sources // 2, rows, width), bf16)
    out_shape = [
        half,
        half,
        half,
        half,
        jax.ShapeDtypeStruct((sources, count, rows), f32),
    ]
    out_specs = [
        pl.BlockSpec((1, rows, width), of_pair),
        pl.BlockSpec((1, rows, width), of_pair),
        pl.BlockSpec((1, rows, width), of_pair),
        pl.BlockSpec((1, rows, width), of_pair),
        whole,
    ]
    one = jax.ShapeDtypeStruct((block, hidden), bf16)
    out_shape += [one] * (4 * count)
    out_specs += [hbm] * (4 * count)

    def kernel(*refs):
        expert_kernel(sources, first_source, count, heads, chunk, absolute, *refs)

    return pl.pallas_call(
        kernel,
        grid=(count + sources // 2,),
        in_specs=[pl.BlockSpec(memory_space=pltpu.SMEM)]
        + [hbm] * sources
        + [hbm, whole, whole]
        + [
            of_expert((1, width, hidden)),
            of_expert((1, width, hidden)),
            of_expert((1, hidden, width)),
        ],
        out_specs=out_specs,
        out_shape=out_shape,
        scratch_shapes=[
            pltpu.VMEM((sources, rows, width), bf16),
            pltpu.VMEM((sources, rows, width), bf16),
            pltpu.VMEM((slots_all, width), bf16),
            pltpu.VMEM((slots_all, width), bf16),
            pltpu.VMEM((slots_all, width), bf16),
            pltpu.VMEM((slots_all, hidden), bf16),
            pltpu.VMEM((slots_all, width), bf16),
            pltpu.VMEM((slots_all, 2 * hidden), bf16),
            pltpu.VMEM((slots_all, 1), f32),
            pltpu.VMEM((slots_all, 1), f32),
            pltpu.VMEM((sources, count, CAP, width), bf16),
            pltpu.VMEM((sources, count, CAP, width), bf16),
            pltpu.VMEM((2, 4, block, hidden), bf16),
            pltpu.SemaphoreType.DMA((sources,)),
            pltpu.SemaphoreType.DMA((sources,)),
            pltpu.SemaphoreType.DMA((8,)),
        ],
        compiler_params=pltpu.CompilerParams(vmem_limit_bytes=VMEM_LIMIT),
        cost_estimate=small_cost(),
        name="experts",
    )(where, *hn_list, upstream_all, slots, gate_weights, w_gate, w_up, w_down)


def finish_kernel(*refs):
    in_ref, pair_ref, down_ref, in_sem, out_sem = refs[-5:]
    outs = refs[-8:-5]
    fields = refs[:-8]
    count = len(fields) // 3
    wide, hidden = pair_ref.shape[2:]
    narrow = down_ref.shape[1]

    def arrive(number):
        return pltpu.make_async_copy(fields[number], in_ref.at[number], in_sem.at[number])

    def leave(e, kind):
        source = pair_ref.at[e, kind] if kind < 2 else down_ref.at[e]
        return pltpu.make_async_copy(source, outs[kind].at[e], out_sem.at[3 * e + kind])

    for e in range(count):
        for kind in range(3):
            arrive(kind * count + e).start()
    for e in range(count):
        for kind in range(3):
            arrive(kind * count + e).wait()

        def total(first, rows):
            part = pl.ds(first, rows)
            return (
                in_ref[e, part, :].astype(f32)
                + in_ref[count + e, part, :].astype(f32)
                + in_ref[2 * count + e, part, :].astype(f32)
            )

        for kind in range(2):
            pair_ref[e, kind] = total(kind * wide, wide)
        down_ref[e, :, pl.ds(0, hidden)] = total(2 * wide, narrow)
        down_ref[e, :, pl.ds(hidden, hidden)] = total(2 * wide + narrow, narrow)
        for kind in range(3):
            leave(e, kind).start()
    for e in range(count):
        for kind in range(3):
            leave(e, kind).wait()


def scatter_rows(odd, even):
    arrived = swap(odd, "tokens", 1)
    return scatter_chips([[even[k], arrived[k]] for k in range(even.shape[0])], False)


def place_rows(pieces, place):
    rows = pieces[0].shape[0]
    result = jnp.concatenate([pieces[0]] * (len(pieces) - 1), axis=0)
    for key, piece in list(enumerate(pieces))[1:]:
        start = (place ^ key) * rows if key < 4 else (place ^ 3) * rows + rows // 2
        result = lax.dynamic_update_slice_in_dim(result, piece, start, axis=0)
    return result


def place_small(pieces, place):
    count = len(pieces)
    blocks = []
    for block in range(count):
        chosen = pieces[0]
        for key in range(1, count):
            chosen = jnp.where((place ^ key) == block, pieces[key], chosen)
        blocks.append(chosen)
    return jnp.concatenate(blocks, axis=0)


def exchange_rows(field, place):
    count = lax.axis_size("heads")
    rows = field.shape[0] // count
    pieces = []
    for key in range(count):
        piece = lax.dynamic_slice_in_dim(field, (place ^ key) * rows, rows, axis=0)
        pieces.append(swap(piece, "heads", key) if key else piece)
    return pieces


def gather_heads(field):
    half = field.shape[0] // 2
    one, two = swap(field, "heads", 1), swap(field, "heads", 2)
    return [field, one, two, swap(two[:half], "heads", 1), swap(one[half:], "heads", 2)]


def body(
    tokens,
    segment_ids,
    routes,
    attn_gain,
    w_query,
    w_key,
    w_value,
    w_out,
    ffn_gain,
    router,
    w_gate,
    w_up,
    w_down,
    cotangent,
):
    rows_here = tokens.shape[0]
    model_width = tokens.shape[1]
    local_heads = w_query.shape[1] // HEAD_DIM
    local_kv = w_key.shape[1] // HEAD_DIM
    group_size = local_heads // local_kv
    seq_len = segment_ids.shape[1]
    experts_here = w_gate.shape[0]
    hidden = w_gate.shape[2]
    token_groups = lax.axis_size("tokens")
    head_groups = lax.axis_size("heads")
    place = lax.axis_index("tokens")
    head = lax.axis_index("heads")
    scaling = HEAD_DIM ** (-0.5)
    inputs = tokens.astype(f32)
    scale_one = lax.rsqrt(jnp.mean(inputs * inputs, axis=-1, keepdims=True) + epsilon)
    normed_one = (inputs * scale_one * attn_gain).astype(bf16)
    normed_pieces = gather_heads(normed_one)
    weights_packed = jnp.concatenate([w_query, w_key, w_value], axis=1)

    expert_ids = jnp.arange(EXPERTS, dtype=i32)
    own_mask = jnp.sum(
        (routes.T[:, None, :] == expert_ids[None, :, None]).astype(f32), axis=0
    )

    def to_experts(field):
        return lax.all_to_all(
            field, "tokens", split_axis=0, concat_axis=0, tiled=True
        ).reshape(token_groups, experts_here, rows_here)

    masks = to_experts(own_mask)
    normed_full = place_rows([after(normed_one, masks), *normed_pieces[1:]], head)
    upstream_all = lax.all_gather(cotangent, "tokens", axis=0, tiled=False)
    before = jnp.triu(jnp.ones((rows_here, rows_here), bf16), 1)
    slots = jnp.einsum("set,tu->seu", masks.astype(bf16), before, preferred_element_type=f32)
    slots = jnp.where(masks > 0, slots, -1.0).astype(i32)
    slots = jnp.pad(slots, ((0, 0), (0, (-experts_here) % 8), (0, 0)), constant_values=-1)
    positions = doc_positions(segment_ids)[0]
    starts = jnp.arange(seq_len, dtype=i32) - positions
    wide_positions = jnp.broadcast_to(positions[:, None], (seq_len, 128))
    cosine_table, sine_table = wide_tables(wide_positions)
    start_column, start_row = starts[:, None], starts[None]
    normed_full, slots, cosine_table, sine_table, weights_packed, start_column, start_row = (
        lax.optimization_barrier(
            (
                normed_full, slots, cosine_table, sine_table, weights_packed, start_column,
                start_row,
            )
        )
    )
    core = place % 2
    half_rows = w_out.shape[0] // 2
    out_half = lax.dynamic_slice_in_dim(w_out, core * half_rows, half_rows, axis=0)
    out_half = after(after(out_half, slots, cosine_table, sine_table), *normed_pieces[3:])
    out_halves = [swap(out_half, "heads", key) for key in range(1, head_groups)]

    group_width = local_heads * HEAD_DIM
    key_start, value_start = group_width, group_width + local_kv * HEAD_DIM
    raw = jnp.dot(normed_full, weights_packed, preferred_element_type=f32)
    attended, turned, logs = attention_forward(raw, cosine_table, sine_table, start_column)
    out_halves = lax.optimization_barrier((*out_halves, attended))[:-1]
    out_pieces = [w_out]
    for mine in out_halves:
        other = swap(mine, "tokens", 1)
        out_pieces.append(jnp.where(core == 0, mine, other))
        out_pieces.append(jnp.where(core == 0, other, mine))
    w_out_all = jnp.concatenate(out_pieces, axis=0)
    attended_rows = jnp.concatenate(exchange_rows(attended, head), axis=1)
    residual = inputs + jnp.dot(attended_rows, w_out_all, preferred_element_type=f32)
    scale_two = lax.rsqrt(jnp.mean(residual * residual, axis=-1, keepdims=True) + epsilon)
    normed_two = (residual * scale_two * ffn_gain).astype(bf16)
    logits = jnp.einsum("de,rd->er", router, normed_two, preferred_element_type=f32)
    top = jnp.max(jnp.where(own_mask > 0, logits, masked_value), axis=0, keepdims=True)
    exponent = jnp.where(own_mask > 0, jnp.exp(logits - top), 0.0)
    own_gate_weights = exponent / jnp.sum(exponent, axis=0, keepdims=True)
    gate_weights = to_experts(own_gate_weights)
    normed_list, early = gather_tokens(normed_two, gate_weights)
    weights_sent = after(weights_packed, early)
    weight_pieces = [weights_packed] + [
        swap(weights_sent, "heads", key) for key in range(1, head_groups)
    ]
    weights_all = jnp.concatenate(weight_pieces, axis=1)

    where = jnp.stack([place, head]).astype(i32)
    chunk_sources = min(8, token_groups)
    results = []
    for first in range(0, token_groups, chunk_sources):
        results.append(
            run_experts(
                where, normed_list[first : first + chunk_sources], upstream_all, first, slots,
                gate_weights, w_gate, w_up, w_down, head_groups,
            )
        )

    def joined(parts):
        return parts[0] if len(parts) == 1 else jnp.concatenate(parts, axis=0)

    grad_even, grad_odd, mixed_even, mixed_odd, dgw_all = (
        joined([r[k] for r in results]) for k in range(5)
    )
    weight_sums = results[0][5:]
    for other in results[1:]:
        weight_sums = [add_low(mine, more) for mine, more in zip(weight_sums, other[5:])]
    if len(results) > 1:
        dgw_all = xor_order(dgw_all, place)
    grad_odd = after(grad_odd, *weight_pieces[1:])
    normed_grad, marks = scatter_rows(grad_odd, grad_even)
    own_gate_weights = after(own_gate_weights, marks[0])
    dgw = lax.all_to_all(
        dgw_all, "tokens", split_axis=0, concat_axis=0, tiled=True
    ).reshape(EXPERTS, rows_here)
    def send(expert, number, *anchors):
        part = weight_sums[4 * expert + number]
        part = after(part, *anchors) if anchors else part
        return swap(part, "heads", 1 + expert % 2)

    pair = min(2, experts_here)
    arrived = {(e, number): send(e, number) for e in range(pair) for number in (1, 0)}

    def passed_on(expert, anchor):
        kept = after(weight_sums[4 * expert + 2], anchor)
        return add_low(kept, arrived[expert, 1])

    middle = {e: passed_on(e, marks[-1]) for e in range(pair)}
    normed_grad = after(normed_grad, *middle.values(), *[arrived[e, 0] for e in range(pair)])
    passed = {e: swap(middle[e], "heads", 2 - e % 2) for e in middle}
    weighted_sum = jnp.sum(own_gate_weights * dgw, axis=0, keepdims=True)
    logit_grads = (own_gate_weights * (dgw - weighted_sum)).astype(bf16)
    upstream = cotangent.astype(f32)
    normed_grad = normed_grad + jnp.einsum(
        "er,de->rd", logit_grads, router, preferred_element_type=f32
    )
    router_grad = jnp.einsum("er,rd->ed", logit_grads, normed_two, preferred_element_type=f32)
    hatted_two = residual * scale_two
    ffn_gain_grad = jnp.sum(normed_grad * hatted_two, axis=0)
    scaled_two = normed_grad * ffn_gain
    residual_grad = upstream + scale_two * (
        scaled_two - hatted_two * jnp.mean(scaled_two * hatted_two, axis=-1, keepdims=True)
    )
    attn_grad = residual_grad.astype(bf16)
    out_bounds = [0, group_width, 2 * group_width, 3 * group_width]
    attended_rel = jnp.einsum(
        "ld,hd->lh", attn_grad, w_out_all, preferred_element_type=f32
    ).astype(bf16)
    attended_pieces = []
    for key in range(head_groups):
        piece = attended_rel[:, out_bounds[key] : out_bounds[key] + group_width]
        attended_pieces.append(swap(piece, "heads", key) if key else piece)
    attended_grad = place_small(attended_pieces, head)

    mixed_even = after(mixed_even, attended_rel)
    mixed_arrived = swap(mixed_odd, "tokens", 1)
    mixed_terms = {k: [mixed_even[k], mixed_arrived[k]] for k in range(mixed_even.shape[0])}
    mixed_sent = scatter_step(mixed_terms, 1, False)

    out_w_grad = jnp.einsum("rh,rd->hd", attended_rows, attn_grad, preferred_element_type=f32)
    out_rows = group_width // token_groups
    out_w_grad = (
        out_w_grad.astype(bf16)
        .reshape(head_groups, token_groups, out_rows, model_width)
        .swapaxes(0, 1)
        .reshape(token_groups * head_groups * out_rows, model_width)
    )
    attended_grad = after(attended_grad, out_w_grad, *mixed_sent, *passed.values())
    arrived.update({(e, 1): send(e, 1, attended_grad) for e in range(pair, experts_here)})
    out_w_grad = lax.psum_scatter(out_w_grad, "tokens", scatter_dimension=0, tiled=True)
    packed_grad = attention_backward(
        turned, attended_grad, logs.T, start_row, cosine_table, sine_table
    )
    mixture, sent = scatter_rest(mixed_terms, attended_grad)
    packed_grad = after(packed_grad, *sent)
    middle.update({e: passed_on(e, packed_grad) for e in range(pair, experts_here)})
    grad_pieces = exchange_rows(packed_grad, head)
    packed_w_grad = jnp.einsum("ld,lh->dh", normed_full, packed_grad, preferred_element_type=f32)
    attn_gain_grad = jnp.sum(packed_w_grad * weights_packed.astype(f32), axis=1) / attn_gain
    small = jnp.concatenate(
        [
            router_grad,
            ffn_gain_grad[None],
            attn_gain_grad[None],
            jnp.zeros((6, model_width), f32),
        ],
        axis=0,
    )
    packed_w_grad, packed_w_both = scatter_tokens(
        packed_w_grad.astype(bf16).reshape(
            token_groups, model_width // token_groups, packed_grad.shape[1]
        )
    )
    grad_rows = jnp.concatenate(grad_pieces, axis=1)
    later = range(pair, experts_here)
    passed.update(
        {e: swap(after(middle[e], grad_rows), "heads", 2 - e % 2) for e in later}
    )
    out_w_grad = after(out_w_grad, grad_rows).reshape(head_groups, out_rows, model_width)
    out_w_grad = out_w_grad[0].astype(f32) + sum(
        swap(out_w_grad[key], "heads", key).astype(f32) for key in range(1, head_groups)
    )
    arrived.update({(e, 0): send(e, 0, grad_rows) for e in later})
    grad_rows = after(grad_rows, packed_w_both, *[middle[e] for e in later])
    normed_one_grad = jnp.einsum("lh,dh->ld", grad_rows, weights_all, preferred_element_type=f32)
    hatted_one = inputs * scale_one
    scaled_one = normed_one_grad * attn_gain
    input_grad = residual_grad + scale_one * (
        scaled_one - hatted_one * jnp.mean(scaled_one * hatted_one, axis=-1, keepdims=True)
    )
    output = (after(residual, input_grad) + mixture).astype(bf16)
    small = after(small, output, out_w_grad, *[passed[e] for e in later])
    small = sum_axis(small, "tokens")
    small = after(small, *[arrived[e, 0] for e in later])
    small = sum_heads(small)
    router_grad = small[:EXPERTS].T
    ffn_gain_grad, attn_gain_grad = small[EXPERTS], small[EXPERTS + 1]
    wide, narrow = model_width // head_groups, hidden // head_groups
    block = 3 * wide
    gate_w_grad, up_w_grad, down_w_grad = pl.pallas_call(
        finish_kernel,
        in_specs=[pl.BlockSpec(memory_space=pl.ANY)] * (3 * experts_here),
        out_specs=[pl.BlockSpec(memory_space=pl.ANY)] * 3,
        out_shape=[
            jax.ShapeDtypeStruct((experts_here, wide, hidden), f32),
            jax.ShapeDtypeStruct((experts_here, wide, hidden), f32),
            jax.ShapeDtypeStruct((experts_here, narrow, model_width), f32),
        ],
        scratch_shapes=[
            pltpu.VMEM((3 * experts_here, block, hidden), bf16),
            pltpu.VMEM((experts_here, 2, wide, hidden), f32),
            pltpu.VMEM((experts_here, narrow, model_width), f32),
            pltpu.SemaphoreType.DMA((3 * experts_here,)),
            pltpu.SemaphoreType.DMA((3 * experts_here,)),
        ],
        compiler_params=pltpu.CompilerParams(vmem_limit_bytes=ATTENTION_LIMIT),
        cost_estimate=small_cost(),
        name="finish",
    )(
        *[after(weight_sums[4 * e + 3], input_grad) for e in range(experts_here)],
        *[arrived[e, 0] for e in range(experts_here)],
        *[passed[e] for e in range(experts_here)],
    )
    return (
        output,
        input_grad,
        attn_gain_grad,
        packed_w_grad[:, :key_start],
        packed_w_grad[:, key_start:value_start],
        packed_w_grad[:, value_start:],
        out_w_grad,
        ffn_gain_grad,
        router_grad,
        gate_w_grad,
        up_w_grad,
        down_w_grad,
    )


def solution(mesh):
    placed = (
        P(("tokens", "heads"), None),
        P("tokens", None),
        P(("tokens", "heads"), None),
        P(),
        P(None, "heads"),
        P(None, "heads"),
        P(None, "heads"),
        P("heads", None),
        P(),
        P(),
        P("tokens", None, None),
        P("tokens", None, None),
        P("tokens", None, None),
        P(("tokens", "heads"), None),
    )
    return jax.shard_map(
        body,
        mesh=mesh,
        in_specs=placed,
        out_specs=(
            P(("tokens", "heads"), None),
            P(("tokens", "heads"), None),
            P(),
            P("tokens", "heads"),
            P("tokens", "heads"),
            P("tokens", "heads"),
            P(("heads", "tokens"), None),
            P(),
            P(),
            P("tokens", "heads", None),
            P("tokens", "heads", None),
            P("tokens", "heads", None),
        ),
        check_vma=False,
    )
```
